32 devices in a mesh: paths: 2 (over x), hi: 16 (over z, y, core).
Axes of the slice: x: 2, y: 2, z: 4, core: 2. Of those that a mesh axis runs over, the one named last changes fastest.
Arguments:
- amplitudes: float32 [2, 2097152], P(None, ('paths', 'hi')), parts along dimension 1, may hold values from -6 to 6
- gate_matrices: bfloat16 [6, 2, 128, 128], replicated, may hold values from -0.375 to 0.375
- phase_qubits: int32 [12, 8, 2], P('paths'), parts along dimension 0, may hold values from 0 to 19
- phase_angles: float32 [12, 8], P('paths'), parts along dimension 0, may hold values from -3.140625 to 3.140625
- cut_qubits: int32 [12, 2], P('paths'), parts along dimension 0, may hold values from 0 to 19
- cut_angle: float32 [12], P('paths'), parts along dimension 0, may hold values from 0.6 to 0.97
- path_index: int32 [12], P('paths'), parts along dimension 0, may hold values from 0 to 1
Outputs:
- final_state: float32 [2, 2097152], P(None, ('paths', 'hi')), parts along dimension 1
The draws below stay inside these ranges and needn't reach their ends.
There are 2 independent parts, one for each index of `paths`. The reference program is written for one: setup_inputs(seed, part) draws one part's arguments, and reference() takes and returns one part's arrays. A program takes and returns all parts, laid end to end along the dimension named above; an argument that names none is the same for every part. Nothing has to cross between parts.
All inputs are finite; a program needn't handle non-finite values.
Results may differ from the reference program's by a relative error of at most 0.0003.
Values sent between devices are 32-bit elements; how exact they have to be, the bound alone decides.
No kernel may reach another device: no remote copies, remote signals or barrier semaphores. Data moves between devices by JAX's collectives and lax.ppermute only.
A program may use at most 64 MiB of HBM per device.

```python
import jax
import jax.numpy as jnp
from jax import lax

LOCAL_Q = 16
GLOBAL_Q = 4
QUBITS = 20
AMPS = 1048576
GATE_DIM = 128
LAYERS = 6
PAIRS = 8
CUTS = 6


def set_ends(entries, key, least, top_value):
    dims = entries.shape
    index_at = [jax.random.randint(jax.random.fold_in(key, axis), (), 0, dims[axis]) for axis in range(len(dims))]
    entries = entries.at[tuple(index_at)].set(least)
    longest = dims.index(max(dims))
    index_at[longest] = (index_at[longest] + 1) % dims[longest]
    return entries.at[tuple(index_at)].set(top_value)


def levels(key, extent, cuts, low, high):
    def one(position, parts):
        heights = jax.random.uniform(jax.random.fold_in(jax.random.fold_in(key, 6), position), (parts,), jnp.float32, low / len(cuts), high / len(cuts))
        return jnp.repeat(jnp.exp(heights), extent[position] // parts).reshape((-1,) + (1,) * (len(extent) - position - 1))

    level = one(*cuts[0])
    for cut in cuts[1:]:
        level = level * one(*cut)
    return level


def centred(rng, shape, deviation, bound, cuts=(), held_as=jnp.bfloat16):
    drawn = jax.random.normal(rng, shape, jnp.float32) * deviation
    if len(cuts) > 0:
        drawn = levels(rng, shape, cuts, -0.22, 0.18) * drawn
    return jnp.clip(drawn, min=-bound, max=bound).astype(held_as)


def setup_inputs(seed: int = 0, part: int = 0) -> dict:
    keys = jax.random.split(jax.random.key(seed), 8)
    part_keys = jax.random.split(jax.random.fold_in(keys[7], part), 8)
    return {
        "amplitudes": centred(part_keys[0], (2, AMPS), 1.0, 6.0, ((1, 16),), jnp.float32),
        "gate_matrices": centred(keys[1], (LAYERS, 2, GATE_DIM, GATE_DIM), (2 * GATE_DIM) ** -0.5, 0.375),
        "phase_qubits": set_ends(jax.random.randint(part_keys[2], (LAYERS, PAIRS, 2), 0, QUBITS), jax.random.fold_in(part_keys[2], 1), 0, QUBITS - 1).astype(jnp.int32),
        "phase_angles": jnp.clip(jax.random.uniform(part_keys[3], (LAYERS, PAIRS), jnp.float32, -3.140625, 3.140625), -3.140625, 3.140625),
        "cut_qubits": set_ends(jax.random.randint(part_keys[4], (CUTS, 2), 0, QUBITS), jax.random.fold_in(part_keys[4], 1), 0, QUBITS - 1).astype(jnp.int32),
        "cut_angle": jnp.clip(jax.random.uniform(part_keys[5], (CUTS,), jnp.float32, 0.6, 0.97), 0.6, 0.97),
        "path_index": set_ends(jax.random.randint(part_keys[6], (CUTS,), 0, 2), jax.random.fold_in(part_keys[6], 1), 0, 1).astype(jnp.int32),
    }


def real_form(matrix):
    real_part = matrix[0].astype(jnp.float32)
    imag_part = matrix[1].astype(jnp.float32)
    upper_rows = jnp.stack((real_part, -imag_part), axis=1)
    lower_rows = jnp.stack((imag_part, real_part), axis=1)
    stacked = jnp.stack((upper_rows, lower_rows), axis=0)
    return stacked.reshape(2, 2, 64, 2, 2, 64)


def apply_gate(amps_now, matrix, target, total_bits):
    shaped = amps_now.reshape(2, 2 ** (total_bits - 1 - target), 2, 2 ** (target - 7), 2, 64)
    result = jnp.einsum("wxyzbd,zabced->waxcey", real_form(matrix), shaped,
                        precision=lax.Precision.HIGHEST)
    return result.reshape(2, -1)


def swap_bits(amps_now, low_bit, high_bit, total_bits):
    shaped = amps_now.reshape(2, 2 ** (total_bits - 1 - high_bit), 2, 2 ** (high_bit - low_bit - 1), 2, 2 ** low_bit)
    return jnp.swapaxes(shaped, 2, 4).reshape(2, -1)


def rotate(amps_now, theta):
    cosine = jnp.cos(theta)
    sine = jnp.sin(theta)
    return jnp.stack((cosine * amps_now[0] - sine * amps_now[1], sine * amps_now[0] + cosine * amps_now[1]))


def bit_of(index_all, qubit):
    return jnp.bitwise_and(jnp.right_shift(index_all, qubit), 1)


def reference(amplitudes, gate_matrices, phase_qubits, phase_angles, cut_qubits, cut_angle, path_index):
    total_bits = QUBITS
    index_all = lax.iota(jnp.int32, 2 ** total_bits)
    result = amplitudes
    for layer_number in range(LAYERS):
        if layer_number < GLOBAL_Q:
            result = swap_bits(result, 7 + layer_number, LOCAL_Q + layer_number, total_bits)
            target = 7 + layer_number
        else:
            if layer_number == GLOBAL_Q:
                block_size = 2 ** GLOBAL_Q
                shaped = result.reshape(2, block_size, block_size, 2 ** (LOCAL_Q - GLOBAL_Q))
                result = jnp.swapaxes(shaped, 1, 2).reshape(2, -1)
            target = LOCAL_Q - 2 * GLOBAL_Q + layer_number
        result = apply_gate(result, gate_matrices[layer_number], target, total_bits)
        theta = jnp.zeros((2 ** total_bits,), jnp.float32)
        for pair_number in range(PAIRS):
            first_bit = bit_of(index_all, phase_qubits[layer_number, pair_number, 0])
            second_bit = bit_of(index_all, phase_qubits[layer_number, pair_number, 1])
            theta = theta + phase_angles[layer_number, pair_number] * (first_bit * second_bit).astype(jnp.float32)
        result = rotate(result, theta)
        if layer_number == 0:
            for cut_number in range(CUTS):
                parity = jnp.bitwise_xor(bit_of(index_all, cut_qubits[cut_number, 0]), bit_of(index_all, cut_qubits[cut_number, 1]))
                signs = (1 - 2 * parity).astype(jnp.float32)
                chosen = path_index[cut_number] == 0
                angle_now = cut_angle[cut_number]
                keep_part = jnp.where(chosen, jnp.cos(angle_now), jnp.zeros_like(angle_now))
                turn_part = jnp.where(chosen, jnp.zeros_like(angle_now), jnp.sin(angle_now))
                result = jnp.stack((keep_part * result[0] + turn_part * signs * result[1],
                                    keep_part * result[1] - turn_part * signs * result[0]))
    return result
```

```python
import functools

import jax
import jax.numpy as jnp
import numpy as np
from jax import lax
from jax.experimental import pallas as pl
from jax.experimental.pallas import tpu as pltpu
from jax.sharding import PartitionSpec as P

LANE_BITS = 7
GATE_BITS = 6


def fitted(function, degree):
    nodes = np.cos(np.pi * (np.arange(64) + 0.5) / 64) * 0.125 + 0.125
    series = np.polynomial.chebyshev.Chebyshev.fit(nodes, function(np.sqrt(nodes)), degree, domain=[0, 0.25])
    return [float(c) for c in series.convert(kind=np.polynomial.Polynomial).coef]


COS_TERMS = fitted(lambda v: np.cos(2 * np.pi * v), 7)
SIN_TERMS = fitted(lambda v: np.sin(2 * np.pi * v) / v, 6)


def horner(terms, w):
    total = jnp.full_like(w, terms[-1])
    for term in terms[-2::-1]:
        total = total * w + term
    return total


def turn(angle):
    part = angle - jnp.round(angle)
    square = part * part
    return horner(COS_TERMS, square), part * horner(SIN_TERMS, square)


class Plan:
    def __init__(self, global_count, local_bits, layers):
        self.global_count, self.local_bits, self.layers = global_count, local_bits, layers
        self.top = top = local_bits - global_count
        place = {}
        for label in range(local_bits + global_count):
            if label < top:
                place[label] = label
            elif label < local_bits:
                place[label] = label + global_count
            else:
                place[label] = label - global_count
        held = list(range(local_bits + global_count))
        self.targets = []
        for layer in range(layers):
            if layer < global_count:
                low, high = 7 + layer, local_bits + layer
                held[low], held[high] = held[high], held[low]
                target = low
            else:
                if layer == global_count:
                    held = held[:top] + held[local_bits:] + held[top:local_bits]
                target = local_bits - 2 * global_count + layer
            self.targets.append(place[held[target]])
        assert all(LANE_BITS <= bit < local_bits for bit in self.targets)
        ends = [place[label] for label in held]
        self.extra = sum(ends[local_bits + k] != local_bits + k for k in range(global_count))
        swapped = ends[:]
        for k in range(self.extra):
            low, high = local_bits - self.extra + k, local_bits + k
            assert ends[low] == high
            swapped[low], swapped[high] = ends[high], ends[low]
        assert swapped[local_bits:] == list(range(local_bits, local_bits + global_count))
        assert swapped[:LANE_BITS] == list(range(LANE_BITS))
        self.wanted = swapped[LANE_BITS:local_bits]
        self.orders, self.steps = [], []
        order = list(range(LANE_BITS, local_bits))
        for layer, target in enumerate(self.targets):
            step = 0
            if target in order[:3]:
                def lasts(at):
                    triple = order[at:at + 3]
                    if triple == self.wanted[:3] and not set(triple) & set(self.targets[layer:]):
                        return layers + 1
                    return next((k for k, bit in enumerate(self.targets[layer:]) if bit in triple), layers)
                step = max(range(1, len(order) - 2), key=lasts)
                triple = order[step:step + 3]
                assert target not in triple
                if triple == self.wanted[:3]:
                    order = self.wanted
                else:
                    order = triple + [bit for bit in order if bit not in triple]
            self.steps.append(step)
            self.orders.append(order)

    def locate(self, qubit, layer):
        low, count = 7, min(layer + 1, self.global_count)
        size, high = self.global_count, self.local_bits
        if layer >= size:
            qubit = jnp.where(qubit >= high, qubit - size, jnp.where(qubit >= self.top, qubit + size, qubit))
        up = (qubit >= low) & (qubit < low + count)
        down = (qubit >= high) & (qubit < high + count)
        label = jnp.where(up, qubit + (high - low), jnp.where(down, qubit - (high - low), qubit))
        return jnp.where(label >= high, label - size, jnp.where(label >= self.top, label + size, label))


def tables_kernel(plan, rows, gates, pair_qubits, pair_angles, cut_qubits, cut_angle, path_index,
                  weights, cosines, sines):
    device_part = lax.axis_index("hi") << plan.local_bits
    lane = lax.broadcasted_iota(jnp.int32, (128, 128), 1)
    for layer in range(plan.layers):
        turned = [gates[layer, part].astype(jnp.float32).T for part in range(2)]
        for from_part in range(2):
            for to_part in range(2):
                block = turned[from_part ^ to_part]
                if (from_part, to_part) == (1, 0):
                    block = -block
                for to_bit in range(2):
                    kept = jnp.where((lane >= 64) == (to_bit == 1), block, 0.0)
                    moved = pltpu.roll(kept, 64, 1)
                    first, second = (kept, moved) if to_bit == 0 else (moved, kept)
                    for from_bit in range(2):
                        part = slice(64 * from_bit, 64 * from_bit + 64)
                        both = jnp.concatenate([first[part], second[part]], axis=0)
                        at_row, at_col = 256 * from_part + 128 * from_bit, 256 * to_part + 128 * to_bit
                        weights[layer, at_row:at_row + 128, at_col:at_col + 128] = both.astype(jnp.bfloat16)

    block_rows = 64
    block_bits = block_rows.bit_length() - 1
    row = lax.broadcasted_iota(jnp.int32, (block_rows, 128), 0)
    lanes = lax.broadcasted_iota(jnp.int32, (block_rows, 128), 1)
    for layer in range(plan.layers):
        order = plan.orders[layer]
        base = lanes + device_part
        for bit in range(block_bits):
            base = base + (((row >> bit) & 1) << order[bit])
        masks, turns = [], []
        for pair in range(pair_qubits.shape[1]):
            first = plan.locate(pair_qubits[layer, pair, 0], layer)
            second = plan.locate(pair_qubits[layer, pair, 1], layer)
            one = jnp.int32(1)
            masks.append((one << first) | (one << second))
            turns.append(pair_angles[layer, pair] * np.float32(0.5 / np.pi))
        if layer == 0:
            size = jnp.ones((8, 128), jnp.float32)
            cut_masks, cut_turns = [], []
            for cut in range(cut_qubits.shape[0]):
                first = plan.locate(cut_qubits[cut, 0], layer)
                second = plan.locate(cut_qubits[cut, 1], layer)
                one = jnp.int32(1)
                cut_masks.append((one << first) | (one << second))
                chosen = path_index[cut] == 0
                cosine, sine = turn(jnp.full((8, 128), cut_angle[cut] * np.float32(0.5 / np.pi)))
                size = size * jnp.where(chosen, cosine, sine)
                cut_turns.append(jnp.where(chosen, 0.0, 0.25))
            size = jnp.broadcast_to(size[:1], (block_rows, 128))

        @pl.loop(0, rows // block_rows)
        def _(block):
            offset = jnp.int32(0)
            for bit in range(block_bits, len(order)):
                offset = offset + (((block >> (bit - block_bits)) & 1) << order[bit])
            index = base + offset
            angle = jnp.zeros((block_rows, 128), jnp.float32)
            for mask, amount in zip(masks, turns):
                angle = angle + jnp.where((index & mask) == mask, amount, 0.0)
            if layer == 0:
                for mask, amount in zip(cut_masks, cut_turns):
                    both = index & mask
                    angle = angle + jnp.where((both == 0) | (both == mask), -amount, amount)
            cosine, sine = turn(angle)
            if layer == 0:
                cosine, sine = cosine * size, sine * size
            at = pl.ds(pl.multiple_of(block * block_rows, block_rows), block_rows)
            cosines[layer, at, :] = cosine
            sines[layer, at, :] = sine


def offset_of(number, bits, order):
    return sum(((number >> k) & 1) << order.index(bit) for k, bit in enumerate(bits))


def layers_kernel(plan, rows, state, weights, cosines, sines, out, held):
    order = list(range(LANE_BITS, plan.local_bits))
    for layer in range(plan.layers):
        new_order, step, target = plan.orders[layer], plan.steps[layer], plan.targets[layer]
        rest = [bit for bit in new_order if bit != target]
        pieces = []
        for part in range(2):
            for side in range(2):
                tiles = []
                for tile in range(rows // 16):
                    at = offset_of(tile, rest[3:], order) + side * (1 << order.index(target))
                    if layer == 0:
                        tiles.append(state[pl.ds(2 * at + part, 8, 2 << step), :])
                    elif step:
                        tiles.append(held[(layer - 1) % 2, part, pl.ds(at, 8, 1 << step), :])
                    else:
                        tiles.append(held[(layer - 1) % 2, part, pl.ds(at, 8), :])
                pieces.append(jnp.concatenate(tiles, axis=0))
        joined = jnp.concatenate(pieces, axis=1)
        large = joined.astype(jnp.bfloat16)
        small = (joined - large.astype(jnp.float32)).astype(jnp.bfloat16)
        both = jnp.dot(jnp.concatenate([large, small], axis=0), weights[layer],
                       preferred_element_type=jnp.float32)
        result = both[:rows // 2] + both[rows // 2:]
        for side in range(2):
            for tile in range(rows // 16):
                at = offset_of(tile, rest[3:], new_order) + side * (1 << new_order.index(target))
                real = result[8 * tile:8 * tile + 8, 128 * side:128 * side + 128]
                imag = result[8 * tile:8 * tile + 8, 256 + 128 * side:384 + 128 * side]
                cosine, sine = cosines[layer, at:at + 8, :], sines[layer, at:at + 8, :]
                new_real, new_imag = cosine * real - sine * imag, sine * real + cosine * imag
                if layer == plan.layers - 1:
                    out[pl.ds(2 * at, 8, 2), :] = new_real
                    out[pl.ds(2 * at + 1, 8, 2), :] = new_imag
                else:
                    held[layer % 2, 0, at:at + 8, :] = new_real
                    held[layer % 2, 1, at:at + 8, :] = new_imag
        order = new_order


def shards(
    amplitudes, gate_matrices, phase_qubits, phase_angles, cut_qubits, cut_angle, path_index
):
    devices = lax.axis_size("hi")
    global_count = devices.bit_length() - 1
    amp_count = amplitudes.shape[1]
    rows = amp_count >> LANE_BITS
    layers = gate_matrices.shape[0]
    plan = Plan(global_count, amp_count.bit_length() - 1, layers)

    sent = amplitudes.reshape(2, rows, 128).transpose(1, 0, 2).reshape(devices, -1, 128)
    came = lax.all_to_all(sent, "hi", split_axis=0, concat_axis=0, tiled=True).reshape(2 * rows, 128)

    vmem, smem = pl.BlockSpec(memory_space=pltpu.VMEM), pl.BlockSpec(memory_space=pltpu.SMEM)
    table = jax.ShapeDtypeStruct((layers, rows, 128), jnp.float32)
    weights, cosines, sines = pl.pallas_call(
        functools.partial(tables_kernel, plan, rows),
        out_shape=(jax.ShapeDtypeStruct((layers, 512, 512), jnp.bfloat16), table, table),
        in_specs=[vmem] + [smem] * 5,
        out_specs=[vmem] * 3,
        cost_estimate=pl.CostEstimate(flops=100 * layers * amp_count, bytes_accessed=4 * layers * amp_count, transcendentals=0),
        compiler_params=pltpu.CompilerParams(vmem_limit_bytes=40 << 20),
        name="tables",
    )(gate_matrices, phase_qubits, phase_angles, cut_qubits, cut_angle, path_index)

    result = pl.pallas_call(
        functools.partial(layers_kernel, plan, rows),
        out_shape=jax.ShapeDtypeStruct((2 * rows, 128), jnp.float32),
        in_specs=[vmem] * 4,
        out_specs=vmem,
        scratch_shapes=[pltpu.VMEM((2, 2, rows, 128), jnp.float32)],
        compiler_params=pltpu.CompilerParams(vmem_limit_bytes=40 << 20),
        name="layers",
    )(came, weights, cosines, sines)

    if plan.orders[-1] != plan.wanted:
        bits = len(plan.wanted)
        shaped = result.reshape((2,) * bits + (2, 128))
        axes = [bits - 1 - plan.orders[-1].index(plan.wanted[bits - 1 - axis]) for axis in range(bits)]
        result = shaped.transpose(axes + [bits, bits + 1]).reshape(2 * rows, 128)
    if plan.extra:
        size = 1 << plan.extra
        groups = [list(range(first, first + size)) for first in range(0, devices, size)]
        result = lax.all_to_all(
            result.reshape(size, -1, 128), "hi", split_axis=0, concat_axis=0,
            axis_index_groups=groups, tiled=True,
        )
    return result.reshape(rows, 2, 128).transpose(1, 0, 2).reshape(2, amp_count)


def solution(mesh):
    placed = (
        P(None, ("paths", "hi")),
        P(),
        P("paths", None, None),
        P("paths", None),
        P("paths", None),
        P("paths"),
        P("paths"),
    )
    return jax.shard_map(
        shards, mesh=mesh, in_specs=placed, out_specs=P(None, ("paths", "hi")), check_vma=False
    )
```

```python
import functools

import jax
import jax.numpy as jnp
import numpy as np
from jax import lax
from jax.experimental import pallas as pl
from jax.experimental.layout import Layout, with_layout_constraint
from jax.experimental.pallas import tpu as pltpu
from jax.sharding import PartitionSpec as P

LANE_BITS = 7
GATE_BITS = 6


def fitted(function, degree):
    nodes = np.cos(np.pi * (np.arange(64) + 0.5) / 64) * 0.125 + 0.125
    series = np.polynomial.chebyshev.Chebyshev.fit(nodes, function(np.sqrt(nodes)), degree, domain=[0, 0.25])
    return [float(c) for c in series.convert(kind=np.polynomial.Polynomial).coef]


COS_TERMS = fitted(lambda v: np.cos(2 * np.pi * v), 7)
SIN_TERMS = fitted(lambda v: np.sin(2 * np.pi * v) / v, 6)


def horner(terms, w):
    total = jnp.full_like(w, terms[-1])
    for term in terms[-2::-1]:
        total = total * w + term
    return total


def turn(angle):
    part = angle - jnp.round(angle)
    square = part * part
    return horner(COS_TERMS, square), part * horner(SIN_TERMS, square)


class Plan:
    def __init__(self, global_count, local_bits, layers):
        self.global_count, self.local_bits, self.layers = global_count, local_bits, layers
        self.top = top = local_bits - global_count
        place = {}
        for label in range(local_bits + global_count):
            if label < top:
                place[label] = label
            elif label < local_bits:
                place[label] = label + global_count
            else:
                place[label] = label - global_count
        held = list(range(local_bits + global_count))
        self.targets = []
        for layer in range(layers):
            if layer < global_count:
                low, high = 7 + layer, local_bits + layer
                held[low], held[high] = held[high], held[low]
                target = low
            else:
                if layer == global_count:
                    held = held[:top] + held[local_bits:] + held[top:local_bits]
                target = local_bits - 2 * global_count + layer
            self.targets.append(place[held[target]])
        assert all(LANE_BITS <= bit < local_bits for bit in self.targets)
        ends = [place[label] for label in held]
        self.extra = sum(ends[local_bits + k] != local_bits + k for k in range(global_count))
        swapped = ends[:]
        for k in range(self.extra):
            low, high = local_bits - self.extra + k, local_bits + k
            assert ends[low] == high
            swapped[low], swapped[high] = ends[high], ends[low]
        assert swapped[local_bits:] == list(range(local_bits, local_bits + global_count))
        assert swapped[:LANE_BITS] == list(range(LANE_BITS))
        self.wanted = swapped[LANE_BITS:local_bits]
        self.orders, self.steps = [], []
        order = list(range(LANE_BITS, local_bits))
        for layer, target in enumerate(self.targets):
            step = 0
            if target in order[:3]:
                def lasts(at):
                    triple = order[at:at + 3]
                    if triple == self.wanted[:3] and not set(triple) & set(self.targets[layer:]):
                        return layers + 1
                    return next((k for k, bit in enumerate(self.targets[layer:]) if bit in triple), layers)
                step = max(range(1, len(order) - 2), key=lasts)
                triple = order[step:step + 3]
                assert target not in triple
                if triple == self.wanted[:3]:
                    order = self.wanted
                else:
                    order = triple + [bit for bit in order if bit not in triple]
            self.steps.append(step)
            self.orders.append(order)

    def locate(self, qubit, layer):
        low, count = 7, min(layer + 1, self.global_count)
        size, high = self.global_count, self.local_bits
        if layer >= size:
            qubit = jnp.where(qubit >= high, qubit - size, jnp.where(qubit >= self.top, qubit + size, qubit))
        up = (qubit >= low) & (qubit < low + count)
        down = (qubit >= high) & (qubit < high + count)
        label = jnp.where(up, qubit + (high - low), jnp.where(down, qubit - (high - low), qubit))
        return jnp.where(label >= high, label - size, jnp.where(label >= self.top, label + size, label))


def tables_kernel(plan, rows, gates, pair_qubits, pair_angles, cut_qubits, cut_angle, path_index,
                  weights, cosines, sines):
    device_part = lax.axis_index("hi") << plan.local_bits
    lane = lax.broadcasted_iota(jnp.int32, (128, 128), 1)
    for layer in range(plan.layers):
        turned = [gates[layer, part].astype(jnp.float32).T for part in range(2)]
        for from_part in range(2):
            for to_part in range(2):
                block = turned[from_part ^ to_part]
                if (from_part, to_part) == (1, 0):
                    block = -block
                for to_bit in range(2):
                    kept = jnp.where((lane >= 64) == (to_bit == 1), block, 0.0)
                    moved = pltpu.roll(kept, 64, 1)
                    first, second = (kept, moved) if to_bit == 0 else (moved, kept)
                    for from_bit in range(2):
                        part = slice(64 * from_bit, 64 * from_bit + 64)
                        both = jnp.concatenate([first[part], second[part]], axis=0)
                        at_row, at_col = 256 * from_part + 128 * from_bit, 256 * to_part + 128 * to_bit
                        weights[layer, at_row:at_row + 128, at_col:at_col + 128] = both.astype(jnp.bfloat16)

    block_rows = 64
    block_bits = block_rows.bit_length() - 1
    row = lax.broadcasted_iota(jnp.int32, (block_rows, 128), 0)
    lanes = lax.broadcasted_iota(jnp.int32, (block_rows, 128), 1)
    for layer in range(plan.layers):
        order = plan.orders[layer]
        base = lanes + device_part
        for bit in range(block_bits):
            base = base + (((row >> bit) & 1) << order[bit])
        masks, turns = [], []
        for pair in range(pair_qubits.shape[2]):
            first = plan.locate(pair_qubits[layer, 0, pair], layer)
            second = plan.locate(pair_qubits[layer, 1, pair], layer)
            one = jnp.int32(1)
            masks.append((one << first) | (one << second))
            turns.append(pair_angles[layer, pair] * np.float32(0.5 / np.pi))
        if layer == 0:
            size = jnp.ones((8, 128), jnp.float32)
            cut_masks, cut_turns = [], []
            for cut in range(cut_qubits.shape[1]):
                first = plan.locate(cut_qubits[0, cut], layer)
                second = plan.locate(cut_qubits[1, cut], layer)
                one = jnp.int32(1)
                cut_masks.append((one << first) | (one << second))
                chosen = path_index[cut] == 0
                cosine, sine = turn(jnp.full((8, 128), cut_angle[cut] * np.float32(0.5 / np.pi)))
                size = size * jnp.where(chosen, cosine, sine)
                cut_turns.append(jnp.where(chosen, 0.0, 0.25))
            size = jnp.broadcast_to(size[:1], (block_rows, 128))

        @pl.loop(0, rows // block_rows)
        def _(block):
            offset = jnp.int32(0)
            for bit in range(block_bits, len(order)):
                offset = offset + (((block >> (bit - block_bits)) & 1) << order[bit])
            index = base + offset
            angle = jnp.zeros((block_rows, 128), jnp.float32)
            for mask, amount in zip(masks, turns):
                angle = angle + jnp.where((index & mask) == mask, amount, 0.0)
            if layer == 0:
                for mask, amount in zip(cut_masks, cut_turns):
                    both = index & mask
                    angle = angle + jnp.where((both == 0) | (both == mask), -amount, amount)
            cosine, sine = turn(angle)
            if layer == 0:
                cosine, sine = cosine * size, sine * size
            at = pl.ds(pl.multiple_of(block * block_rows, block_rows), block_rows)
            cosines[layer, at, :] = cosine
            sines[layer, at, :] = sine


def offset_of(number, bits, order):
    return sum(((number >> k) & 1) << order.index(bit) for k, bit in enumerate(bits))


def layers_kernel(plan, rows, count, *refs):
    pieces, (weights, cosines, sines, out, held, state) = refs[:count], refs[count:]
    if count == 1:
        state = pieces[0]
    else:
        size = pieces[0].shape[0]
        for number, piece in enumerate(pieces):
            place = lax.axis_index("hi") ^ number
            state[pl.ds(pl.multiple_of(place * size, size), size), :] = piece[...]
    order = list(range(LANE_BITS, plan.local_bits))
    for layer in range(plan.layers):
        new_order, step, target = plan.orders[layer], plan.steps[layer], plan.targets[layer]
        rest = [bit for bit in new_order if bit != target]
        pieces = []
        for part in range(2):
            for side in range(2):
                tiles = []
                for tile in range(rows // 16):
                    at = offset_of(tile, rest[3:], order) + side * (1 << order.index(target))
                    if layer == 0:
                        tiles.append(state[pl.ds(2 * at + part, 8, 2 << step), :])
                    elif step:
                        tiles.append(held[(layer - 1) % 2, part, pl.ds(at, 8, 1 << step), :])
                    else:
                        tiles.append(held[(layer - 1) % 2, part, pl.ds(at, 8), :])
                pieces.append(jnp.concatenate(tiles, axis=0))
        joined = jnp.concatenate(pieces, axis=1)
        large = joined.astype(jnp.bfloat16)
        small = (joined - large.astype(jnp.float32)).astype(jnp.bfloat16)
        both = jnp.dot(jnp.concatenate([large, small], axis=0), weights[layer],
                       preferred_element_type=jnp.float32)
        result = both[:rows // 2] + both[rows // 2:]
        for side in range(2):
            for tile in range(rows // 16):
                at = offset_of(tile, rest[3:], new_order) + side * (1 << new_order.index(target))
                real = result[8 * tile:8 * tile + 8, 128 * side:128 * side + 128]
                imag = result[8 * tile:8 * tile + 8, 256 + 128 * side:384 + 128 * side]
                cosine, sine = cosines[layer, at:at + 8, :], sines[layer, at:at + 8, :]
                new_real, new_imag = cosine * real - sine * imag, sine * real + cosine * imag
                if layer == plan.layers - 1:
                    out[pl.ds(2 * at, 8, 2), :] = new_real
                    out[pl.ds(2 * at + 1, 8, 2), :] = new_imag
                else:
                    held[layer % 2, 0, at:at + 8, :] = new_real
                    held[layer % 2, 1, at:at + 8, :] = new_imag
        order = new_order


def shards(
    amplitudes, gate_matrices, phase_qubits, phase_angles, cut_qubits, cut_angle, path_index
):
    devices = lax.axis_size("hi")
    global_count = devices.bit_length() - 1
    amp_count = amplitudes.shape[1]
    rows = amp_count >> LANE_BITS
    layers = gate_matrices.shape[0]
    plan = Plan(global_count, amp_count.bit_length() - 1, layers)

    shaped = with_layout_constraint(amplitudes.reshape(2, rows, 128), Layout(major_to_minor=(1, 0, 2)))
    sent = shaped.transpose(1, 0, 2).reshape(devices, -1, 128)
    if devices <= 32:
        place = lax.axis_index("hi")
        pieces = [lax.dynamic_index_in_dim(sent, place ^ k, keepdims=False) for k in range(devices)]
        for k in range(devices - 1, 0, -1):
            pieces[k] = lax.ppermute(pieces[k], "hi", [(i, i ^ k) for i in range(devices)])
    else:
        came = lax.all_to_all(sent, "hi", split_axis=0, concat_axis=0, tiled=True)
        pieces = [came.reshape(2 * rows, 128)]

    vmem, smem = pl.BlockSpec(memory_space=pltpu.VMEM), pl.BlockSpec(memory_space=pltpu.SMEM)
    table = jax.ShapeDtypeStruct((layers, rows, 128), jnp.float32)
    weights, cosines, sines = pl.pallas_call(
        functools.partial(tables_kernel, plan, rows),
        out_shape=(jax.ShapeDtypeStruct((layers, 512, 512), jnp.bfloat16), table, table),
        in_specs=[vmem] + [smem] * 5,
        out_specs=[vmem] * 3,
        cost_estimate=pl.CostEstimate(flops=100 * layers * amp_count, bytes_accessed=4 * layers * amp_count, transcendentals=0),
        compiler_params=pltpu.CompilerParams(vmem_limit_bytes=24 << 20),
        name="tables",
    )(gate_matrices, phase_qubits.transpose(0, 2, 1), phase_angles, cut_qubits.T, cut_angle, path_index)

    result = pl.pallas_call(
        functools.partial(layers_kernel, plan, rows, len(pieces)),
        out_shape=jax.ShapeDtypeStruct((2 * rows, 128), jnp.float32),
        in_specs=[vmem] * (len(pieces) + 3),
        out_specs=vmem,
        scratch_shapes=[pltpu.VMEM((2, 2, rows, 128), jnp.float32), pltpu.VMEM((2 * rows, 128), jnp.float32)],
        compiler_params=pltpu.CompilerParams(vmem_limit_bytes=24 << 20),
        name="layers",
    )(*pieces, weights, cosines, sines)

    if plan.orders[-1] != plan.wanted:
        bits = len(plan.wanted)
        shaped = result.reshape((2,) * bits + (2, 128))
        axes = [bits - 1 - plan.orders[-1].index(plan.wanted[bits - 1 - axis]) for axis in range(bits)]
        result = shaped.transpose(axes + [bits, bits + 1]).reshape(2 * rows, 128)
    if plan.extra:
        size = 1 << plan.extra
        groups = [list(range(first, first + size)) for first in range(0, devices, size)]
        result = lax.all_to_all(
            result.reshape(size, -1, 128), "hi", split_axis=0, concat_axis=0,
            axis_index_groups=groups, tiled=True,
        )
    return result.reshape(rows, 2, 128).transpose(1, 0, 2).reshape(2, amp_count)


def solution(mesh):
    placed = (
        P(None, ("paths", "hi")),
        P(),
        P("paths", None, None),
        P("paths", None),
        P("paths", None),
        P("paths"),
        P("paths"),
    )
    return jax.shard_map(
        shards, mesh=mesh, in_specs=placed, out_specs=P(None, ("paths", "hi")), check_vma=False
    )
```

```python
import functools

import jax
import jax.numpy as jnp
import numpy as np
from jax import lax
from jax.experimental import pallas as pl
from jax.experimental.layout import Layout, with_layout_constraint
from jax.experimental.pallas import tpu as pltpu
from jax.sharding import PartitionSpec as P

LANE_BITS = 7
GATE_BITS = 6


def fitted(function, degree):
    nodes = np.cos(np.pi * (np.arange(64) + 0.5) / 64) * 0.125 + 0.125
    series = np.polynomial.chebyshev.Chebyshev.fit(nodes, function(np.sqrt(nodes)), degree, domain=[0, 0.25])
    return [float(c) for c in series.convert(kind=np.polynomial.Polynomial).coef]


COS_TERMS = fitted(lambda v: np.cos(2 * np.pi * v), 7)
SIN_TERMS = fitted(lambda v: np.sin(2 * np.pi * v) / v, 6)


def horner(terms, w):
    total = jnp.full_like(w, terms[-1])
    for term in terms[-2::-1]:
        total = total * w + term
    return total


def turn(angle):
    part = angle - jnp.round(angle)
    square = part * part
    return horner(COS_TERMS, square), part * horner(SIN_TERMS, square)


class Plan:
    def __init__(self, global_count, local_bits, layers):
        self.global_count, self.local_bits, self.layers = global_count, local_bits, layers
        self.top = top = local_bits - global_count
        place = {}
        for label in range(local_bits + global_count):
            if label < top:
                place[label] = label
            elif label < local_bits:
                place[label] = label + global_count
            else:
                place[label] = label - global_count
        held = list(range(local_bits + global_count))
        self.targets = []
        for layer in range(layers):
            if layer < global_count:
                low, high = 7 + layer, local_bits + layer
                held[low], held[high] = held[high], held[low]
                target = low
            else:
                if layer == global_count:
                    held = held[:top] + held[local_bits:] + held[top:local_bits]
                target = local_bits - 2 * global_count + layer
            self.targets.append(place[held[target]])
        assert all(LANE_BITS <= bit < local_bits for bit in self.targets)
        ends = [place[label] for label in held]
        self.extra = sum(ends[local_bits + k] != local_bits + k for k in range(global_count))
        swapped = ends[:]
        for k in range(self.extra):
            low, high = local_bits - self.extra + k, local_bits + k
            assert ends[low] == high
            swapped[low], swapped[high] = ends[high], ends[low]
        assert swapped[local_bits:] == list(range(local_bits, local_bits + global_count))
        assert swapped[:LANE_BITS] == list(range(LANE_BITS))
        self.wanted = swapped[LANE_BITS:local_bits]
        self.orders, self.steps, self.slots = [], [], []
        order, lane_top = list(range(LANE_BITS, local_bits)), GATE_BITS
        for layer, target in enumerate(self.targets + [GATE_BITS]):
            step = 0
            if target in order[:3]:
                step = max(range(1, len(order) - 2), key=lambda at: self.lasts(order[at:at + 3], layer))
                triple = order[step:step + 3]
                assert target not in triple
                order = triple + [bit for bit in order if bit not in triple]
            slot = order.index(target)
            order = order[:slot] + [lane_top] + order[slot + 1:]
            lane_top = target
            self.steps.append(step)
            self.slots.append(slot)
            self.orders.append(order)
        at = [self.wanted.index(bit) for bit in order[:3]]
        self.direct = at == list(range(at[0], at[0] + 3))

    def lasts(self, triple, layer):
        uses = self.targets[layer:] + [GATE_BITS]
        count = next((k for k, bit in enumerate(uses) if bit in triple), len(uses))
        at = [self.wanted.index(bit) for bit in triple if bit in self.wanted]
        if count == len(uses) and at == list(range(at[0], at[0] + 3)):
            count += 1
        return count

    def locate(self, qubit, layer):
        low, count = 7, min(layer + 1, self.global_count)
        size, high = self.global_count, self.local_bits
        if layer >= size:
            qubit = jnp.where(qubit >= high, qubit - size, jnp.where(qubit >= self.top, qubit + size, qubit))
        up = (qubit >= low) & (qubit < low + count)
        down = (qubit >= high) & (qubit < high + count)
        label = jnp.where(up, qubit + (high - low), jnp.where(down, qubit - (high - low), qubit))
        return jnp.where(label >= high, label - size, jnp.where(label >= self.top, label + size, label))


def tables_kernel(plan, rows, gates, pair_qubits, pair_angles, cut_qubits, cut_angle, path_index,
                  weights, phases, weights_here, phases_here, done):
    device_part = lax.axis_index("hi") << plan.local_bits
    copies = []
    for layer in range(plan.layers):
        real, imag = [gates[layer, part].astype(jnp.float32).T for part in range(2)]
        joined = jnp.concatenate(
            [jnp.concatenate([real, imag], axis=1), jnp.concatenate([-imag, real], axis=1)], axis=0
        )
        weights_here[layer] = joined.astype(jnp.bfloat16)
    copies.append(pltpu.make_async_copy(weights_here, weights, done.at[plan.layers]))
    copies[-1].start()

    block_rows = 64
    block_bits = block_rows.bit_length() - 1
    row = lax.broadcasted_iota(jnp.int32, (block_rows, 128), 0)
    lane = lax.broadcasted_iota(jnp.int32, (block_rows, 128), 1)
    for layer in range(plan.layers):
        order = plan.orders[layer]
        base = (lane & 63) + ((lane >> 6) << plan.targets[layer]) + device_part
        for bit in range(block_bits):
            base = base + (((row >> bit) & 1) << order[bit])
        masks, turns = [], []
        one = jnp.int32(1)
        for pair in range(pair_qubits.shape[2]):
            first = plan.locate(pair_qubits[layer, 0, pair], layer)
            second = plan.locate(pair_qubits[layer, 1, pair], layer)
            masks.append((one << first) | (one << second))
            turns.append(pair_angles[layer, pair] * np.float32(0.5 / np.pi))
        if layer == 0:
            size = jnp.ones((8, 128), jnp.float32)
            cut_masks, cut_turns = [], []
            for cut in range(cut_qubits.shape[1]):
                first = plan.locate(cut_qubits[0, cut], layer)
                second = plan.locate(cut_qubits[1, cut], layer)
                cut_masks.append((one << first) | (one << second))
                chosen = path_index[cut] == 0
                cosine, sine = turn(jnp.full((8, 128), cut_angle[cut] * np.float32(0.5 / np.pi)))
                size = size * jnp.where(chosen, cosine, sine)
                cut_turns.append(jnp.where(chosen, 0.0, 0.25))
            size = jnp.broadcast_to(size[:1], (block_rows, 128))

        @pl.loop(0, rows // block_rows)
        def _(block):
            offset = jnp.int32(0)
            for bit in range(block_bits, len(order)):
                offset = offset + (((block >> (bit - block_bits)) & 1) << order[bit])
            index = base + offset
            angle = jnp.zeros((block_rows, 128), jnp.float32)
            for mask, amount in zip(masks, turns):
                angle = angle + jnp.where((index & mask) == mask, amount, 0.0)
            if layer == 0:
                for mask, amount in zip(cut_masks, cut_turns):
                    both = index & mask
                    angle = angle + jnp.where((both == 0) | (both == mask), -amount, amount)
            cosine, sine = turn(angle)
            if layer == 0:
                cosine, sine = cosine * size, sine * size
            at = pl.ds(pl.multiple_of(block * block_rows, block_rows), block_rows)
            phases_here[layer, 0, at, :] = cosine
            phases_here[layer, 1, at, :] = sine

        copies.append(pltpu.make_async_copy(phases_here.at[layer], phases.at[layer], done.at[layer]))
        copies[-1].start()
    for copy in copies:
        copy.wait()


def offset_of(number, bits, order):
    return sum(((number >> k) & 1) << order.index(bit) for k, bit in enumerate(bits))


def trade(low, high):
    lane = lax.broadcasted_iota(jnp.int32, low.shape, 1)
    return (jnp.where(lane < 64, low, pltpu.roll(high, 64, 1)),
            jnp.where(lane < 64, pltpu.roll(low, 64, 1), high))


def layers_kernel(plan, rows, state, weights, phases, out, state_here, weights_here, phases_here, held, done):
    layers = plan.layers
    copies = [pltpu.make_async_copy(state, state_here, done.at[0])]
    for layer in range(layers):
        copies.append(pltpu.make_async_copy(weights.at[layer], weights_here.at[layer], done.at[1 + 2 * layer]))
        copies.append(pltpu.make_async_copy(phases.at[layer], phases_here.at[layer], done.at[2 + 2 * layer]))
    for copy in copies:
        copy.start()
    copies[0].wait()

    tiles = rows // 8
    old_order = list(range(LANE_BITS, plan.local_bits))
    for layer in range(layers + 1):
        order, step, slot = plan.orders[layer], plan.steps[layer], plan.slots[layer]
        lane_top = plan.targets[layer - 1] if layer else GATE_BITS
        target = (plan.targets + [GATE_BITS])[layer]
        read_order = [target if bit == lane_top else bit for bit in order]
        values = [[None] * tiles, [None] * tiles]
        for tile in range(tiles):
            pair = tile | 1 << (slot - 3)
            if pair == tile:
                continue
            for part in range(2):
                loaded = []
                for number in (tile, pair):
                    at = offset_of(number, read_order[3:], old_order)
                    if layer == 0:
                        loaded.append(state_here[pl.ds(2 * at + part, 8, 2 << step), :])
                    elif step:
                        loaded.append(held[(layer - 1) % 2, part, pl.ds(at, 8, 1 << step), :])
                    else:
                        loaded.append(held[(layer - 1) % 2, part, pl.ds(at, 8), :])
                values[part][tile], values[part][pair] = trade(*loaded)
        old_order = order
        if layer == layers:
            break
        joined = jnp.concatenate([jnp.concatenate(values[part], axis=0) for part in range(2)], axis=1)
        large = joined.astype(jnp.bfloat16)
        small = (joined - large.astype(jnp.float32)).astype(jnp.bfloat16)
        copies[1 + 2 * layer].wait()
        weight = weights_here[layer]
        result = jnp.dot(jnp.concatenate([large, small], axis=1), jnp.concatenate([weight, weight], axis=0),
                         preferred_element_type=jnp.float32)
        real, imag = result[:, :128], result[:, 128:]
        copies[2 + 2 * layer].wait()
        cosine, sine = phases_here[layer, 0], phases_here[layer, 1]
        held[layer % 2, 0] = cosine * real - sine * imag
        held[layer % 2, 1] = sine * real + cosine * imag

    for tile in range(tiles):
        for part in range(2):
            if plan.direct:
                at = offset_of(tile, old_order[3:], plan.wanted)
                stride = 2 << plan.wanted.index(old_order[0])
                out[pl.ds(2 * at + part, 8, stride), :] = values[part][tile]
            else:
                out[pl.ds(16 * tile + part, 8, 2), :] = values[part][tile]


def shards(
    amplitudes, gate_matrices, phase_qubits, phase_angles, cut_qubits, cut_angle, path_index
):
    devices = lax.axis_size("hi")
    global_count = devices.bit_length() - 1
    amp_count = amplitudes.shape[1]
    rows = amp_count >> LANE_BITS
    layers = gate_matrices.shape[0]
    plan = Plan(global_count, amp_count.bit_length() - 1, layers)

    shaped = with_layout_constraint(amplitudes.reshape(2, rows, 128), Layout(major_to_minor=(1, 0, 2)))
    sent = shaped.transpose(1, 0, 2).reshape(devices, -1, 128)
    came = lax.all_to_all(sent, "hi", split_axis=0, concat_axis=0, tiled=True).reshape(2 * rows, 128)

    vmem, smem = pl.BlockSpec(memory_space=pltpu.VMEM), pl.BlockSpec(memory_space=pltpu.SMEM)
    hbm = pl.BlockSpec(memory_space=pltpu.HBM)
    weights_shape, phases_shape = (layers, 256, 256), (layers, 2, rows, 128)
    here = [pltpu.VMEM(weights_shape, jnp.bfloat16), pltpu.VMEM(phases_shape, jnp.float32)]
    weights, phases = pl.pallas_call(
        functools.partial(tables_kernel, plan, rows),
        out_shape=(
            jax.ShapeDtypeStruct(weights_shape, jnp.bfloat16),
            jax.ShapeDtypeStruct(phases_shape, jnp.float32),
        ),
        in_specs=[vmem] + [smem] * 5,
        out_specs=[hbm] * 2,
        scratch_shapes=here + [pltpu.SemaphoreType.DMA((layers + 1,))],
        cost_estimate=pl.CostEstimate(flops=100 * layers * amp_count, bytes_accessed=8 * layers * amp_count, transcendentals=0),
        compiler_params=pltpu.CompilerParams(vmem_limit_bytes=24 << 20),
        name="tables",
    )(gate_matrices, phase_qubits.transpose(0, 2, 1), phase_angles, cut_qubits.T, cut_angle, path_index)

    result = pl.pallas_call(
        functools.partial(layers_kernel, plan, rows),
        out_shape=jax.ShapeDtypeStruct((2 * rows, 128), jnp.float32),
        in_specs=[hbm] * 3,
        out_specs=vmem,
        scratch_shapes=[pltpu.VMEM((2 * rows, 128), jnp.float32)] + here
        + [pltpu.VMEM((2, 2, rows, 128), jnp.float32), pltpu.SemaphoreType.DMA((2 * layers + 1,))],
        compiler_params=pltpu.CompilerParams(vmem_limit_bytes=24 << 20),
        name="layers",
    )(came, weights, phases)

    if not plan.direct:
        bits = len(plan.wanted)
        shaped = result.reshape((2,) * bits + (2, 128))
        axes = [bits - 1 - plan.orders[-1].index(plan.wanted[bits - 1 - axis]) for axis in range(bits)]
        result = shaped.transpose(axes + [bits, bits + 1]).reshape(2 * rows, 128)
    if plan.extra:
        size = 1 << plan.extra
        groups = [list(range(first, first + size)) for first in range(0, devices, size)]
        result = lax.all_to_all(
            result.reshape(size, -1, 128), "hi", split_axis=0, concat_axis=0,
            axis_index_groups=groups, tiled=True,
        )
    return result.reshape(rows, 2, 128).transpose(1, 0, 2).reshape(2, amp_count)


def solution(mesh):
    placed = (
        P(None, ("paths", "hi")),
        P(),
        P("paths", None, None),
        P("paths", None),
        P("paths", None),
        P("paths"),
        P("paths"),
    )
    return jax.shard_map(
        shards, mesh=mesh, in_specs=placed, out_specs=P(None, ("paths", "hi")), check_vma=False
    )
```

```python
import functools

import jax
import jax.numpy as jnp
import numpy as np
from jax import lax
from jax.experimental import pallas as pl
from jax.experimental.layout import Layout, with_layout_constraint
from jax.experimental.pallas import tpu as pltpu
from jax.sharding import PartitionSpec as P

LANE_BITS = 7
GATE_BITS = 6


def fitted(function, degree):
    nodes = np.cos(np.pi * (np.arange(64) + 0.5) / 64) * 0.125 + 0.125
    series = np.polynomial.chebyshev.Chebyshev.fit(nodes, function(np.sqrt(nodes)), degree, domain=[0, 0.25])
    return [float(c) for c in series.convert(kind=np.polynomial.Polynomial).coef]


COS_TERMS = fitted(lambda v: np.cos(2 * np.pi * v), 7)
SIN_TERMS = fitted(lambda v: np.sin(2 * np.pi * v) / v, 6)


def horner(terms, w):
    total = jnp.full_like(w, terms[-1])
    for term in terms[-2::-1]:
        total = total * w + term
    return total


def turn(angle):
    part = angle - jnp.round(angle)
    square = part * part
    return horner(COS_TERMS, square), part * horner(SIN_TERMS, square)


class Plan:
    def __init__(self, global_count, local_bits, layers):
        self.global_count, self.local_bits, self.layers = global_count, local_bits, layers
        self.top = top = local_bits - global_count
        place = {}
        for label in range(local_bits + global_count):
            if label < top:
                place[label] = label
            elif label < local_bits:
                place[label] = label + global_count
            else:
                place[label] = label - global_count
        held = list(range(local_bits + global_count))
        self.targets = []
        for layer in range(layers):
            if layer < global_count:
                low, high = 7 + layer, local_bits + layer
                held[low], held[high] = held[high], held[low]
                target = low
            else:
                if layer == global_count:
                    held = held[:top] + held[local_bits:] + held[top:local_bits]
                target = local_bits - 2 * global_count + layer
            self.targets.append(place[held[target]])
        assert all(LANE_BITS <= bit < local_bits for bit in self.targets)
        ends = [place[label] for label in held]
        self.extra = sum(ends[local_bits + k] != local_bits + k for k in range(global_count))
        swapped = ends[:]
        for k in range(self.extra):
            low, high = local_bits - self.extra + k, local_bits + k
            assert ends[low] == high
            swapped[low], swapped[high] = ends[high], ends[low]
        assert swapped[local_bits:] == list(range(local_bits, local_bits + global_count))
        assert swapped[:LANE_BITS] == list(range(LANE_BITS))
        self.wanted = swapped[LANE_BITS:local_bits]
        self.orders, self.steps, self.slots = [], [], []
        order, lane_top = list(range(LANE_BITS, local_bits)), GATE_BITS
        for layer, target in enumerate(self.targets + [GATE_BITS]):
            step = 0
            if target in order[:3]:
                step = max(range(1, len(order) - 2), key=lambda at: self.lasts(order[at:at + 3], layer))
                triple = order[step:step + 3]
                assert target not in triple
                order = triple + [bit for bit in order if bit not in triple]
            slot = order.index(target)
            order = order[:slot] + [lane_top] + order[slot + 1:]
            lane_top = target
            self.steps.append(step)
            self.slots.append(slot)
            self.orders.append(order)
        at = [self.wanted.index(bit) for bit in order[:3]]
        self.direct = at == list(range(at[0], at[0] + 3))

    def lasts(self, triple, layer):
        uses = self.targets[layer:] + [GATE_BITS]
        count = next((k for k, bit in enumerate(uses) if bit in triple), len(uses))
        at = [self.wanted.index(bit) for bit in triple if bit in self.wanted]
        if count == len(uses) and at == list(range(at[0], at[0] + 3)):
            count += 1
        return count

    def locate(self, qubit, layer):
        low, count = 7, min(layer + 1, self.global_count)
        size, high = self.global_count, self.local_bits
        if layer >= size:
            qubit = jnp.where(qubit >= high, qubit - size, jnp.where(qubit >= self.top, qubit + size, qubit))
        up = (qubit >= low) & (qubit < low + count)
        down = (qubit >= high) & (qubit < high + count)
        label = jnp.where(up, qubit + (high - low), jnp.where(down, qubit - (high - low), qubit))
        return jnp.where(label >= high, label - size, jnp.where(label >= self.top, label + size, label))


def tables_kernel(plan, rows, gates, pair_qubits, pair_angles, cut_qubits, cut_angle, path_index,
                  weights, phases, weights_here, phases_here, done):
    device_part = lax.axis_index("hi") << plan.local_bits
    copies = []
    for layer in range(plan.layers):
        real, imag = [gates[layer, part].astype(jnp.float32).T for part in range(2)]
        joined = jnp.concatenate(
            [jnp.concatenate([real, imag], axis=1), jnp.concatenate([-imag, real], axis=1)], axis=0
        )
        weights_here[layer] = joined.astype(jnp.bfloat16)
    copies.append(pltpu.make_async_copy(weights_here, weights, done.at[plan.layers]))
    copies[-1].start()

    block_rows = 64
    block_bits = block_rows.bit_length() - 1
    row = lax.broadcasted_iota(jnp.int32, (block_rows, 128), 0)
    lane = lax.broadcasted_iota(jnp.int32, (block_rows, 128), 1)
    for layer in range(plan.layers):
        order = plan.orders[layer]
        base = (lane & 63) + ((lane >> 6) << plan.targets[layer]) + device_part
        for bit in range(block_bits):
            base = base + (((row >> bit) & 1) << order[bit])
        masks, turns = [], []
        one = jnp.int32(1)
        for pair in range(pair_qubits.shape[2]):
            first = plan.locate(pair_qubits[layer, 0, pair], layer)
            second = plan.locate(pair_qubits[layer, 1, pair], layer)
            masks.append((one << first) | (one << second))
            turns.append(pair_angles[layer, pair] * np.float32(0.5 / np.pi))
        if layer == 0:
            size = jnp.ones((8, 128), jnp.float32)
            cut_masks, cut_turns = [], []
            for cut in range(cut_qubits.shape[1]):
                first = plan.locate(cut_qubits[0, cut], layer)
                second = plan.locate(cut_qubits[1, cut], layer)
                cut_masks.append((one << first) | (one << second))
                chosen = path_index[cut] == 0
                cosine, sine = turn(jnp.full((8, 128), cut_angle[cut] * np.float32(0.5 / np.pi)))
                size = size * jnp.where(chosen, cosine, sine)
                cut_turns.append(jnp.where(chosen, 0.0, 0.25))
            size = jnp.broadcast_to(size[:1], (block_rows, 128))

        @pl.loop(0, rows // block_rows)
        def _(block):
            offset = jnp.int32(0)
            for bit in range(block_bits, len(order)):
                offset = offset + (((block >> (bit - block_bits)) & 1) << order[bit])
            index = base + offset
            angle = jnp.zeros((block_rows, 128), jnp.float32)
            for mask, amount in zip(masks, turns):
                angle = angle + jnp.where((index & mask) == mask, amount, 0.0)
            if layer == 0:
                for mask, amount in zip(cut_masks, cut_turns):
                    both = index & mask
                    angle = angle + jnp.where((both == 0) | (both == mask), -amount, amount)
            cosine, sine = turn(angle)
            if layer == 0:
                cosine, sine = cosine * size, sine * size
            at = pl.ds(pl.multiple_of(block * block_rows, block_rows), block_rows)
            phases_here[layer, 0, at, :] = cosine
            phases_here[layer, 1, at, :] = sine

        copies.append(pltpu.make_async_copy(phases_here.at[layer], phases.at[layer], done.at[layer]))
        copies[-1].start()
    for copy in copies:
        copy.wait()


def offset_of(number, bits, order):
    return sum(((number >> k) & 1) << order.index(bit) for k, bit in enumerate(bits))


def trade(low, high):
    lane = lax.broadcasted_iota(jnp.int32, low.shape, 1)
    return (jnp.where(lane < 64, low, pltpu.roll(high, 64, 1)),
            jnp.where(lane < 64, pltpu.roll(low, 64, 1), high))


def layers_kernel(plan, rows, state, weights, phases, out, state_here, weights_here, phases_here, held, done):
    layers = plan.layers
    copies = [pltpu.make_async_copy(state, state_here, done.at[0])]
    for layer in range(layers):
        copies.append(pltpu.make_async_copy(weights.at[layer], weights_here.at[layer], done.at[1 + 2 * layer]))
        copies.append(pltpu.make_async_copy(phases.at[layer], phases_here.at[layer], done.at[2 + 2 * layer]))
    for copy in copies:
        copy.start()
    copies[0].wait()

    tiles = rows // 8
    old_order = list(range(LANE_BITS, plan.local_bits))
    for layer in range(layers + 1):
        order, step, slot = plan.orders[layer], plan.steps[layer], plan.slots[layer]
        lane_top = plan.targets[layer - 1] if layer else GATE_BITS
        target = (plan.targets + [GATE_BITS])[layer]
        read_order = [target if bit == lane_top else bit for bit in order]
        values = [[None] * tiles, [None] * tiles]
        for tile in range(tiles):
            pair = tile | 1 << (slot - 3)
            if pair == tile:
                continue
            for part in range(2):
                loaded = []
                for number in (tile, pair):
                    at = offset_of(number, read_order[3:], old_order)
                    if layer == 0:
                        loaded.append(state_here[pl.ds(2 * at + part, 8, 2 << step), :])
                    elif step:
                        loaded.append(held[(layer - 1) % 2, part, pl.ds(at, 8, 1 << step), :])
                    else:
                        loaded.append(held[(layer - 1) % 2, part, pl.ds(at, 8), :])
                values[part][tile], values[part][pair] = trade(*loaded)
        old_order = order
        if layer == layers:
            break
        joined = jnp.concatenate([jnp.concatenate(values[part], axis=0) for part in range(2)], axis=1)
        large = joined.astype(jnp.bfloat16)
        small = (joined - large.astype(jnp.float32)).astype(jnp.bfloat16)
        copies[1 + 2 * layer].wait()
        weight = weights_here[layer]
        result = jnp.dot(jnp.concatenate([large, small], axis=1), jnp.concatenate([weight, weight], axis=0),
                         preferred_element_type=jnp.float32)
        real, imag = result[:, :128], result[:, 128:]
        copies[2 + 2 * layer].wait()
        cosine, sine = phases_here[layer, 0], phases_here[layer, 1]
        held[layer % 2, 0] = cosine * real - sine * imag
        held[layer % 2, 1] = sine * real + cosine * imag

    for tile in range(tiles):
        for part in range(2):
            if plan.direct:
                at = offset_of(tile, old_order[3:], plan.wanted)
                stride = 2 << plan.wanted.index(old_order[0])
                out[pl.ds(2 * at + part, 8, stride), :] = values[part][tile]
            else:
                out[pl.ds(16 * tile + part, 8, 2), :] = values[part][tile]


def shards(
    amplitudes, gate_matrices, phase_qubits, phase_angles, cut_qubits, cut_angle, path_index
):
    devices = lax.axis_size("hi")
    global_count = devices.bit_length() - 1
    amp_count = amplitudes.shape[1]
    rows = amp_count >> LANE_BITS
    layers = gate_matrices.shape[0]
    plan = Plan(global_count, amp_count.bit_length() - 1, layers)

    shaped = with_layout_constraint(amplitudes.reshape(2, rows, 128), Layout(major_to_minor=(1, 0, 2)))
    sent = shaped.transpose(1, 0, 2).reshape(devices, -1, 128)
    came = lax.all_to_all(sent, "hi", split_axis=0, concat_axis=0, tiled=True).reshape(2 * rows, 128)

    vmem, smem = pl.BlockSpec(memory_space=pltpu.VMEM), pl.BlockSpec(memory_space=pltpu.SMEM)
    hbm = pl.BlockSpec(memory_space=pltpu.HBM)
    weights_shape, phases_shape = (layers, 256, 256), (layers, 2, rows, 128)
    here = [pltpu.VMEM(weights_shape, jnp.bfloat16), pltpu.VMEM(phases_shape, jnp.float32)]
    weights, phases = pl.pallas_call(
        functools.partial(tables_kernel, plan, rows),
        out_shape=(
            jax.ShapeDtypeStruct(weights_shape, jnp.bfloat16),
            jax.ShapeDtypeStruct(phases_shape, jnp.float32),
        ),
        in_specs=[vmem] + [smem] * 5,
        out_specs=[hbm] * 2,
        scratch_shapes=here + [pltpu.SemaphoreType.DMA((layers + 1,))],
        cost_estimate=pl.CostEstimate(flops=100 * layers * amp_count, bytes_accessed=8 * layers * amp_count, transcendentals=0),
        compiler_params=pltpu.CompilerParams(vmem_limit_bytes=60 << 20),
        name="tables",
    )(gate_matrices, phase_qubits.transpose(0, 2, 1), phase_angles, cut_qubits.T, cut_angle, path_index)

    result = pl.pallas_call(
        functools.partial(layers_kernel, plan, rows),
        out_shape=jax.ShapeDtypeStruct((2 * rows, 128), jnp.float32),
        in_specs=[hbm] * 3,
        out_specs=vmem,
        scratch_shapes=[pltpu.VMEM((2 * rows, 128), jnp.float32)] + here
        + [pltpu.VMEM((2, 2, rows, 128), jnp.float32), pltpu.SemaphoreType.DMA((2 * layers + 1,))],
        compiler_params=pltpu.CompilerParams(vmem_limit_bytes=60 << 20),
        name="layers",
    )(came, weights, phases)

    if not plan.direct:
        bits = len(plan.wanted)
        shaped = result.reshape((2,) * bits + (2, 128))
        axes = [bits - 1 - plan.orders[-1].index(plan.wanted[bits - 1 - axis]) for axis in range(bits)]
        result = shaped.transpose(axes + [bits, bits + 1]).reshape(2 * rows, 128)
    if plan.extra:
        size = 1 << plan.extra
        groups = [list(range(first, first + size)) for first in range(0, devices, size)]
        result = lax.all_to_all(
            result.reshape(size, -1, 128), "hi", split_axis=0, concat_axis=0,
            axis_index_groups=groups, tiled=True,
        )
    return result.reshape(rows, 2, 128).transpose(1, 0, 2).reshape(2, amp_count)


def solution(mesh):
    placed = (
        P(None, ("paths", "hi")),
        P(),
        P("paths", None, None),
        P("paths", None),
        P("paths", None),
        P("paths"),
        P("paths"),
    )
    return jax.shard_map(
        shards, mesh=mesh, in_specs=placed, out_specs=P(None, ("paths", "hi")), check_vma=False
    )
```

```python
import functools

import jax
import jax.numpy as jnp
import numpy as np
from jax import lax
from jax.experimental import pallas as pl
from jax.experimental.layout import Layout, with_layout_constraint
from jax.experimental.pallas import tpu as pltpu
from jax.sharding import PartitionSpec as P

LANE_BITS = 7
GATE_BITS = 6


def fitted(function, degree):
    nodes = np.cos(np.pi * (np.arange(64) + 0.5) / 64) * 0.125 + 0.125
    series = np.polynomial.chebyshev.Chebyshev.fit(nodes, function(np.sqrt(nodes)), degree, domain=[0, 0.25])
    return [float(c) for c in series.convert(kind=np.polynomial.Polynomial).coef]


COS_TERMS = fitted(lambda v: np.cos(2 * np.pi * v), 7)
SIN_TERMS = fitted(lambda v: np.sin(2 * np.pi * v) / v, 6)


def horner(terms, w):
    total = jnp.full_like(w, terms[-1])
    for term in terms[-2::-1]:
        total = total * w + term
    return total


def turn(angle):
    part = angle - jnp.round(angle)
    square = part * part
    return horner(COS_TERMS, square), part * horner(SIN_TERMS, square)


class Plan:
    def __init__(self, global_count, local_bits, layers):
        self.global_count, self.local_bits, self.layers = global_count, local_bits, layers
        self.top = top = local_bits - global_count
        place = {}
        for label in range(local_bits + global_count):
            if label < top:
                place[label] = label
            elif label < local_bits:
                place[label] = label + global_count
            else:
                place[label] = label - global_count
        held = list(range(local_bits + global_count))
        self.targets = []
        for layer in range(layers):
            if layer < global_count:
                low, high = 7 + layer, local_bits + layer
                held[low], held[high] = held[high], held[low]
                target = low
            else:
                if layer == global_count:
                    held = held[:top] + held[local_bits:] + held[top:local_bits]
                target = local_bits - 2 * global_count + layer
            self.targets.append(place[held[target]])
        assert all(LANE_BITS <= bit < local_bits for bit in self.targets)
        ends = [place[label] for label in held]
        self.extra = sum(ends[local_bits + k] != local_bits + k for k in range(global_count))
        swapped = ends[:]
        for k in range(self.extra):
            low, high = local_bits - self.extra + k, local_bits + k
            assert ends[low] == high
            swapped[low], swapped[high] = ends[high], ends[low]
        assert swapped[local_bits:] == list(range(local_bits, local_bits + global_count))
        assert swapped[:LANE_BITS] == list(range(LANE_BITS))
        self.wanted = swapped[LANE_BITS:local_bits]
        self.orders, self.steps = [], []
        order = list(range(LANE_BITS, local_bits))
        for layer, target in enumerate(self.targets):
            step = 0
            if target in order[:4]:
                step = max(range(1, len(order) - 2), key=lambda at: self.lasts(order[at:at + 3], layer))
                triple = order[step:step + 3]
                if triple == self.wanted[:3] and not set(self.wanted[:4]) & set(self.targets[layer:]):
                    order = self.wanted
                else:
                    rest = sorted((bit for bit in order if bit not in triple), key=lambda bit: -self.lasts([bit], layer))
                    order = triple + rest
                assert target not in order[:4]
            self.steps.append(step)
            self.orders.append(order)

    def lasts(self, bits, layer):
        uses = self.targets[layer:]
        count = next((k for k, bit in enumerate(uses) if bit in bits), len(uses))
        return count + (count == len(uses) and bits == self.wanted[:3])

    def locate(self, qubit, layer):
        low, count = 7, min(layer + 1, self.global_count)
        size, high = self.global_count, self.local_bits
        if layer >= size:
            qubit = jnp.where(qubit >= high, qubit - size, jnp.where(qubit >= self.top, qubit + size, qubit))
        up = (qubit >= low) & (qubit < low + count)
        down = (qubit >= high) & (qubit < high + count)
        label = jnp.where(up, qubit + (high - low), jnp.where(down, qubit - (high - low), qubit))
        return jnp.where(label >= high, label - size, jnp.where(label >= self.top, label + size, label))


def tables_kernel(plan, rows, gates, pair_qubits, pair_angles, cut_qubits, cut_angle, path_index,
                  weights, phases, weights_here, phases_here, done):
    device_part = lax.axis_index("hi") << plan.local_bits
    copies = []
    lane = lax.broadcasted_iota(jnp.int32, (128, 128), 1)
    for layer in range(plan.layers):
        turned = [gates[layer, part].astype(jnp.float32).T for part in range(2)]
        for from_part in range(2):
            for to_part in range(2):
                block = turned[from_part ^ to_part]
                if (from_part, to_part) == (1, 0):
                    block = -block
                for to_bit in range(2):
                    kept = jnp.where((lane >= 64) == (to_bit == 1), block, 0.0)
                    moved = pltpu.roll(kept, 64, 1)
                    first, second = (kept, moved) if to_bit == 0 else (moved, kept)
                    for from_bit in range(2):
                        part = slice(64 * from_bit, 64 * from_bit + 64)
                        both = jnp.concatenate([first[part], second[part]], axis=0)
                        at_row, at_col = 256 * from_part + 128 * from_bit, 256 * to_part + 128 * to_bit
                        weights_here[layer, at_row:at_row + 128, at_col:at_col + 128] = both.astype(jnp.bfloat16)
        copies.append(pltpu.make_async_copy(weights_here.at[layer], weights.at[layer], done.at[layer]))
        copies[-1].start()

    block_rows = 64
    block_bits = block_rows.bit_length() - 1
    row = lax.broadcasted_iota(jnp.int32, (block_rows, 128), 0)
    lane = lax.broadcasted_iota(jnp.int32, (block_rows, 128), 1)
    for layer in range(plan.layers):
        order = plan.orders[layer]
        base = lane + device_part
        for bit in range(block_bits):
            base = base + (((row >> bit) & 1) << order[bit])
        masks, turns = [], []
        one = jnp.int32(1)
        for pair in range(pair_qubits.shape[2]):
            first = plan.locate(pair_qubits[layer, 0, pair], layer)
            second = plan.locate(pair_qubits[layer, 1, pair], layer)
            masks.append((one << first) | (one << second))
            turns.append(pair_angles[layer, pair] * np.float32(0.5 / np.pi))
        if layer == 0:
            size = jnp.ones((8, 128), jnp.float32)
            cut_masks, cut_turns = [], []
            for cut in range(cut_qubits.shape[1]):
                first = plan.locate(cut_qubits[0, cut], layer)
                second = plan.locate(cut_qubits[1, cut], layer)
                cut_masks.append((one << first) | (one << second))
                chosen = path_index[cut] == 0
                cosine, sine = turn(jnp.full((8, 128), cut_angle[cut] * np.float32(0.5 / np.pi)))
                size = size * jnp.where(chosen, cosine, sine)
                cut_turns.append(jnp.where(chosen, 0.0, 0.25))
            size = jnp.broadcast_to(size[:1], (block_rows, 128))

        @pl.loop(0, rows // block_rows)
        def _(block):
            offset = jnp.int32(0)
            for bit in range(block_bits, len(order)):
                offset = offset + (((block >> (bit - block_bits)) & 1) << order[bit])
            index = base + offset
            angle = jnp.zeros((block_rows, 128), jnp.float32)
            for mask, amount in zip(masks, turns):
                angle = angle + jnp.where((index & mask) == mask, amount, 0.0)
            if layer == 0:
                for mask, amount in zip(cut_masks, cut_turns):
                    both = index & mask
                    angle = angle + jnp.where((both == 0) | (both == mask), -amount, amount)
            cosine, sine = turn(angle)
            if layer == 0:
                cosine, sine = cosine * size, sine * size
            at = pl.ds(pl.multiple_of(block * block_rows, block_rows), block_rows)
            phases_here[layer, 0, at, :] = cosine
            phases_here[layer, 1, at, :] = sine

        copies.append(pltpu.make_async_copy(phases_here.at[layer], phases.at[layer], done.at[plan.layers + layer]))
        copies[-1].start()
    for copy in copies:
        copy.wait()


def offset_of(number, bits, order):
    return sum(((number >> k) & 1) << order.index(bit) for k, bit in enumerate(bits))


def split(values):
    large = values.astype(jnp.bfloat16)
    return large, (values - large.astype(jnp.float32)).astype(jnp.bfloat16)


def layers_kernel(plan, rows, state, weights, phases, out, weights_here, phases_here, held, parts, done):
    layers = plan.layers
    copies = []
    for layer in range(layers):
        copies.append(pltpu.make_async_copy(weights.at[layer], weights_here.at[layer], done.at[2 * layer]))
        copies.append(pltpu.make_async_copy(phases.at[layer], phases_here.at[layer], done.at[2 * layer + 1]))
    for copy in copies:
        copy.start()

    old_order = list(range(LANE_BITS, plan.local_bits))
    for layer in range(layers):
        order, step, target = plan.orders[layer], plan.steps[layer], plan.targets[layer]
        rest = [bit for bit in order if bit != target]
        pieces = []
        for part in range(2):
            for side in range(2):
                if layer == 0 or step:
                    tiles = []
                    for tile in range(rows // 16):
                        at = offset_of(tile, rest[3:], old_order) + (side << old_order.index(target))
                        if layer == 0:
                            tiles.append(state[pl.ds(2 * at + part, 8, 2 << step), :])
                        else:
                            tiles.append(held[part, pl.ds(at, 8, 1 << step), :])
                    pieces.append(split(jnp.concatenate(tiles, axis=0)))
                else:
                    starts = [offset_of(tile, rest[4:], order) + (side << order.index(target))
                              for tile in range(rows // 32)]
                    pieces.append([
                        jnp.concatenate([parts[layer % 2, size, part, at:at + 16, :] for at in starts], axis=0)
                        for size in range(2)
                    ])
        joined = jnp.concatenate(
            [jnp.concatenate([piece[size] for piece in pieces], axis=1) for size in range(2)], axis=0
        )
        copies[2 * layer].wait()
        both = jnp.dot(joined, weights_here[layer], preferred_element_type=jnp.float32)
        result = both[:rows // 2] + both[rows // 2:]
        copies[2 * layer + 1].wait()
        for side in range(2):
            for tile in range(rows // 32):
                at = offset_of(tile, rest[4:], order) + (side << order.index(target))
                real = result[16 * tile:16 * tile + 16, 128 * side:128 * side + 128]
                imag = result[16 * tile:16 * tile + 16, 256 + 128 * side:384 + 128 * side]
                cosine, sine = phases_here[layer, 0, at:at + 16, :], phases_here[layer, 1, at:at + 16, :]
                for part, value in enumerate((cosine * real - sine * imag, sine * real + cosine * imag)):
                    if layer == layers - 1:
                        out[pl.ds(2 * at + part, 16, 2), :] = value
                    elif plan.steps[layer + 1]:
                        held[part, at:at + 16, :] = value
                    else:
                        large, small = split(value)
                        parts[(layer + 1) % 2, 0, part, at:at + 16, :] = large
                        parts[(layer + 1) % 2, 1, part, at:at + 16, :] = small
        old_order = order


def shards(
    amplitudes, gate_matrices, phase_qubits, phase_angles, cut_qubits, cut_angle, path_index
):
    devices = lax.axis_size("hi")
    global_count = devices.bit_length() - 1
    amp_count = amplitudes.shape[1]
    rows = amp_count >> LANE_BITS
    layers = gate_matrices.shape[0]
    plan = Plan(global_count, amp_count.bit_length() - 1, layers)

    shaped = with_layout_constraint(amplitudes.reshape(2, rows, 128), Layout(major_to_minor=(1, 0, 2)))
    sent = shaped.transpose(1, 0, 2).reshape(devices, -1, 128)
    came = lax.all_to_all(sent, "hi", split_axis=0, concat_axis=0, tiled=True).reshape(2 * rows, 128)

    vmem, smem = pl.BlockSpec(memory_space=pltpu.VMEM), pl.BlockSpec(memory_space=pltpu.SMEM)
    hbm = pl.BlockSpec(memory_space=pltpu.HBM)
    weights_shape, phases_shape = (layers, 512, 512), (layers, 2, rows, 128)
    here = [pltpu.VMEM(weights_shape, jnp.bfloat16), pltpu.VMEM(phases_shape, jnp.float32)]
    weights, phases = pl.pallas_call(
        functools.partial(tables_kernel, plan, rows),
        out_shape=(
            jax.ShapeDtypeStruct(weights_shape, jnp.bfloat16),
            jax.ShapeDtypeStruct(phases_shape, jnp.float32),
        ),
        in_specs=[vmem] + [smem] * 5,
        out_specs=[hbm] * 2,
        scratch_shapes=here + [pltpu.SemaphoreType.DMA((2 * layers,))],
        cost_estimate=pl.CostEstimate(flops=100 * layers * amp_count, bytes_accessed=8 * layers * amp_count, transcendentals=0),
        compiler_params=pltpu.CompilerParams(vmem_limit_bytes=60 << 20),
        name="tables",
    )(gate_matrices, phase_qubits.transpose(0, 2, 1), phase_angles, cut_qubits.T, cut_angle, path_index)

    result = pl.pallas_call(
        functools.partial(layers_kernel, plan, rows),
        out_shape=jax.ShapeDtypeStruct((2 * rows, 128), jnp.float32),
        in_specs=[vmem, hbm, hbm],
        out_specs=vmem,
        scratch_shapes=here + [
            pltpu.VMEM((2, rows, 128), jnp.float32),
            pltpu.VMEM((2, 2, 2, rows, 128), jnp.bfloat16),
            pltpu.SemaphoreType.DMA((2 * layers,)),
        ],
        compiler_params=pltpu.CompilerParams(vmem_limit_bytes=58 << 20),
        name="layers",
    )(came, weights, phases)

    if plan.orders[-1] != plan.wanted:
        bits = len(plan.wanted)
        shaped = result.reshape((2,) * bits + (2, 128))
        axes = [bits - 1 - plan.orders[-1].index(plan.wanted[bits - 1 - axis]) for axis in range(bits)]
        result = shaped.transpose(axes + [bits, bits + 1]).reshape(2 * rows, 128)
    if plan.extra:
        size = 1 << plan.extra
        groups = [list(range(first, first + size)) for first in range(0, devices, size)]
        result = lax.all_to_all(
            result.reshape(size, -1, 128), "hi", split_axis=0, concat_axis=0,
            axis_index_groups=groups, tiled=True,
        )
    return result.reshape(rows, 2, 128).transpose(1, 0, 2).reshape(2, amp_count)


def solution(mesh):
    placed = (
        P(None, ("paths", "hi")),
        P(),
        P("paths", None, None),
        P("paths", None),
        P("paths", None),
        P("paths"),
        P("paths"),
    )
    return jax.shard_map(
        shards, mesh=mesh, in_specs=placed, out_specs=P(None, ("paths", "hi")), check_vma=False
    )
```

```python
import functools

import jax
import jax.numpy as jnp
import numpy as np
from jax import lax
from jax.experimental import pallas as pl
from jax.experimental.layout import Layout, with_layout_constraint
from jax.experimental.pallas import tpu as pltpu
from jax.sharding import PartitionSpec as P

LANE_BITS = 7
GATE_BITS = 6
STEPS = 32767.0


def fitted(function, degree):
    nodes = np.cos(np.pi * (np.arange(64) + 0.5) / 64) * 0.125 + 0.125
    series = np.polynomial.chebyshev.Chebyshev.fit(nodes, function(np.sqrt(nodes)), degree, domain=[0, 0.25])
    return [float(c) for c in series.convert(kind=np.polynomial.Polynomial).coef]


COS_TERMS = fitted(lambda v: np.cos(2 * np.pi * v), 7)
SIN_TERMS = fitted(lambda v: np.sin(2 * np.pi * v) / v, 6)


def horner(terms, w):
    total = jnp.full_like(w, terms[-1])
    for term in terms[-2::-1]:
        total = total * w + term
    return total


def turn(angle):
    part = angle - jnp.round(angle)
    square = part * part
    return horner(COS_TERMS, square), part * horner(SIN_TERMS, square)


class Plan:
    def __init__(self, global_count, local_bits, layers):
        self.global_count, self.local_bits, self.layers = global_count, local_bits, layers
        self.top = top = local_bits - global_count
        place = {}
        for label in range(local_bits + global_count):
            if label < top:
                place[label] = label
            elif label < local_bits:
                place[label] = label + global_count
            else:
                place[label] = label - global_count
        held = list(range(local_bits + global_count))
        self.targets = []
        for layer in range(layers):
            if layer < global_count:
                low, high = 7 + layer, local_bits + layer
                held[low], held[high] = held[high], held[low]
                target = low
            else:
                if layer == global_count:
                    held = held[:top] + held[local_bits:] + held[top:local_bits]
                target = local_bits - 2 * global_count + layer
            self.targets.append(place[held[target]])
        assert all(LANE_BITS <= bit < local_bits for bit in self.targets)
        ends = [place[label] for label in held]
        self.extra = sum(ends[local_bits + k] != local_bits + k for k in range(global_count))
        swapped = ends[:]
        for k in range(self.extra):
            low, high = local_bits - self.extra + k, local_bits + k
            assert ends[low] == high
            swapped[low], swapped[high] = ends[high], ends[low]
        assert swapped[local_bits:] == list(range(local_bits, local_bits + global_count))
        assert swapped[:LANE_BITS] == list(range(LANE_BITS))
        self.wanted = swapped[LANE_BITS:local_bits]
        self.orders, self.steps = [], []
        order = list(range(LANE_BITS, local_bits))
        for layer, target in enumerate(self.targets):
            step = 0
            if target in order[:4]:
                step = max(range(1, len(order) - 2), key=lambda at: self.lasts(order[at:at + 3], layer))
                triple = order[step:step + 3]
                if triple == self.wanted[:3] and not set(self.wanted[:4]) & set(self.targets[layer:]):
                    order = self.wanted
                else:
                    rest = sorted((bit for bit in order if bit not in triple), key=lambda bit: -self.lasts([bit], layer))
                    order = triple + rest
                assert target not in order[:4]
            self.steps.append(step)
            self.orders.append(order)

    def lasts(self, bits, layer):
        uses = self.targets[layer:]
        count = next((k for k, bit in enumerate(uses) if bit in bits), len(uses))
        return count + (count == len(uses) and bits == self.wanted[:3])

    def locate(self, qubit, layer):
        low, count = 7, min(layer + 1, self.global_count)
        size, high = self.global_count, self.local_bits
        if layer >= size:
            qubit = jnp.where(qubit >= high, qubit - size, jnp.where(qubit >= self.top, qubit + size, qubit))
        up = (qubit >= low) & (qubit < low + count)
        down = (qubit >= high) & (qubit < high + count)
        label = jnp.where(up, qubit + (high - low), jnp.where(down, qubit - (high - low), qubit))
        return jnp.where(label >= high, label - size, jnp.where(label >= self.top, label + size, label))


def tables_kernel(plan, rows, gates, pair_qubits, pair_angles, cut_qubits, cut_angle, path_index,
                  near, far, phases, sizes, far_here, done):
    device_part = lax.axis_index("hi") << plan.local_bits
    lane = lax.broadcasted_iota(jnp.int32, (128, 128), 1)
    for layer in range(plan.layers - 1, -1, -1):
        for kind in range(2):
            turned = gates[layer, kind].astype(jnp.float32).T
            for to_bit in range(2):
                kept = jnp.where((lane >= 64) == (to_bit == 1), turned, 0.0)
                moved = pltpu.roll(kept, 64, 1)
                first, second = (kept, moved) if to_bit == 0 else (moved, kept)
                for from_bit in range(2):
                    part = slice(64 * from_bit, 64 * from_bit + 64)
                    both = jnp.concatenate([first[part], second[part]], axis=0).astype(jnp.bfloat16)
                    at_row, at_col = slice(128 * from_bit, 128 * from_bit + 128), slice(128 * to_bit, 128 * to_bit + 128)
                    if layer == plan.layers - 1:
                        far_here[kind, at_row, at_col] = both
                    else:
                        near[layer, kind, at_row, at_col] = both
        if layer == plan.layers - 1:
            copy = pltpu.make_async_copy(far_here, far, done)
            copy.start()

    block_rows = 64
    block_bits = block_rows.bit_length() - 1
    row = lax.broadcasted_iota(jnp.int32, (block_rows, 128), 0)
    lane = lax.broadcasted_iota(jnp.int32, (block_rows, 128), 1)
    for layer in range(plan.layers):
        order = plan.orders[layer]
        base = lane + device_part
        for bit in range(block_bits):
            base = base + (((row >> bit) & 1) << order[bit])
        masks, turns = [], []
        one = jnp.int32(1)
        for pair in range(pair_qubits.shape[2]):
            first = plan.locate(pair_qubits[layer, 0, pair], layer)
            second = plan.locate(pair_qubits[layer, 1, pair], layer)
            masks.append((one << first) | (one << second))
            turns.append(pair_angles[layer, pair] * np.float32(0.5 / np.pi))
        if layer == 0:
            size = jnp.ones((8, 128), jnp.float32)
            cut_masks, cut_turns = [], []
            for cut in range(cut_qubits.shape[1]):
                first = plan.locate(cut_qubits[0, cut], layer)
                second = plan.locate(cut_qubits[1, cut], layer)
                cut_masks.append((one << first) | (one << second))
                chosen = path_index[cut] == 0
                cosine, sine = turn(jnp.full((8, 128), cut_angle[cut] * np.float32(0.5 / np.pi)))
                size = size * jnp.where(chosen, cosine, sine)
                cut_turns.append(jnp.where(chosen, 0.0, 0.25))
            sizes[...] = size

        @pl.loop(0, rows // block_rows)
        def _(block):
            offset = jnp.int32(0)
            for bit in range(block_bits, len(order)):
                offset = offset + (((block >> (bit - block_bits)) & 1) << order[bit])
            index = base + offset
            angle = jnp.zeros((block_rows, 128), jnp.float32)
            for mask, amount in zip(masks, turns):
                angle = angle + jnp.where((index & mask) == mask, amount, 0.0)
            if layer == 0:
                for mask, amount in zip(cut_masks, cut_turns):
                    both = index & mask
                    angle = angle + jnp.where((both == 0) | (both == mask), -amount, amount)
            cosine, sine = turn(angle)
            at = pl.ds(pl.multiple_of(block * block_rows, block_rows), block_rows)
            cosine = jnp.round(cosine * STEPS).astype(jnp.int32)
            sine = jnp.round(sine * STEPS).astype(jnp.int32)
            phases[layer, at, :] = (cosine << 16) | (sine & 0xFFFF)

    copy.wait()


def offset_of(number, bits, order):
    return sum(((number >> k) & 1) << order.index(bit) for k, bit in enumerate(bits))


def split(values):
    large = values.astype(jnp.bfloat16)
    return large, (values - large.astype(jnp.float32)).astype(jnp.bfloat16)


def layers_kernel(plan, rows, state, near, far, phases, sizes, out, far_here, held, parts, done):
    layers = plan.layers
    copy = pltpu.make_async_copy(far, far_here, done)
    copy.start()

    old_order = list(range(LANE_BITS, plan.local_bits))
    for layer in range(layers):
        order, step, target = plan.orders[layer], plan.steps[layer], plan.targets[layer]
        rest = [bit for bit in order if bit != target]
        pieces = []
        for part in range(2):
            for side in range(2):
                if layer == 0 or step:
                    tiles = []
                    for tile in range(rows // 16):
                        at = offset_of(tile, rest[3:], old_order) + (side << old_order.index(target))
                        if layer == 0:
                            tiles.append(state[pl.ds(2 * at + part, 8, 2 << step), :])
                        else:
                            tiles.append(held[part, pl.ds(at, 8, 1 << step), :])
                    pieces.append(split(jnp.concatenate(tiles, axis=0)))
                else:
                    starts = [offset_of(tile, rest[4:], order) + (side << order.index(target))
                              for tile in range(rows // 32)]
                    pieces.append([
                        jnp.concatenate([parts[layer % 2, size, part, at:at + 16, :] for at in starts], axis=0)
                        for size in range(2)
                    ])
        joined = jnp.concatenate(
            [jnp.concatenate([piece[size] for piece in pieces], axis=1) for size in range(2)], axis=0
        )
        if layer == layers - 1:
            copy.wait()
            weights = far_here
        else:
            weights = near.at[layer]
        real, imag = weights[0], weights[1]
        weight = jnp.concatenate(
            [jnp.concatenate([real, imag], axis=1), jnp.concatenate([-imag, real], axis=1)], axis=0
        )
        both = jnp.dot(joined, weight, preferred_element_type=jnp.float32)
        result = both[:rows // 2] + both[rows // 2:]
        unit = jnp.full((16, 128), 1 / STEPS, jnp.float32)
        if layer == 0:
            unit = unit * sizes[0:1, :]
        for side in range(2):
            for tile in range(rows // 32):
                at = offset_of(tile, rest[4:], order) + (side << order.index(target))
                real = result[16 * tile:16 * tile + 16, 128 * side:128 * side + 128]
                imag = result[16 * tile:16 * tile + 16, 256 + 128 * side:384 + 128 * side]
                word = phases[layer, at:at + 16, :]
                cosine = (word >> 16).astype(jnp.float32) * unit
                sine = ((word << 16) >> 16).astype(jnp.float32) * unit
                for part, value in enumerate((cosine * real - sine * imag, sine * real + cosine * imag)):
                    if layer == layers - 1:
                        out[pl.ds(2 * at + part, 16, 2), :] = value
                    elif plan.steps[layer + 1]:
                        held[part, at:at + 16, :] = value
                    else:
                        large, small = split(value)
                        parts[(layer + 1) % 2, 0, part, at:at + 16, :] = large
                        parts[(layer + 1) % 2, 1, part, at:at + 16, :] = small
        old_order = order


def shards(
    amplitudes, gate_matrices, phase_qubits, phase_angles, cut_qubits, cut_angle, path_index
):
    devices = lax.axis_size("hi")
    global_count = devices.bit_length() - 1
    amp_count = amplitudes.shape[1]
    rows = amp_count >> LANE_BITS
    layers = gate_matrices.shape[0]
    plan = Plan(global_count, amp_count.bit_length() - 1, layers)

    shaped = with_layout_constraint(amplitudes.reshape(2, rows, 128), Layout(major_to_minor=(1, 0, 2)))
    sent = shaped.transpose(1, 0, 2).reshape(devices, -1, 128)
    came = lax.all_to_all(sent, "hi", split_axis=0, concat_axis=0, tiled=True).reshape(2 * rows, 128)

    vmem, smem = pl.BlockSpec(memory_space=pltpu.VMEM), pl.BlockSpec(memory_space=pltpu.SMEM)
    hbm = pl.BlockSpec(memory_space=pltpu.HBM)
    weights_shape = (2, 256, 256)
    near, far, phases, sizes = pl.pallas_call(
        functools.partial(tables_kernel, plan, rows),
        out_shape=(
            jax.ShapeDtypeStruct((layers - 1,) + weights_shape, jnp.bfloat16),
            jax.ShapeDtypeStruct(weights_shape, jnp.bfloat16),
            jax.ShapeDtypeStruct((layers, rows, 128), jnp.int32),
            jax.ShapeDtypeStruct((8, 128), jnp.float32),
        ),
        in_specs=[vmem] + [smem] * 5,
        out_specs=[vmem, hbm, vmem, vmem],
        scratch_shapes=[pltpu.VMEM(weights_shape, jnp.bfloat16), pltpu.SemaphoreType.DMA],
        cost_estimate=pl.CostEstimate(flops=100 * layers * amp_count, bytes_accessed=4 * layers * amp_count, transcendentals=0),
        compiler_params=pltpu.CompilerParams(vmem_limit_bytes=24 << 20),
        name="tables",
    )(gate_matrices, phase_qubits.transpose(0, 2, 1), phase_angles, cut_qubits.T, cut_angle, path_index)

    result = pl.pallas_call(
        functools.partial(layers_kernel, plan, rows),
        out_shape=jax.ShapeDtypeStruct((2 * rows, 128), jnp.float32),
        in_specs=[vmem, vmem, hbm, vmem, vmem],
        out_specs=vmem,
        scratch_shapes=[
            pltpu.VMEM(weights_shape, jnp.bfloat16),
            pltpu.VMEM((2, rows, 128), jnp.float32),
            pltpu.VMEM((2, 2, 2, rows, 128), jnp.bfloat16),
            pltpu.SemaphoreType.DMA,
        ],
        compiler_params=pltpu.CompilerParams(vmem_limit_bytes=24 << 20),
        name="layers",
    )(came, near, far, phases, sizes)

    if plan.orders[-1] != plan.wanted:
        bits = len(plan.wanted)
        shaped = result.reshape((2,) * bits + (2, 128))
        axes = [bits - 1 - plan.orders[-1].index(plan.wanted[bits - 1 - axis]) for axis in range(bits)]
        result = shaped.transpose(axes + [bits, bits + 1]).reshape(2 * rows, 128)
    if plan.extra:
        size = 1 << plan.extra
        groups = [list(range(first, first + size)) for first in range(0, devices, size)]
        result = lax.all_to_all(
            result.reshape(size, -1, 128), "hi", split_axis=0, concat_axis=0,
            axis_index_groups=groups, tiled=True,
        )
    return result.reshape(rows, 2, 128).transpose(1, 0, 2).reshape(2, amp_count)


def solution(mesh):
    placed = (
        P(None, ("paths", "hi")),
        P(),
        P("paths", None, None),
        P("paths", None),
        P("paths", None),
        P("paths"),
        P("paths"),
    )
    return jax.shard_map(
        shards, mesh=mesh, in_specs=placed, out_specs=P(None, ("paths", "hi")), check_vma=False
    )
```

```python
import functools

import jax
import jax.numpy as jnp
import numpy as np
from jax import lax
from jax.experimental import pallas as pl
from jax.experimental.layout import Layout, with_layout_constraint
from jax.experimental.pallas import tpu as pltpu
from jax.sharding import PartitionSpec as P

LANE_BITS = 7
GATE_BITS = 6
STEPS = 32767.0


def fitted(function, degree):
    nodes = np.cos(np.pi * (np.arange(64) + 0.5) / 64) * 0.125 + 0.125
    series = np.polynomial.chebyshev.Chebyshev.fit(nodes, function(np.sqrt(nodes)), degree, domain=[0, 0.25])
    return [float(c) for c in series.convert(kind=np.polynomial.Polynomial).coef]


COS_TERMS = fitted(lambda v: np.cos(2 * np.pi * v), 7)
SIN_TERMS = fitted(lambda v: np.sin(2 * np.pi * v) / v, 6)


def horner(terms, w):
    total = jnp.full_like(w, terms[-1])
    for term in terms[-2::-1]:
        total = total * w + term
    return total


def turn(angle):
    part = angle - jnp.round(angle)
    square = part * part
    return horner(COS_TERMS, square), part * horner(SIN_TERMS, square)


class Plan:
    def __init__(self, global_count, local_bits, layers):
        self.global_count, self.local_bits, self.layers = global_count, local_bits, layers
        self.top = top = local_bits - global_count
        place = {}
        for label in range(local_bits + global_count):
            if label < top:
                place[label] = label
            elif label < local_bits:
                place[label] = label + global_count
            else:
                place[label] = label - global_count
        held = list(range(local_bits + global_count))
        self.targets = []
        for layer in range(layers):
            if layer < global_count:
                low, high = 7 + layer, local_bits + layer
                held[low], held[high] = held[high], held[low]
                target = low
            else:
                if layer == global_count:
                    held = held[:top] + held[local_bits:] + held[top:local_bits]
                target = local_bits - 2 * global_count + layer
            self.targets.append(place[held[target]])
        assert all(LANE_BITS <= bit < local_bits for bit in self.targets)
        ends = [place[label] for label in held]
        self.extra = sum(ends[local_bits + k] != local_bits + k for k in range(global_count))
        swapped = ends[:]
        for k in range(self.extra):
            low, high = local_bits - self.extra + k, local_bits + k
            assert ends[low] == high
            swapped[low], swapped[high] = ends[high], ends[low]
        assert swapped[local_bits:] == list(range(local_bits, local_bits + global_count))
        assert swapped[:LANE_BITS] == list(range(LANE_BITS))
        self.wanted = swapped[LANE_BITS:local_bits]
        self.orders, self.steps = [], []
        order = list(range(LANE_BITS, local_bits))
        for layer, target in enumerate(self.targets):
            step = 0
            if target in order[:4]:
                step = max(range(1, len(order) - 2), key=lambda at: self.lasts(order[at:at + 3], layer))
                triple = order[step:step + 3]
                if triple == self.wanted[:3] and not set(self.wanted[:4]) & set(self.targets[layer:]):
                    order = self.wanted
                else:
                    rest = sorted((bit for bit in order if bit not in triple), key=lambda bit: -self.lasts([bit], layer))
                    order = triple + rest
                assert target not in order[:4]
            self.steps.append(step)
            self.orders.append(order)

    def lasts(self, bits, layer):
        uses = self.targets[layer:]
        count = next((k for k, bit in enumerate(uses) if bit in bits), len(uses))
        return count + (count == len(uses) and bits == self.wanted[:3])

    def locate(self, qubit, layer):
        low, count = 7, min(layer + 1, self.global_count)
        size, high = self.global_count, self.local_bits
        if layer >= size:
            qubit = jnp.where(qubit >= high, qubit - size, jnp.where(qubit >= self.top, qubit + size, qubit))
        up = (qubit >= low) & (qubit < low + count)
        down = (qubit >= high) & (qubit < high + count)
        label = jnp.where(up, qubit + (high - low), jnp.where(down, qubit - (high - low), qubit))
        return jnp.where(label >= high, label - size, jnp.where(label >= self.top, label + size, label))


def widen(turned, block):
    lane = lax.broadcasted_iota(jnp.int32, (128, 128), 1)
    for to_bit in range(2):
        kept = jnp.where((lane >= 64) == (to_bit == 1), turned, 0.0)
        moved = pltpu.roll(kept, 64, 1)
        first, second = (kept, moved) if to_bit == 0 else (moved, kept)
        for from_bit in range(2):
            part = slice(64 * from_bit, 64 * from_bit + 64)
            both = jnp.concatenate([first[part], second[part]], axis=0)
            block[128 * from_bit:128 * from_bit + 128, 128 * to_bit:128 * to_bit + 128] = both.astype(jnp.bfloat16)


def tables_kernel(plan, rows, gates, pair_qubits, pair_angles, cut_qubits, cut_angle, path_index,
                  near, last, phases, sizes):
    device_part = lax.axis_index("hi") << plan.local_bits
    for layer in range(plan.layers):
        for kind in range(2):
            turned = gates[layer, kind].astype(jnp.float32).T
            if layer == plan.layers - 1:
                last[kind] = turned.astype(jnp.bfloat16)
            else:
                widen(turned, near.at[layer, kind])

    block_rows = 64
    block_bits = block_rows.bit_length() - 1
    row = lax.broadcasted_iota(jnp.int32, (block_rows, 128), 0)
    lane = lax.broadcasted_iota(jnp.int32, (block_rows, 128), 1)
    for layer in range(plan.layers):
        order = plan.orders[layer]
        base = lane + device_part
        for bit in range(block_bits):
            base = base + (((row >> bit) & 1) << order[bit])
        masks, turns = [], []
        one = jnp.int32(1)
        for pair in range(pair_qubits.shape[2]):
            first = plan.locate(pair_qubits[layer, 0, pair], layer)
            second = plan.locate(pair_qubits[layer, 1, pair], layer)
            masks.append((one << first) | (one << second))
            turns.append(pair_angles[layer, pair] * np.float32(0.5 / np.pi))
        if layer == 0:
            size = jnp.ones((8, 128), jnp.float32)
            cut_masks, cut_turns = [], []
            for cut in range(cut_qubits.shape[1]):
                first = plan.locate(cut_qubits[0, cut], layer)
                second = plan.locate(cut_qubits[1, cut], layer)
                cut_masks.append((one << first) | (one << second))
                chosen = path_index[cut] == 0
                cosine, sine = turn(jnp.full((8, 128), cut_angle[cut] * np.float32(0.5 / np.pi)))
                size = size * jnp.where(chosen, cosine, sine)
                cut_turns.append(jnp.where(chosen, 0.0, 0.25))
            sizes[...] = size

        @pl.loop(0, rows // block_rows)
        def _(block):
            offset = jnp.int32(0)
            for bit in range(block_bits, len(order)):
                offset = offset + (((block >> (bit - block_bits)) & 1) << order[bit])
            index = base + offset
            angle = jnp.zeros((block_rows, 128), jnp.float32)
            for mask, amount in zip(masks, turns):
                angle = angle + jnp.where((index & mask) == mask, amount, 0.0)
            if layer == 0:
                for mask, amount in zip(cut_masks, cut_turns):
                    both = index & mask
                    angle = angle + jnp.where((both == 0) | (both == mask), -amount, amount)
            cosine, sine = turn(angle)
            at = pl.ds(pl.multiple_of(block * block_rows, block_rows), block_rows)
            cosine = jnp.round(cosine * STEPS).astype(jnp.int32)
            sine = jnp.round(sine * STEPS).astype(jnp.int32)
            phases[layer, at, :] = (cosine << 16) | (sine & 0xFFFF)


def offset_of(number, bits, order):
    return sum(((number >> k) & 1) << order.index(bit) for k, bit in enumerate(bits))


def split(values):
    large = values.astype(jnp.bfloat16)
    return large, (values - large.astype(jnp.float32)).astype(jnp.bfloat16)


def layers_kernel(plan, rows, state, near, last, phases, sizes, out, last_here, held, parts):
    layers = plan.layers
    for kind in range(2):
        widen(last[kind].astype(jnp.float32), last_here.at[kind])

    old_order = list(range(LANE_BITS, plan.local_bits))
    for layer in range(layers):
        order, step, target = plan.orders[layer], plan.steps[layer], plan.targets[layer]
        rest = [bit for bit in order if bit != target]
        pieces = []
        for part in range(3):
            if layer == 0 or step:
                if part == 2:
                    pieces.append([-value for value in pieces[1]])
                    continue
                sides = []
                for side in range(2):
                    tiles = []
                    for tile in range(rows // 16):
                        at = offset_of(tile, rest[3:], old_order) + (side << old_order.index(target))
                        if layer == 0:
                            tiles.append(state[pl.ds(2 * at + part, 8, 2 << step), :])
                        else:
                            tiles.append(held[part, pl.ds(at, 8, 1 << step), :])
                    sides.append(jnp.concatenate(tiles, axis=0))
                pieces.append(split(jnp.concatenate(sides, axis=1)))
            else:
                starts = [[offset_of(tile, rest[4:], order) + (side << order.index(target))
                           for tile in range(rows // 32)] for side in range(2)]
                pieces.append([
                    jnp.concatenate([
                        jnp.concatenate([parts[layer % 2, size, part, at:at + 16, :] for at in side], axis=0)
                        for side in starts
                    ], axis=1)
                    for size in range(2)
                ])
        weights = last_here if layer == layers - 1 else near.at[layer]
        real, imag = weights[0], weights[1]
        results = []
        for second, (upper, lower) in ((2, (real, imag)), (1, (imag, real))):
            joined = jnp.concatenate([pieces[part][size] for size in range(2) for part in (0, second)], axis=1)
            weight = jnp.concatenate([upper, lower, upper, lower], axis=0)
            results.append(jnp.dot(joined, weight, preferred_element_type=jnp.float32))
        unit = jnp.full((16, 128), 1 / STEPS, jnp.float32)
        if layer == 0:
            unit = unit * sizes[0:1, :]
        for side in range(2):
            for tile in range(rows // 32):
                at = offset_of(tile, rest[4:], order) + (side << order.index(target))
                real = results[0][16 * tile:16 * tile + 16, 128 * side:128 * side + 128]
                imag = results[1][16 * tile:16 * tile + 16, 128 * side:128 * side + 128]
                word = phases[layer, at:at + 16, :]
                cosine = (word >> 16).astype(jnp.float32) * unit
                sine = ((word << 16) >> 16).astype(jnp.float32) * unit
                for part, value in enumerate((cosine * real - sine * imag, sine * real + cosine * imag)):
                    if layer == layers - 1:
                        out[pl.ds(2 * at + part, 16, 2), :] = value
                    elif plan.steps[layer + 1]:
                        held[part, at:at + 16, :] = value
                    else:
                        large, small = split(value)
                        parts[(layer + 1) % 2, 0, part, at:at + 16, :] = large
                        parts[(layer + 1) % 2, 1, part, at:at + 16, :] = small
                        if part == 1:
                            parts[(layer + 1) % 2, 0, 2, at:at + 16, :] = -large
                            parts[(layer + 1) % 2, 1, 2, at:at + 16, :] = -small
        old_order = order


def shards(
    amplitudes, gate_matrices, phase_qubits, phase_angles, cut_qubits, cut_angle, path_index
):
    devices = lax.axis_size("hi")
    global_count = devices.bit_length() - 1
    amp_count = amplitudes.shape[1]
    rows = amp_count >> LANE_BITS
    layers = gate_matrices.shape[0]
    plan = Plan(global_count, amp_count.bit_length() - 1, layers)

    shaped = with_layout_constraint(amplitudes.reshape(2, rows, 128), Layout(major_to_minor=(1, 0, 2)))
    sent = shaped.transpose(1, 0, 2).reshape(devices, -1, 128)
    came = lax.all_to_all(sent, "hi", split_axis=0, concat_axis=0, tiled=True).reshape(2 * rows, 128)

    vmem, smem = pl.BlockSpec(memory_space=pltpu.VMEM), pl.BlockSpec(memory_space=pltpu.SMEM)
    weights_shape = (2, 256, 256)
    near, last, phases, sizes = pl.pallas_call(
        functools.partial(tables_kernel, plan, rows),
        out_shape=(
            jax.ShapeDtypeStruct((layers - 1,) + weights_shape, jnp.bfloat16),
            jax.ShapeDtypeStruct((2, 128, 128), jnp.bfloat16),
            jax.ShapeDtypeStruct((layers, rows, 128), jnp.int32),
            jax.ShapeDtypeStruct((8, 128), jnp.float32),
        ),
        in_specs=[vmem] + [smem] * 5,
        out_specs=[vmem] * 4,
        cost_estimate=pl.CostEstimate(flops=100 * layers * amp_count, bytes_accessed=4 * layers * amp_count, transcendentals=0),
        compiler_params=pltpu.CompilerParams(vmem_limit_bytes=24 << 20),
        name="tables",
    )(gate_matrices, phase_qubits.transpose(0, 2, 1), phase_angles, cut_qubits.T, cut_angle, path_index)

    result = pl.pallas_call(
        functools.partial(layers_kernel, plan, rows),
        out_shape=jax.ShapeDtypeStruct((2 * rows, 128), jnp.float32),
        in_specs=[vmem] * 5,
        out_specs=vmem,
        scratch_shapes=[
            pltpu.VMEM(weights_shape, jnp.bfloat16),
            pltpu.VMEM((2, rows, 128), jnp.float32),
            pltpu.VMEM((2, 2, 3, rows, 128), jnp.bfloat16),
        ],
        compiler_params=pltpu.CompilerParams(vmem_limit_bytes=24 << 20),
        name="layers",
    )(came, near, last, phases, sizes)

    if plan.orders[-1] != plan.wanted:
        bits = len(plan.wanted)
        shaped = result.reshape((2,) * bits + (2, 128))
        axes = [bits - 1 - plan.orders[-1].index(plan.wanted[bits - 1 - axis]) for axis in range(bits)]
        result = shaped.transpose(axes + [bits, bits + 1]).reshape(2 * rows, 128)
    if plan.extra:
        size = 1 << plan.extra
        groups = [list(range(first, first + size)) for first in range(0, devices, size)]
        result = lax.all_to_all(
            result.reshape(size, -1, 128), "hi", split_axis=0, concat_axis=0,
            axis_index_groups=groups, tiled=True,
        )
    return result.reshape(rows, 2, 128).transpose(1, 0, 2).reshape(2, amp_count)


def solution(mesh):
    placed = (
        P(None, ("paths", "hi")),
        P(),
        P("paths", None, None),
        P("paths", None),
        P("paths", None),
        P("paths"),
        P("paths"),
    )
    return jax.shard_map(
        shards, mesh=mesh, in_specs=placed, out_specs=P(None, ("paths", "hi")), check_vma=False
    )
```

```python
import functools

import jax
import jax.numpy as jnp
import numpy as np
from jax import lax
from jax.experimental import pallas as pl
from jax.experimental.layout import Layout, with_layout_constraint
from jax.experimental.pallas import tpu as pltpu
from jax.sharding import PartitionSpec as P

LANE_BITS = 7
GATE_BITS = 6
STEPS = 32767.0


def fitted(function, degree):
    nodes = np.cos(np.pi * (np.arange(64) + 0.5) / 64) * 0.125 + 0.125
    series = np.polynomial.chebyshev.Chebyshev.fit(nodes, function(np.sqrt(nodes)), degree, domain=[0, 0.25])
    return [float(c) for c in series.convert(kind=np.polynomial.Polynomial).coef]


COS_TERMS = fitted(lambda v: np.cos(2 * np.pi * v), 7)
SIN_TERMS = fitted(lambda v: np.sin(2 * np.pi * v) / v, 6)


def horner(terms, w):
    total = jnp.full_like(w, terms[-1])
    for term in terms[-2::-1]:
        total = total * w + term
    return total


def turn(angle):
    part = angle - jnp.round(angle)
    square = part * part
    return horner(COS_TERMS, square), part * horner(SIN_TERMS, square)


class Plan:
    def __init__(self, global_count, local_bits, layers):
        self.global_count, self.local_bits, self.layers = global_count, local_bits, layers
        self.top = top = local_bits - global_count
        place = {}
        for label in range(local_bits + global_count):
            if label < top:
                place[label] = label
            elif label < local_bits:
                place[label] = label + global_count
            else:
                place[label] = label - global_count
        held = list(range(local_bits + global_count))
        self.targets = []
        for layer in range(layers):
            if layer < global_count:
                low, high = 7 + layer, local_bits + layer
                held[low], held[high] = held[high], held[low]
                target = low
            else:
                if layer == global_count:
                    held = held[:top] + held[local_bits:] + held[top:local_bits]
                target = local_bits - 2 * global_count + layer
            self.targets.append(place[held[target]])
        assert all(LANE_BITS <= bit < local_bits for bit in self.targets)
        ends = [place[label] for label in held]
        self.extra = sum(ends[local_bits + k] != local_bits + k for k in range(global_count))
        swapped = ends[:]
        for k in range(self.extra):
            low, high = local_bits - self.extra + k, local_bits + k
            assert ends[low] == high
            swapped[low], swapped[high] = ends[high], ends[low]
        assert swapped[local_bits:] == list(range(local_bits, local_bits + global_count))
        assert swapped[:LANE_BITS] == list(range(LANE_BITS))
        self.wanted = swapped[LANE_BITS:local_bits]
        self.orders, self.steps = [], []
        order = list(range(LANE_BITS, local_bits))
        for layer, target in enumerate(self.targets):
            step = 0
            if target in order[:4]:
                step = max(range(1, len(order) - 2), key=lambda at: self.lasts(order[at:at + 3], layer))
                triple = order[step:step + 3]
                if triple == self.wanted[:3] and not set(self.wanted[:4]) & set(self.targets[layer:]):
                    order = self.wanted
                else:
                    rest = sorted((bit for bit in order if bit not in triple), key=lambda bit: -self.lasts([bit], layer))
                    order = triple + rest
                assert target not in order[:4]
            self.steps.append(step)
            self.orders.append(order)

        self.halves = [bit for bit in order if bit not in self.targets
                       and all(other.index(bit) >= 4 for other in self.orders)][:1]

    def lasts(self, bits, layer):
        uses = self.targets[layer:]
        count = next((k for k, bit in enumerate(uses) if bit in bits), len(uses))
        return count + (count == len(uses) and bits == self.wanted[:3])

    def locate(self, qubit, layer):
        low, count = 7, min(layer + 1, self.global_count)
        size, high = self.global_count, self.local_bits
        if layer >= size:
            qubit = jnp.where(qubit >= high, qubit - size, jnp.where(qubit >= self.top, qubit + size, qubit))
        up = (qubit >= low) & (qubit < low + count)
        down = (qubit >= high) & (qubit < high + count)
        label = jnp.where(up, qubit + (high - low), jnp.where(down, qubit - (high - low), qubit))
        return jnp.where(label >= high, label - size, jnp.where(label >= self.top, label + size, label))


def widen(turned, block):
    lane = lax.broadcasted_iota(jnp.int32, (128, 128), 1)
    for to_bit in range(2):
        kept = jnp.where((lane >= 64) == (to_bit == 1), turned, 0.0)
        moved = pltpu.roll(kept, 64, 1)
        first, second = (kept, moved) if to_bit == 0 else (moved, kept)
        for from_bit in range(2):
            part = slice(64 * from_bit, 64 * from_bit + 64)
            both = jnp.concatenate([first[part], second[part]], axis=0)
            block[128 * from_bit:128 * from_bit + 128, 128 * to_bit:128 * to_bit + 128] = both.astype(jnp.bfloat16)


def tables_kernel(plan, rows, gates, pair_qubits, pair_angles, cut_qubits, cut_angle, path_index,
                  near, last, phases, sizes):
    device_part = lax.axis_index("hi") << plan.local_bits
    for layer in range(plan.layers):
        for kind in range(2):
            turned = gates[layer, kind].astype(jnp.float32).T
            if layer == plan.layers - 1:
                last[kind] = turned.astype(jnp.bfloat16)
            else:
                widen(turned, near.at[layer, kind])

    block_rows = 64
    block_bits = block_rows.bit_length() - 1
    row = lax.broadcasted_iota(jnp.int32, (block_rows, 128), 0)
    lane = lax.broadcasted_iota(jnp.int32, (block_rows, 128), 1)
    for layer in range(plan.layers):
        order = plan.orders[layer]
        base = lane + device_part
        for bit in range(block_bits):
            base = base + (((row >> bit) & 1) << order[bit])
        masks, turns = [], []
        one = jnp.int32(1)
        for pair in range(pair_qubits.shape[2]):
            first = plan.locate(pair_qubits[layer, 0, pair], layer)
            second = plan.locate(pair_qubits[layer, 1, pair], layer)
            masks.append((one << first) | (one << second))
            turns.append(pair_angles[layer, pair] * np.float32(0.5 / np.pi))
        if layer == 0:
            size = jnp.ones((8, 128), jnp.float32)
            cut_masks, cut_turns = [], []
            for cut in range(cut_qubits.shape[1]):
                first = plan.locate(cut_qubits[0, cut], layer)
                second = plan.locate(cut_qubits[1, cut], layer)
                cut_masks.append((one << first) | (one << second))
                chosen = path_index[cut] == 0
                cosine, sine = turn(jnp.full((8, 128), cut_angle[cut] * np.float32(0.5 / np.pi)))
                size = size * jnp.where(chosen, cosine, sine)
                cut_turns.append(jnp.where(chosen, 0.0, 0.25))
            sizes[...] = size

        @pl.loop(0, rows // block_rows)
        def _(block):
            offset = jnp.int32(0)
            for bit in range(block_bits, len(order)):
                offset = offset + (((block >> (bit - block_bits)) & 1) << order[bit])
            index = base + offset
            angle = jnp.zeros((block_rows, 128), jnp.float32)
            for mask, amount in zip(masks, turns):
                angle = angle + jnp.where((index & mask) == mask, amount, 0.0)
            if layer == 0:
                for mask, amount in zip(cut_masks, cut_turns):
                    both = index & mask
                    angle = angle + jnp.where((both == 0) | (both == mask), -amount, amount)
            cosine, sine = turn(angle)
            at = pl.ds(pl.multiple_of(block * block_rows, block_rows), block_rows)
            cosine = jnp.round(cosine * STEPS).astype(jnp.int32)
            sine = jnp.round(sine * STEPS).astype(jnp.int32)
            phases[layer, at, :] = (cosine << 16) | (sine & 0xFFFF)


def offset_of(number, bits, order):
    return sum(((number >> k) & 1) << order.index(bit) for k, bit in enumerate(bits))


def split(values):
    large = values.astype(jnp.bfloat16)
    return large, (values - large.astype(jnp.float32)).astype(jnp.bfloat16)


def layers_kernel(plan, rows, state, near, last, phases, sizes, out, last_here, held, parts):
    layers = plan.layers
    for kind in range(2):
        widen(last[kind].astype(jnp.float32), last_here.at[kind])

    def starts(layer, side, half, order, height):
        fixed = [plan.targets[layer]] + plan.halves
        rest = [bit for bit in plan.orders[layer] if bit not in fixed][height:]
        base = side << order.index(plan.targets[layer])
        if plan.halves:
            base += half << order.index(plan.halves[0])
        return [base + offset_of(number, rest, order) for number in range(1 << len(rest))]

    def products(layer, half):
        order, step = plan.orders[layer], plan.steps[layer]
        pieces = []
        for part in range(3):
            if layer == 0 or step:
                if part == 2:
                    pieces.append([-value for value in pieces[1]])
                    continue
                old_order = plan.orders[layer - 1] if layer else list(range(LANE_BITS, plan.local_bits))
                sides = []
                for side in range(2):
                    if layer == 0:
                        tiles = [state[pl.ds(2 * at + part, 8, 2 << step), :]
                                 for at in starts(layer, side, half, old_order, 3)]
                    else:
                        tiles = [held[part, pl.ds(at, 8, 1 << step), :]
                                 for at in starts(layer, side, half, old_order, 3)]
                    sides.append(jnp.concatenate(tiles, axis=0))
                pieces.append(split(jnp.concatenate(sides, axis=1)))
            else:
                pieces.append([
                    jnp.concatenate([
                        jnp.concatenate([parts[layer % 2, size, part, at:at + 16, :]
                                         for at in starts(layer, side, half, order, 4)], axis=0)
                        for side in range(2)
                    ], axis=1)
                    for size in range(2)
                ])
        weights = last_here if layer == layers - 1 else near.at[layer]
        real, imag = weights[0], weights[1]
        results = []
        for second, (upper, lower) in ((2, (real, imag)), (1, (imag, real))):
            joined = jnp.concatenate(
                [jnp.concatenate([pieces[0][size], pieces[second][size]], axis=1) for size in range(2)], axis=0
            )
            both = jnp.dot(joined, jnp.concatenate([upper, lower], axis=0), preferred_element_type=jnp.float32)
            results.append(both[:both.shape[0] // 2] + both[both.shape[0] // 2:])
        return results

    def turned(layer, half, results):
        order = plan.orders[layer]
        unit = jnp.full((16, 128), 1 / STEPS, jnp.float32)
        if layer == 0:
            unit = unit * sizes[0:1, :]
        for side in range(2):
            for tile, at in enumerate(starts(layer, side, half, order, 4)):
                real, imag = [result[16 * tile:16 * tile + 16, 128 * side:128 * side + 128] for result in results]
                word = phases[layer, at:at + 16, :]
                cosine = (word >> 16).astype(jnp.float32) * unit
                sine = ((word << 16) >> 16).astype(jnp.float32) * unit
                for part, value in enumerate((cosine * real - sine * imag, sine * real + cosine * imag)):
                    if layer == layers - 1:
                        out[pl.ds(2 * at + part, 16, 2), :] = value
                    elif plan.steps[layer + 1]:
                        held[part, at:at + 16, :] = value
                    else:
                        large, small = split(value)
                        parts[(layer + 1) % 2, 0, part, at:at + 16, :] = large
                        parts[(layer + 1) % 2, 1, part, at:at + 16, :] = small
                        if part == 1:
                            parts[(layer + 1) % 2, 0, 2, at:at + 16, :] = -large
                            parts[(layer + 1) % 2, 1, 2, at:at + 16, :] = -small

    waiting = None
    for layer in range(layers):
        for half in range(1 << len(plan.halves)):
            results = products(layer, half)
            if plan.halves and waiting:
                turned(*waiting)
                waiting = None
            if plan.halves:
                waiting = (layer, half, results)
            else:
                turned(layer, half, results)
    if waiting:
        turned(*waiting)


def shards(
    amplitudes, gate_matrices, phase_qubits, phase_angles, cut_qubits, cut_angle, path_index
):
    devices = lax.axis_size("hi")
    global_count = devices.bit_length() - 1
    amp_count = amplitudes.shape[1]
    rows = amp_count >> LANE_BITS
    layers = gate_matrices.shape[0]
    plan = Plan(global_count, amp_count.bit_length() - 1, layers)

    shaped = with_layout_constraint(amplitudes.reshape(2, rows, 128), Layout(major_to_minor=(1, 0, 2)))
    sent = shaped.transpose(1, 0, 2).reshape(devices, -1, 128)
    came = lax.all_to_all(sent, "hi", split_axis=0, concat_axis=0, tiled=True).reshape(2 * rows, 128)

    vmem, smem = pl.BlockSpec(memory_space=pltpu.VMEM), pl.BlockSpec(memory_space=pltpu.SMEM)
    weights_shape = (2, 256, 256)
    near, last, phases, sizes = pl.pallas_call(
        functools.partial(tables_kernel, plan, rows),
        out_shape=(
            jax.ShapeDtypeStruct((layers - 1,) + weights_shape, jnp.bfloat16),
            jax.ShapeDtypeStruct((2, 128, 128), jnp.bfloat16),
            jax.ShapeDtypeStruct((layers, rows, 128), jnp.int32),
            jax.ShapeDtypeStruct((8, 128), jnp.float32),
        ),
        in_specs=[vmem] + [smem] * 5,
        out_specs=[vmem] * 4,
        cost_estimate=pl.CostEstimate(flops=100 * layers * amp_count, bytes_accessed=4 * layers * amp_count, transcendentals=0),
        compiler_params=pltpu.CompilerParams(vmem_limit_bytes=24 << 20),
        name="tables",
    )(gate_matrices, phase_qubits.transpose(0, 2, 1), phase_angles, cut_qubits.T, cut_angle, path_index)

    result = pl.pallas_call(
        functools.partial(layers_kernel, plan, rows),
        out_shape=jax.ShapeDtypeStruct((2 * rows, 128), jnp.float32),
        in_specs=[vmem] * 5,
        out_specs=vmem,
        scratch_shapes=[
            pltpu.VMEM(weights_shape, jnp.bfloat16),
            pltpu.VMEM((2, rows, 128), jnp.float32),
            pltpu.VMEM((2, 2, 3, rows, 128), jnp.bfloat16),
        ],
        compiler_params=pltpu.CompilerParams(vmem_limit_bytes=24 << 20),
        name="layers",
    )(came, near, last, phases, sizes)

    if plan.orders[-1] != plan.wanted:
        bits = len(plan.wanted)
        shaped = result.reshape((2,) * bits + (2, 128))
        axes = [bits - 1 - plan.orders[-1].index(plan.wanted[bits - 1 - axis]) for axis in range(bits)]
        result = shaped.transpose(axes + [bits, bits + 1]).reshape(2 * rows, 128)
    if plan.extra:
        size = 1 << plan.extra
        groups = [list(range(first, first + size)) for first in range(0, devices, size)]
        result = lax.all_to_all(
            result.reshape(size, -1, 128), "hi", split_axis=0, concat_axis=0,
            axis_index_groups=groups, tiled=True,
        )
    return result.reshape(rows, 2, 128).transpose(1, 0, 2).reshape(2, amp_count)


def solution(mesh):
    placed = (
        P(None, ("paths", "hi")),
        P(),
        P("paths", None, None),
        P("paths", None),
        P("paths", None),
        P("paths"),
        P("paths"),
    )
    return jax.shard_map(
        shards, mesh=mesh, in_specs=placed, out_specs=P(None, ("paths", "hi")), check_vma=False
    )
```

```python
import functools

import jax
import jax.numpy as jnp
import numpy as np
from jax import lax
from jax.experimental import pallas as pl
from jax.experimental.layout import Layout, with_layout_constraint
from jax.experimental.pallas import tpu as pltpu
from jax.sharding import PartitionSpec as P

LANE_BITS = 7
GATE_BITS = 6
STEPS = 32767.0


def fitted(function, degree):
    nodes = np.cos(np.pi * (np.arange(64) + 0.5) / 64) * 0.125 + 0.125
    series = np.polynomial.chebyshev.Chebyshev.fit(nodes, function(np.sqrt(nodes)), degree, domain=[0, 0.25])
    return [float(c) for c in series.convert(kind=np.polynomial.Polynomial).coef]


COS_TERMS = fitted(lambda v: np.cos(2 * np.pi * v), 7)
SIN_TERMS = fitted(lambda v: np.sin(2 * np.pi * v) / v, 6)


def horner(terms, w):
    total = jnp.full_like(w, terms[-1])
    for term in terms[-2::-1]:
        total = total * w + term
    return total


def turn(angle):
    part = angle - jnp.round(angle)
    square = part * part
    return horner(COS_TERMS, square), part * horner(SIN_TERMS, square)


class Plan:
    def __init__(self, global_count, local_bits, layers):
        self.global_count, self.local_bits, self.layers = global_count, local_bits, layers
        self.top = top = local_bits - global_count
        place = {}
        for label in range(local_bits + global_count):
            if label < top:
                place[label] = label
            elif label < local_bits:
                place[label] = label + global_count
            else:
                place[label] = label - global_count
        held = list(range(local_bits + global_count))
        self.targets = []
        for layer in range(layers):
            if layer < global_count:
                low, high = 7 + layer, local_bits + layer
                held[low], held[high] = held[high], held[low]
                target = low
            else:
                if layer == global_count:
                    held = held[:top] + held[local_bits:] + held[top:local_bits]
                target = local_bits - 2 * global_count + layer
            self.targets.append(place[held[target]])
        assert all(LANE_BITS <= bit < local_bits for bit in self.targets)
        ends = [place[label] for label in held]
        self.extra = sum(ends[local_bits + k] != local_bits + k for k in range(global_count))
        swapped = ends[:]
        for k in range(self.extra):
            low, high = local_bits - self.extra + k, local_bits + k
            assert ends[low] == high
            swapped[low], swapped[high] = ends[high], ends[low]
        assert swapped[local_bits:] == list(range(local_bits, local_bits + global_count))
        assert swapped[:LANE_BITS] == list(range(LANE_BITS))
        self.wanted = swapped[LANE_BITS:local_bits]
        self.orders, self.steps = [], []
        order = list(range(LANE_BITS, local_bits))
        for layer, target in enumerate(self.targets):
            step = 0
            if target in order[:4]:
                step = max(range(1, len(order) - 2), key=lambda at: self.lasts(order[at:at + 3], layer))
                triple = order[step:step + 3]
                if triple == self.wanted[:3] and not set(self.wanted[:4]) & set(self.targets[layer:]):
                    order = self.wanted
                else:
                    rest = sorted((bit for bit in order if bit not in triple), key=lambda bit: -self.lasts([bit], layer))
                    order = triple + rest
                assert target not in order[:4]
            self.steps.append(step)
            self.orders.append(order)

        self.halves = [bit for bit in order if bit not in self.targets
                       and all(other.index(bit) >= 4 for other in self.orders)][:1]

        self.axes, shape = [], []
        for bit in order[:3:-1]:
            apart = bit in [self.targets[-1]] + self.halves
            if not apart and self.axes and self.axes[-1] is None:
                shape[-1] *= 2
            else:
                self.axes.append(bit if apart else None)
                shape.append(2)
        self.shape = tuple(shape)

    def lasts(self, bits, layer):
        uses = self.targets[layer:]
        count = next((k for k, bit in enumerate(uses) if bit in bits), len(uses))
        return count + (count == len(uses) and bits == self.wanted[:3])

    def locate(self, qubit, layer):
        low, count = 7, min(layer + 1, self.global_count)
        size, high = self.global_count, self.local_bits
        if layer >= size:
            qubit = jnp.where(qubit >= high, qubit - size, jnp.where(qubit >= self.top, qubit + size, qubit))
        up = (qubit >= low) & (qubit < low + count)
        down = (qubit >= high) & (qubit < high + count)
        label = jnp.where(up, qubit + (high - low), jnp.where(down, qubit - (high - low), qubit))
        return jnp.where(label >= high, label - size, jnp.where(label >= self.top, label + size, label))


def widen(turned, block):
    lane = lax.broadcasted_iota(jnp.int32, (128, 128), 1)
    for to_bit in range(2):
        kept = jnp.where((lane >= 64) == (to_bit == 1), turned, 0.0)
        moved = pltpu.roll(kept, 64, 1)
        first, second = (kept, moved) if to_bit == 0 else (moved, kept)
        for from_bit in range(2):
            part = slice(64 * from_bit, 64 * from_bit + 64)
            both = jnp.concatenate([first[part], second[part]], axis=0)
            block[128 * from_bit:128 * from_bit + 128, 128 * to_bit:128 * to_bit + 128] = both.astype(jnp.bfloat16)


def tables_kernel(plan, rows, gates, pair_qubits, pair_angles, cut_qubits, cut_angle, path_index,
                  near, last, phases, sizes):
    device_part = lax.axis_index("hi") << plan.local_bits
    for layer in range(plan.layers):
        for kind in range(2):
            turned = gates[layer, kind].astype(jnp.float32).T
            if layer == plan.layers - 1:
                last[kind] = turned.astype(jnp.bfloat16)
            else:
                widen(turned, near.at[layer, kind])

    block_rows = 64
    block_bits = block_rows.bit_length() - 1
    row = lax.broadcasted_iota(jnp.int32, (block_rows, 128), 0)
    lane = lax.broadcasted_iota(jnp.int32, (block_rows, 128), 1)
    for layer in range(plan.layers):
        order = plan.orders[layer]
        base = lane + device_part
        for bit in range(block_bits):
            base = base + (((row >> bit) & 1) << order[bit])
        masks, turns = [], []
        one = jnp.int32(1)
        for pair in range(pair_qubits.shape[2]):
            first = plan.locate(pair_qubits[layer, 0, pair], layer)
            second = plan.locate(pair_qubits[layer, 1, pair], layer)
            masks.append((one << first) | (one << second))
            turns.append(pair_angles[layer, pair] * np.float32(0.5 / np.pi))
        if layer == 0:
            size = jnp.ones((8, 128), jnp.float32)
            cut_masks, cut_turns = [], []
            for cut in range(cut_qubits.shape[1]):
                first = plan.locate(cut_qubits[0, cut], layer)
                second = plan.locate(cut_qubits[1, cut], layer)
                cut_masks.append((one << first) | (one << second))
                chosen = path_index[cut] == 0
                cosine, sine = turn(jnp.full((8, 128), cut_angle[cut] * np.float32(0.5 / np.pi)))
                size = size * jnp.where(chosen, cosine, sine)
                cut_turns.append(jnp.where(chosen, 0.0, 0.25))
            sizes[...] = size

        @pl.loop(0, rows // block_rows)
        def _(block):
            offset = jnp.int32(0)
            for bit in range(block_bits, len(order)):
                offset = offset + (((block >> (bit - block_bits)) & 1) << order[bit])
            index = base + offset
            angle = jnp.zeros((block_rows, 128), jnp.float32)
            for mask, amount in zip(masks, turns):
                angle = angle + jnp.where((index & mask) == mask, amount, 0.0)
            if layer == 0:
                for mask, amount in zip(cut_masks, cut_turns):
                    both = index & mask
                    angle = angle + jnp.where((both == 0) | (both == mask), -amount, amount)
            cosine, sine = turn(angle)
            at = pl.ds(pl.multiple_of(block * block_rows, block_rows), block_rows)
            cosine = jnp.round(cosine * STEPS).astype(jnp.int32)
            sine = jnp.round(sine * STEPS).astype(jnp.int32)
            phases[layer, at, :] = (cosine << 16) | (sine & 0xFFFF)


def offset_of(number, bits, order):
    return sum(((number >> k) & 1) << order.index(bit) for k, bit in enumerate(bits))


def split(values):
    large = values.astype(jnp.bfloat16)
    return large, (values - large.astype(jnp.float32)).astype(jnp.bfloat16)


def layers_kernel(plan, rows, state, near, last, phases, sizes, result, last_here, held, parts, out, done):
    layers = plan.layers
    copies = []

    def starts(layer, side, half, order, height):
        fixed = [plan.targets[layer]] + plan.halves
        rest = [bit for bit in plan.orders[layer] if bit not in fixed][height:]
        base = side << order.index(plan.targets[layer])
        if plan.halves:
            base += half << order.index(plan.halves[0])
        return [base + offset_of(number, rest, order) for number in range(1 << len(rest))]

    def products(layer, half):
        order, step = plan.orders[layer], plan.steps[layer]
        pieces = []
        for part in range(3):
            if layer == 0 or step:
                if part == 2:
                    pieces.append([-value for value in pieces[1]])
                    continue
                old_order = plan.orders[layer - 1] if layer else list(range(LANE_BITS, plan.local_bits))
                sides = []
                for side in range(2):
                    if layer == 0:
                        tiles = [state[pl.ds(2 * at + part, 8, 2 << step), :]
                                 for at in starts(layer, side, half, old_order, 3)]
                    else:
                        tiles = [held[part, pl.ds(at, 8, 1 << step), :]
                                 for at in starts(layer, side, half, old_order, 3)]
                    sides.append(jnp.concatenate(tiles, axis=0))
                pieces.append(split(jnp.concatenate(sides, axis=1)))
            else:
                pieces.append([
                    jnp.concatenate([
                        jnp.concatenate([parts[layer % 2, size, part, at:at + 16, :]
                                         for at in starts(layer, side, half, order, 4)], axis=0)
                        for side in range(2)
                    ], axis=1)
                    for size in range(2)
                ])
        weights = last_here if layer == layers - 1 else near.at[layer]
        real, imag = weights[0], weights[1]
        results = []
        for second, (upper, lower) in ((2, (real, imag)), (1, (imag, real))):
            joined = jnp.concatenate(
                [jnp.concatenate([pieces[0][size], pieces[second][size]], axis=1) for size in range(2)], axis=0
            )
            both = jnp.dot(joined, jnp.concatenate([upper, lower], axis=0), preferred_element_type=jnp.float32)
            results.append(both[:both.shape[0] // 2] + both[both.shape[0] // 2:])
        return results

    def turned(layer, half, results):
        order = plan.orders[layer]
        unit = jnp.full((16, 128), 1 / STEPS, jnp.float32)
        if layer == 0:
            unit = unit * sizes[0:1, :]
        for side in range(2):
            for tile, at in enumerate(starts(layer, side, half, order, 4)):
                real, imag = [result[16 * tile:16 * tile + 16, 128 * side:128 * side + 128] for result in results]
                word = phases[layer, at:at + 16, :]
                cosine = (word >> 16).astype(jnp.float32) * unit
                sine = ((word << 16) >> 16).astype(jnp.float32) * unit
                for part, value in enumerate((cosine * real - sine * imag, sine * real + cosine * imag)):
                    if layer == layers - 1:
                        block = tuple(int(k) for k in np.unravel_index(at // 16, plan.shape))
                        out[block + (pl.ds(part, 16, 2), slice(None))] = value
                    elif plan.steps[layer + 1]:
                        held[part, at:at + 16, :] = value
                    else:
                        large, small = split(value)
                        parts[(layer + 1) % 2, 0, part, at:at + 16, :] = large
                        parts[(layer + 1) % 2, 1, part, at:at + 16, :] = small
                        if part == 1:
                            parts[(layer + 1) % 2, 0, 2, at:at + 16, :] = -large
                            parts[(layer + 1) % 2, 1, 2, at:at + 16, :] = -small
            if layer == layers - 1:
                chosen = {plan.targets[layer]: side}
                if plan.halves:
                    chosen[plan.halves[0]] = half
                here = tuple(chosen.get(bit, slice(None)) for bit in plan.axes)
                copies.append(pltpu.make_async_copy(out.at[here], result.at[here], done.at[len(copies)]))
                copies[-1].start()

    waiting = None
    for layer in range(layers):
        for half in range(1 << len(plan.halves)):
            results = products(layer, half)
            if (layer, half) == (0, 0):
                for kind in range(2):
                    widen(last[kind].astype(jnp.float32), last_here.at[kind])
            if plan.halves and waiting:
                turned(*waiting)
                waiting = None
            if plan.halves:
                waiting = (layer, half, results)
            else:
                turned(layer, half, results)
    if waiting:
        turned(*waiting)
    for copy in copies:
        copy.wait()


def shards(
    amplitudes, gate_matrices, phase_qubits, phase_angles, cut_qubits, cut_angle, path_index
):
    devices = lax.axis_size("hi")
    global_count = devices.bit_length() - 1
    amp_count = amplitudes.shape[1]
    rows = amp_count >> LANE_BITS
    layers = gate_matrices.shape[0]
    plan = Plan(global_count, amp_count.bit_length() - 1, layers)

    shaped = with_layout_constraint(amplitudes.reshape(2, rows, 128), Layout(major_to_minor=(1, 0, 2)))
    sent = shaped.transpose(1, 0, 2).reshape(devices, -1, 128)
    came = lax.all_to_all(sent, "hi", split_axis=0, concat_axis=0, tiled=True).reshape(2 * rows, 128)

    vmem, smem = pl.BlockSpec(memory_space=pltpu.VMEM), pl.BlockSpec(memory_space=pltpu.SMEM)
    weights_shape = (2, 256, 256)
    near, last, phases, sizes = pl.pallas_call(
        functools.partial(tables_kernel, plan, rows),
        out_shape=(
            jax.ShapeDtypeStruct((layers - 1,) + weights_shape, jnp.bfloat16),
            jax.ShapeDtypeStruct((2, 128, 128), jnp.bfloat16),
            jax.ShapeDtypeStruct((layers, rows, 128), jnp.int32),
            jax.ShapeDtypeStruct((8, 128), jnp.float32),
        ),
        in_specs=[vmem] + [smem] * 5,
        out_specs=[vmem] * 4,
        cost_estimate=pl.CostEstimate(flops=100 * layers * amp_count, bytes_accessed=4 * layers * amp_count, transcendentals=0),
        compiler_params=pltpu.CompilerParams(vmem_limit_bytes=24 << 20),
        name="tables",
    )(gate_matrices, phase_qubits.transpose(0, 2, 1), phase_angles, cut_qubits.T, cut_angle, path_index)

    result = pl.pallas_call(
        functools.partial(layers_kernel, plan, rows),
        out_shape=jax.ShapeDtypeStruct(plan.shape + (32, 128), jnp.float32),
        in_specs=[vmem] * 5,
        out_specs=pl.BlockSpec(memory_space=pltpu.HBM),
        scratch_shapes=[
            pltpu.VMEM(weights_shape, jnp.bfloat16),
            pltpu.VMEM((2, rows, 128), jnp.float32),
            pltpu.VMEM((2, 2, 3, rows, 128), jnp.bfloat16),
            pltpu.VMEM(plan.shape + (32, 128), jnp.float32),
            pltpu.SemaphoreType.DMA((2 << len(plan.halves),)),
        ],
        compiler_params=pltpu.CompilerParams(vmem_limit_bytes=24 << 20),
        name="layers",
    )(came, near, last, phases, sizes).reshape(2 * rows, 128)

    if plan.orders[-1] != plan.wanted:
        bits = len(plan.wanted)
        shaped = result.reshape((2,) * bits + (2, 128))
        axes = [bits - 1 - plan.orders[-1].index(plan.wanted[bits - 1 - axis]) for axis in range(bits)]
        result = shaped.transpose(axes + [bits, bits + 1]).reshape(2 * rows, 128)
    if plan.extra:
        size = 1 << plan.extra
        groups = [list(range(first, first + size)) for first in range(0, devices, size)]
        result = lax.all_to_all(
            result.reshape(size, -1, 128), "hi", split_axis=0, concat_axis=0,
            axis_index_groups=groups, tiled=True,
        )
    return result.reshape(rows, 2, 128).transpose(1, 0, 2).reshape(2, amp_count)


def solution(mesh):
    placed = (
        P(None, ("paths", "hi")),
        P(),
        P("paths", None, None),
        P("paths", None),
        P("paths", None),
        P("paths"),
        P("paths"),
    )
    return jax.shard_map(
        shards, mesh=mesh, in_specs=placed, out_specs=P(None, ("paths", "hi")), check_vma=False
    )
```

```python
import functools

import jax
import jax.numpy as jnp
import numpy as np
from jax import lax
from jax.experimental import pallas as pl
from jax.experimental.layout import Layout, with_layout_constraint
from jax.experimental.pallas import tpu as pltpu
from jax.sharding import PartitionSpec as P

LANE_BITS = 7
GATE_BITS = 6
STEPS = 32767.0


def fitted(function, degree):
    nodes = np.cos(np.pi * (np.arange(64) + 0.5) / 64) * 0.125 + 0.125
    series = np.polynomial.chebyshev.Chebyshev.fit(nodes, function(np.sqrt(nodes)), degree, domain=[0, 0.25])
    return [float(c) for c in series.convert(kind=np.polynomial.Polynomial).coef]


COS_TERMS = fitted(lambda v: np.cos(2 * np.pi * v), 7)
SIN_TERMS = fitted(lambda v: np.sin(2 * np.pi * v) / v, 6)


def horner(terms, w):
    total = jnp.full_like(w, terms[-1])
    for term in terms[-2::-1]:
        total = total * w + term
    return total


def turn(angle):
    part = angle - jnp.round(angle)
    square = part * part
    return horner(COS_TERMS, square), part * horner(SIN_TERMS, square)


class Plan:
    def __init__(self, global_count, local_bits, layers):
        self.global_count, self.local_bits, self.layers = global_count, local_bits, layers
        self.top = top = local_bits - global_count
        place = {}
        for label in range(local_bits + global_count):
            if label < top:
                place[label] = label
            elif label < local_bits:
                place[label] = label + global_count
            else:
                place[label] = label - global_count
        held = list(range(local_bits + global_count))
        self.targets = []
        for layer in range(layers):
            if layer < global_count:
                low, high = 7 + layer, local_bits + layer
                held[low], held[high] = held[high], held[low]
                target = low
            else:
                if layer == global_count:
                    held = held[:top] + held[local_bits:] + held[top:local_bits]
                target = local_bits - 2 * global_count + layer
            self.targets.append(place[held[target]])
        assert all(LANE_BITS <= bit < local_bits for bit in self.targets)
        ends = [place[label] for label in held]
        self.extra = sum(ends[local_bits + k] != local_bits + k for k in range(global_count))
        swapped = ends[:]
        for k in range(self.extra):
            low, high = local_bits - self.extra + k, local_bits + k
            assert ends[low] == high
            swapped[low], swapped[high] = ends[high], ends[low]
        assert swapped[local_bits:] == list(range(local_bits, local_bits + global_count))
        assert swapped[:LANE_BITS] == list(range(LANE_BITS))
        self.wanted = swapped[LANE_BITS:local_bits]
        self.orders, self.steps = [], []
        order = list(range(LANE_BITS, local_bits))
        for layer, target in enumerate(self.targets):
            step = 0
            if target in order[:4]:
                step = max(range(1, len(order) - 2), key=lambda at: self.lasts(order[at:at + 3], layer))
                triple = order[step:step + 3]
                if triple == self.wanted[:3] and not set(self.wanted[:4]) & set(self.targets[layer:]):
                    order = self.wanted
                else:
                    rest = sorted((bit for bit in order if bit not in triple), key=lambda bit: -self.lasts([bit], layer))
                    order = triple + rest
                assert target not in order[:4]
            self.steps.append(step)
            self.orders.append(order)

        self.halves = [bit for bit in order if bit not in self.targets
                       and all(other.index(bit) >= 4 for other in self.orders)][:1]

        self.axes, shape = [], []
        for bit in order[:3:-1]:
            apart = bit in [self.targets[-1]] + self.halves
            if not apart and self.axes and self.axes[-1] is None:
                shape[-1] *= 2
            else:
                self.axes.append(bit if apart else None)
                shape.append(2)
        self.shape = tuple(shape)

    def lasts(self, bits, layer):
        uses = self.targets[layer:]
        count = next((k for k, bit in enumerate(uses) if bit in bits), len(uses))
        return count + (count == len(uses) and bits == self.wanted[:3])

    def locate(self, qubit, layer):
        low, count = 7, min(layer + 1, self.global_count)
        size, high = self.global_count, self.local_bits
        if layer >= size:
            qubit = jnp.where(qubit >= high, qubit - size, jnp.where(qubit >= self.top, qubit + size, qubit))
        up = (qubit >= low) & (qubit < low + count)
        down = (qubit >= high) & (qubit < high + count)
        label = jnp.where(up, qubit + (high - low), jnp.where(down, qubit - (high - low), qubit))
        return jnp.where(label >= high, label - size, jnp.where(label >= self.top, label + size, label))


def widen(turned, block):
    lane = lax.broadcasted_iota(jnp.int32, (128, 128), 1)
    for to_bit in range(2):
        kept = jnp.where((lane >= 64) == (to_bit == 1), turned, 0.0)
        moved = pltpu.roll(kept, 64, 1)
        first, second = (kept, moved) if to_bit == 0 else (moved, kept)
        for from_bit in range(2):
            part = slice(64 * from_bit, 64 * from_bit + 64)
            both = jnp.concatenate([first[part], second[part]], axis=0)
            block[128 * from_bit:128 * from_bit + 128, 128 * to_bit:128 * to_bit + 128] = both.astype(jnp.bfloat16)


def tables_kernel(plan, rows, gates, pair_qubits, pair_angles, cut_qubits, cut_angle, path_index,
                  near, last, phases, sizes):
    device_part = lax.axis_index("hi") << plan.local_bits
    for layer in range(plan.layers):
        for kind in range(2):
            turned = gates[layer, kind].astype(jnp.float32).T
            if layer == plan.layers - 1:
                last[kind] = turned.astype(jnp.bfloat16)
            else:
                widen(turned, near.at[layer, kind])

    block_rows = 64
    block_bits = block_rows.bit_length() - 1
    row = lax.broadcasted_iota(jnp.int32, (block_rows, 128), 0)
    lane = lax.broadcasted_iota(jnp.int32, (block_rows, 128), 1)
    for layer in range(plan.layers):
        order = plan.orders[layer]
        base = lane + device_part
        for bit in range(block_bits):
            base = base + (((row >> bit) & 1) << order[bit])
        masks, turns = [], []
        one = jnp.int32(1)
        for pair in range(pair_qubits.shape[2]):
            first = plan.locate(pair_qubits[layer, 0, pair], layer)
            second = plan.locate(pair_qubits[layer, 1, pair], layer)
            masks.append((one << first) | (one << second))
            turns.append(pair_angles[layer, pair] * np.float32(0.5 / np.pi))
        if layer == 0:
            size = jnp.ones((8, 128), jnp.float32)
            cut_masks, cut_turns = [], []
            for cut in range(cut_qubits.shape[1]):
                first = plan.locate(cut_qubits[0, cut], layer)
                second = plan.locate(cut_qubits[1, cut], layer)
                cut_masks.append((one << first) | (one << second))
                chosen = path_index[cut] == 0
                cosine, sine = turn(jnp.full((8, 128), cut_angle[cut] * np.float32(0.5 / np.pi)))
                size = size * jnp.where(chosen, cosine, sine)
                cut_turns.append(jnp.where(chosen, 0.0, 0.25))
            sizes[...] = size

        @pl.loop(0, rows // block_rows)
        def _(block):
            offset = jnp.int32(0)
            for bit in range(block_bits, len(order)):
                offset = offset + (((block >> (bit - block_bits)) & 1) << order[bit])
            index = base + offset
            angle = jnp.zeros((block_rows, 128), jnp.float32)
            for mask, amount in zip(masks, turns):
                angle = angle + jnp.where((index & mask) == mask, amount, 0.0)
            if layer == 0:
                for mask, amount in zip(cut_masks, cut_turns):
                    both = index & mask
                    angle = angle + jnp.where((both == 0) | (both == mask), -amount, amount)
            cosine, sine = turn(angle)
            at = pl.ds(pl.multiple_of(block * block_rows, block_rows), block_rows)
            cosine = jnp.round(cosine * STEPS).astype(jnp.int32)
            sine = jnp.round(sine * STEPS).astype(jnp.int32)
            phases[layer, at, :] = (cosine << 16) | (sine & 0xFFFF)


def offset_of(number, bits, order):
    return sum(((number >> k) & 1) << order.index(bit) for k, bit in enumerate(bits))


def split(values):
    large = values.astype(jnp.bfloat16)
    return large, (values - large.astype(jnp.float32)).astype(jnp.bfloat16)


def layers_kernel(plan, rows, state, near, last, phases, sizes, result, last_here, held, parts, out, done):
    layers = plan.layers
    copies = []

    def starts(layer, side, half, order, height):
        fixed = [plan.targets[layer]] + plan.halves
        rest = [bit for bit in plan.orders[layer] if bit not in fixed][height:]
        base = side << order.index(plan.targets[layer])
        if plan.halves:
            base += half << order.index(plan.halves[0])
        return [base + offset_of(number, rest, order) for number in range(1 << len(rest))]

    def products(layer, half):
        order, step = plan.orders[layer], plan.steps[layer]
        pieces = []
        for part in range(2):
            if layer == 0 or step:
                old_order = plan.orders[layer - 1] if layer else list(range(LANE_BITS, plan.local_bits))
                sides = []
                for side in range(2):
                    if layer == 0:
                        tiles = [state[pl.ds(2 * at + part, 8, 2 << step), :]
                                 for at in starts(layer, side, half, old_order, 3)]
                    else:
                        tiles = [held[part, pl.ds(at, 8, 1 << step), :]
                                 for at in starts(layer, side, half, old_order, 3)]
                    sides.append(jnp.concatenate(tiles, axis=0))
                pieces.append(split(jnp.concatenate(sides, axis=1)))
            else:
                pieces.append([
                    jnp.concatenate([
                        jnp.concatenate([parts[layer % 2, size, part, at:at + 16, :]
                                         for at in starts(layer, side, half, order, 4)], axis=0)
                        for side in range(2)
                    ], axis=1)
                    for size in range(2)
                ])
        weights = last_here if layer == layers - 1 else near.at[layer]
        joined = jnp.concatenate([pieces[part][size] for part in range(2) for size in range(2)], axis=0)
        count = joined.shape[0] // 4
        sums = []
        for kind in range(2):
            each = jnp.dot(joined, weights[kind], preferred_element_type=jnp.float32)
            sums.append([each[2 * part * count:(2 * part + 1) * count] + each[(2 * part + 1) * count:(2 * part + 2) * count]
                         for part in range(2)])
        return [sums[0][0] - sums[1][1], sums[1][0] + sums[0][1]]

    def turned(layer, half, results):
        order = plan.orders[layer]
        unit = jnp.full((16, 128), 1 / STEPS, jnp.float32)
        if layer == 0:
            unit = unit * sizes[0:1, :]
        for side in range(2):
            for tile, at in enumerate(starts(layer, side, half, order, 4)):
                real, imag = [result[16 * tile:16 * tile + 16, 128 * side:128 * side + 128] for result in results]
                word = phases[layer, at:at + 16, :]
                cosine = (word >> 16).astype(jnp.float32) * unit
                sine = ((word << 16) >> 16).astype(jnp.float32) * unit
                for part, value in enumerate((cosine * real - sine * imag, sine * real + cosine * imag)):
                    if layer == layers - 1:
                        block = tuple(int(k) for k in np.unravel_index(at // 16, plan.shape))
                        out[block + (pl.ds(part, 16, 2), slice(None))] = value
                    elif plan.steps[layer + 1]:
                        held[part, at:at + 16, :] = value
                    else:
                        large, small = split(value)
                        parts[(layer + 1) % 2, 0, part, at:at + 16, :] = large
                        parts[(layer + 1) % 2, 1, part, at:at + 16, :] = small
            if layer == layers - 1:
                chosen = {plan.targets[layer]: side}
                if plan.halves:
                    chosen[plan.halves[0]] = half
                here = tuple(chosen.get(bit, slice(None)) for bit in plan.axes)
                copies.append(pltpu.make_async_copy(out.at[here], result.at[here], done.at[len(copies)]))
                copies[-1].start()

    waiting = None
    for layer in range(layers):
        for half in range(1 << len(plan.halves)):
            results = products(layer, half)
            if (layer, half) == (0, 0):
                for kind in range(2):
                    widen(last[kind].astype(jnp.float32), last_here.at[kind])
            if plan.halves and waiting:
                turned(*waiting)
                waiting = None
            if plan.halves:
                waiting = (layer, half, results)
            else:
                turned(layer, half, results)
    if waiting:
        turned(*waiting)
    for copy in copies:
        copy.wait()


def shards(
    amplitudes, gate_matrices, phase_qubits, phase_angles, cut_qubits, cut_angle, path_index
):
    devices = lax.axis_size("hi")
    global_count = devices.bit_length() - 1
    amp_count = amplitudes.shape[1]
    rows = amp_count >> LANE_BITS
    layers = gate_matrices.shape[0]
    plan = Plan(global_count, amp_count.bit_length() - 1, layers)

    shaped = with_layout_constraint(amplitudes.reshape(2, rows, 128), Layout(major_to_minor=(1, 0, 2)))
    sent = shaped.transpose(1, 0, 2).reshape(devices, -1, 128)
    came = lax.all_to_all(sent, "hi", split_axis=0, concat_axis=0, tiled=True).reshape(2 * rows, 128)

    vmem, smem = pl.BlockSpec(memory_space=pltpu.VMEM), pl.BlockSpec(memory_space=pltpu.SMEM)
    weights_shape = (2, 256, 256)
    near, last, phases, sizes = pl.pallas_call(
        functools.partial(tables_kernel, plan, rows),
        out_shape=(
            jax.ShapeDtypeStruct((layers - 1,) + weights_shape, jnp.bfloat16),
            jax.ShapeDtypeStruct((2, 128, 128), jnp.bfloat16),
            jax.ShapeDtypeStruct((layers, rows, 128), jnp.int32),
            jax.ShapeDtypeStruct((8, 128), jnp.float32),
        ),
        in_specs=[vmem] + [smem] * 5,
        out_specs=[vmem] * 4,
        cost_estimate=pl.CostEstimate(flops=100 * layers * amp_count, bytes_accessed=4 * layers * amp_count, transcendentals=0),
        compiler_params=pltpu.CompilerParams(vmem_limit_bytes=24 << 20),
        name="tables",
    )(gate_matrices, phase_qubits.transpose(0, 2, 1), phase_angles, cut_qubits.T, cut_angle, path_index)

    result = pl.pallas_call(
        functools.partial(layers_kernel, plan, rows),
        out_shape=jax.ShapeDtypeStruct(plan.shape + (32, 128), jnp.float32),
        in_specs=[vmem] * 5,
        out_specs=pl.BlockSpec(memory_space=pltpu.HBM),
        scratch_shapes=[
            pltpu.VMEM(weights_shape, jnp.bfloat16),
            pltpu.VMEM((2, rows, 128), jnp.float32),
            pltpu.VMEM((2, 2, 2, rows, 128), jnp.bfloat16),
            pltpu.VMEM(plan.shape + (32, 128), jnp.float32),
            pltpu.SemaphoreType.DMA((2 << len(plan.halves),)),
        ],
        compiler_params=pltpu.CompilerParams(vmem_limit_bytes=24 << 20),
        name="layers",
    )(came, near, last, phases, sizes).reshape(2 * rows, 128)

    if plan.orders[-1] != plan.wanted:
        bits = len(plan.wanted)
        shaped = result.reshape((2,) * bits + (2, 128))
        axes = [bits - 1 - plan.orders[-1].index(plan.wanted[bits - 1 - axis]) for axis in range(bits)]
        result = shaped.transpose(axes + [bits, bits + 1]).reshape(2 * rows, 128)
    if plan.extra:
        size = 1 << plan.extra
        groups = [list(range(first, first + size)) for first in range(0, devices, size)]
        result = lax.all_to_all(
            result.reshape(size, -1, 128), "hi", split_axis=0, concat_axis=0,
            axis_index_groups=groups, tiled=True,
        )
    return result.reshape(rows, 2, 128).transpose(1, 0, 2).reshape(2, amp_count)


def solution(mesh):
    placed = (
        P(None, ("paths", "hi")),
        P(),
        P("paths", None, None),
        P("paths", None),
        P("paths", None),
        P("paths"),
        P("paths"),
    )
    return jax.shard_map(
        shards, mesh=mesh, in_specs=placed, out_specs=P(None, ("paths", "hi")), check_vma=False
    )
```

```python
import functools

import jax
import jax.numpy as jnp
import numpy as np
from jax import lax
from jax.experimental import pallas as pl
from jax.experimental.layout import Layout, with_layout_constraint
from jax.experimental.pallas import tpu as pltpu
from jax.sharding import PartitionSpec as P

LANE_BITS = 7
GATE_BITS = 6
STEPS = 32767.0


def fitted(function, degree):
    nodes = np.cos(np.pi * (np.arange(64) + 0.5) / 64) * 0.125 + 0.125
    series = np.polynomial.chebyshev.Chebyshev.fit(nodes, function(np.sqrt(nodes)), degree, domain=[0, 0.25])
    return [float(c) for c in series.convert(kind=np.polynomial.Polynomial).coef]


COS_TERMS = fitted(lambda v: np.cos(2 * np.pi * v), 7)
SIN_TERMS = fitted(lambda v: np.sin(2 * np.pi * v) / v, 6)


def horner(terms, w):
    total = jnp.full_like(w, terms[-1])
    for term in terms[-2::-1]:
        total = total * w + term
    return total


def turn(angle):
    part = angle - jnp.round(angle)
    square = part * part
    return horner(COS_TERMS, square), part * horner(SIN_TERMS, square)


class Plan:
    def __init__(self, global_count, local_bits, layers):
        self.global_count, self.local_bits, self.layers = global_count, local_bits, layers
        self.top = top = local_bits - global_count
        place = {}
        for label in range(local_bits + global_count):
            if label < top:
                place[label] = label
            elif label < local_bits:
                place[label] = label + global_count
            else:
                place[label] = label - global_count
        held = list(range(local_bits + global_count))
        self.targets = []
        for layer in range(layers):
            if layer < global_count:
                low, high = 7 + layer, local_bits + layer
                held[low], held[high] = held[high], held[low]
                target = low
            else:
                if layer == global_count:
                    held = held[:top] + held[local_bits:] + held[top:local_bits]
                target = local_bits - 2 * global_count + layer
            self.targets.append(place[held[target]])
        assert all(LANE_BITS <= bit < local_bits for bit in self.targets)
        ends = [place[label] for label in held]
        self.extra = sum(ends[local_bits + k] != local_bits + k for k in range(global_count))
        swapped = ends[:]
        for k in range(self.extra):
            low, high = local_bits - self.extra + k, local_bits + k
            assert ends[low] == high
            swapped[low], swapped[high] = ends[high], ends[low]
        assert swapped[local_bits:] == list(range(local_bits, local_bits + global_count))
        assert swapped[:LANE_BITS] == list(range(LANE_BITS))
        self.wanted = swapped[LANE_BITS:local_bits]
        self.orders, self.steps = [], []
        order = list(range(LANE_BITS, local_bits))
        for layer, target in enumerate(self.targets):
            step = 0
            if target in order[:4]:
                step = max(range(1, len(order) - 2), key=lambda at: self.lasts(order[at:at + 3], layer))
                triple = order[step:step + 3]
                if triple == self.wanted[:3] and not set(self.wanted[:4]) & set(self.targets[layer:]):
                    order = self.wanted
                else:
                    rest = sorted((bit for bit in order if bit not in triple), key=lambda bit: -self.lasts([bit], layer))
                    order = triple + rest
                assert target not in order[:4]
            self.steps.append(step)
            self.orders.append(order)

        self.halves = [bit for bit in order if bit not in self.targets
                       and all(other.index(bit) >= 4 for other in self.orders)][:1]

        self.axes, shape = [], []
        for bit in order[:3:-1]:
            apart = bit in [self.targets[-1]] + self.halves
            if not apart and self.axes and self.axes[-1] is None:
                shape[-1] *= 2
            else:
                self.axes.append(bit if apart else None)
                shape.append(2)
        self.shape = tuple(shape)

    def lasts(self, bits, layer):
        uses = self.targets[layer:]
        count = next((k for k, bit in enumerate(uses) if bit in bits), len(uses))
        return count + (count == len(uses) and bits == self.wanted[:3])

    def locate(self, qubit, layer):
        low, count = 7, min(layer + 1, self.global_count)
        size, high = self.global_count, self.local_bits
        if layer >= size:
            qubit = jnp.where(qubit >= high, qubit - size, jnp.where(qubit >= self.top, qubit + size, qubit))
        up = (qubit >= low) & (qubit < low + count)
        down = (qubit >= high) & (qubit < high + count)
        label = jnp.where(up, qubit + (high - low), jnp.where(down, qubit - (high - low), qubit))
        return jnp.where(label >= high, label - size, jnp.where(label >= self.top, label + size, label))


def widen(turned, block):
    lane = lax.broadcasted_iota(jnp.int32, (128, 128), 1)
    for to_bit in range(2):
        kept = jnp.where((lane >= 64) == (to_bit == 1), turned, 0.0)
        moved = pltpu.roll(kept, 64, 1)
        first, second = (kept, moved) if to_bit == 0 else (moved, kept)
        for from_bit in range(2):
            part = slice(64 * from_bit, 64 * from_bit + 64)
            both = jnp.concatenate([first[part], second[part]], axis=0)
            block[128 * from_bit:128 * from_bit + 128, 128 * to_bit:128 * to_bit + 128] = both.astype(jnp.bfloat16)


def tables_kernel(plan, rows, gates, pair_qubits, pair_angles, cut_qubits, cut_angle, path_index,
                  near, last, phases, sizes):
    device_part = lax.axis_index("hi") << plan.local_bits
    for layer in range(plan.layers):
        for kind in range(2):
            turned = gates[layer, kind].astype(jnp.float32).T
            if layer == plan.layers - 1:
                last[kind] = turned.astype(jnp.bfloat16)
            else:
                widen(turned, near.at[layer, kind])

    block_rows = 64
    block_bits = block_rows.bit_length() - 1
    row = lax.broadcasted_iota(jnp.int32, (block_rows, 128), 0)
    lane = lax.broadcasted_iota(jnp.int32, (block_rows, 128), 1)
    for layer in range(plan.layers):
        order = plan.orders[layer]
        base = lane + device_part
        for bit in range(block_bits):
            base = base + (((row >> bit) & 1) << order[bit])
        masks, turns = [], []
        one = jnp.int32(1)
        for pair in range(pair_qubits.shape[2]):
            first = plan.locate(pair_qubits[layer, 0, pair], layer)
            second = plan.locate(pair_qubits[layer, 1, pair], layer)
            masks.append((one << first) | (one << second))
            turns.append(pair_angles[layer, pair] * np.float32(0.5 / np.pi))
        if layer == 0:
            size = jnp.ones((8, 128), jnp.float32)
            cut_masks, cut_turns = [], []
            for cut in range(cut_qubits.shape[1]):
                first = plan.locate(cut_qubits[0, cut], layer)
                second = plan.locate(cut_qubits[1, cut], layer)
                cut_masks.append((one << first) | (one << second))
                chosen = path_index[cut] == 0
                cosine, sine = turn(jnp.full((8, 128), cut_angle[cut] * np.float32(0.5 / np.pi)))
                size = size * jnp.where(chosen, cosine, sine)
                cut_turns.append(jnp.where(chosen, 0.0, 0.25))
            sizes[...] = size

        @pl.loop(0, rows // block_rows)
        def _(block):
            offset = jnp.int32(0)
            for bit in range(block_bits, len(order)):
                offset = offset + (((block >> (bit - block_bits)) & 1) << order[bit])
            index = base + offset
            angle = jnp.zeros((block_rows, 128), jnp.float32)
            for mask, amount in zip(masks, turns):
                angle = angle + jnp.where((index & mask) == mask, amount, 0.0)
            if layer == 0:
                for mask, amount in zip(cut_masks, cut_turns):
                    both = index & mask
                    angle = angle + jnp.where((both == 0) | (both == mask), -amount, amount)
            cosine, sine = turn(angle)
            at = pl.ds(pl.multiple_of(block * block_rows, block_rows), block_rows)
            cosine = jnp.round(cosine * STEPS).astype(jnp.int32)
            sine = jnp.round(sine * STEPS).astype(jnp.int32)
            phases[layer, at, :] = (cosine << 16) | (sine & 0xFFFF)


def offset_of(number, bits, order):
    return sum(((number >> k) & 1) << order.index(bit) for k, bit in enumerate(bits))


def split(values):
    large = values.astype(jnp.bfloat16)
    return large, (values - large.astype(jnp.float32)).astype(jnp.bfloat16)


def layers_kernel(plan, rows, state, near, last, phases, sizes, result, last_here, held, parts, out, done):
    layers = plan.layers
    copies = []

    def starts(layer, side, half, order, height):
        fixed = [plan.targets[layer]] + plan.halves
        rest = [bit for bit in plan.orders[layer] if bit not in fixed][height:]
        base = side << order.index(plan.targets[layer])
        if plan.halves:
            base += half << order.index(plan.halves[0])
        return [base + offset_of(number, rest, order) for number in range(1 << len(rest))]

    def products(layer, half):
        order, step = plan.orders[layer], plan.steps[layer]
        pieces = []
        for part in range(3):
            if layer == 0 or step:
                if part == 2:
                    pieces.append([-value for value in pieces[1]])
                    continue
                old_order = plan.orders[layer - 1] if layer else list(range(LANE_BITS, plan.local_bits))
                sides = []
                for side in range(2):
                    if layer == 0:
                        tiles = [state[pl.ds(2 * at + part, 8, 2 << step), :]
                                 for at in starts(layer, side, half, old_order, 3)]
                    else:
                        tiles = [held[part, pl.ds(at, 8, 1 << step), :]
                                 for at in starts(layer, side, half, old_order, 3)]
                    sides.append(jnp.concatenate(tiles, axis=0))
                pieces.append(split(jnp.concatenate(sides, axis=1)))
            else:
                pieces.append([
                    jnp.concatenate([
                        jnp.concatenate([parts[layer % 2, size, part, at:at + 16, :]
                                         for at in starts(layer, side, half, order, 4)], axis=0)
                        for side in range(2)
                    ], axis=1)
                    for size in range(2)
                ])
        weights = last_here if layer == layers - 1 else near.at[layer]
        real, imag = weights[0], weights[1]
        results = []
        for second, (upper, lower) in ((2, (real, imag)), (1, (imag, real))):
            joined = jnp.concatenate([pieces[part][size] for size in range(2) for part in (0, second)], axis=1)
            weight = jnp.concatenate([upper, lower, upper, lower], axis=0)
            results.append(jnp.dot(joined, weight, preferred_element_type=jnp.float32))
        return results

    def turned(layer, half, results):
        order = plan.orders[layer]
        unit = jnp.full((16, 128), 1 / STEPS, jnp.float32)
        if layer == 0:
            unit = unit * sizes[0:1, :]
        for side in range(2):
            for tile, at in enumerate(starts(layer, side, half, order, 4)):
                real, imag = [result[16 * tile:16 * tile + 16, 128 * side:128 * side + 128] for result in results]
                word = phases[layer, at:at + 16, :]
                cosine = (word >> 16).astype(jnp.float32) * unit
                sine = ((word << 16) >> 16).astype(jnp.float32) * unit
                for part, value in enumerate((cosine * real - sine * imag, sine * real + cosine * imag)):
                    if layer == layers - 1:
                        block = tuple(int(k) for k in np.unravel_index(at // 16, plan.shape))
                        out[block + (pl.ds(part, 16, 2), slice(None))] = value
                    elif plan.steps[layer + 1]:
                        held[part, at:at + 16, :] = value
                    else:
                        large, small = split(value)
                        parts[(layer + 1) % 2, 0, part, at:at + 16, :] = large
                        parts[(layer + 1) % 2, 1, part, at:at + 16, :] = small
                        if part == 1:
                            parts[(layer + 1) % 2, 0, 2, at:at + 16, :] = -large
                            parts[(layer + 1) % 2, 1, 2, at:at + 16, :] = -small
            if layer == layers - 1:
                chosen = {plan.targets[layer]: side}
                if plan.halves:
                    chosen[plan.halves[0]] = half
                here = tuple(chosen.get(bit, slice(None)) for bit in plan.axes)
                copies.append(pltpu.make_async_copy(out.at[here], result.at[here], done.at[len(copies)]))
                copies[-1].start()

    waiting = None
    for layer in range(layers):
        for half in range(1 << len(plan.halves)):
            results = products(layer, half)
            if (layer, half) == (0, 0):
                for kind in range(2):
                    widen(last[kind].astype(jnp.float32), last_here.at[kind])
            if plan.halves and waiting:
                turned(*waiting)
                waiting = None
            if plan.halves:
                waiting = (layer, half, results)
            else:
                turned(layer, half, results)
    if waiting:
        turned(*waiting)
    for copy in copies:
        copy.wait()


def shards(
    amplitudes, gate_matrices, phase_qubits, phase_angles, cut_qubits, cut_angle, path_index
):
    devices = lax.axis_size("hi")
    global_count = devices.bit_length() - 1
    amp_count = amplitudes.shape[1]
    rows = amp_count >> LANE_BITS
    layers = gate_matrices.shape[0]
    plan = Plan(global_count, amp_count.bit_length() - 1, layers)

    shaped = with_layout_constraint(amplitudes.reshape(2, rows, 128), Layout(major_to_minor=(1, 0, 2)))
    sent = shaped.transpose(1, 0, 2).reshape(devices, -1, 128)
    came = lax.all_to_all(sent, "hi", split_axis=0, concat_axis=0, tiled=True).reshape(2 * rows, 128)

    vmem, smem = pl.BlockSpec(memory_space=pltpu.VMEM), pl.BlockSpec(memory_space=pltpu.SMEM)
    weights_shape = (2, 256, 256)
    near, last, phases, sizes = pl.pallas_call(
        functools.partial(tables_kernel, plan, rows),
        out_shape=(
            jax.ShapeDtypeStruct((layers - 1,) + weights_shape, jnp.bfloat16),
            jax.ShapeDtypeStruct((2, 128, 128), jnp.bfloat16),
            jax.ShapeDtypeStruct((layers, rows, 128), jnp.int32),
            jax.ShapeDtypeStruct((8, 128), jnp.float32),
        ),
        in_specs=[vmem] + [smem] * 5,
        out_specs=[vmem] * 4,
        cost_estimate=pl.CostEstimate(flops=100 * layers * amp_count, bytes_accessed=4 * layers * amp_count, transcendentals=0),
        compiler_params=pltpu.CompilerParams(vmem_limit_bytes=24 << 20),
        name="tables",
    )(gate_matrices, phase_qubits.transpose(0, 2, 1), phase_angles, cut_qubits.T, cut_angle, path_index)

    result = pl.pallas_call(
        functools.partial(layers_kernel, plan, rows),
        out_shape=jax.ShapeDtypeStruct(plan.shape + (32, 128), jnp.float32),
        in_specs=[vmem] * 5,
        out_specs=pl.BlockSpec(memory_space=pltpu.HBM),
        scratch_shapes=[
            pltpu.VMEM(weights_shape, jnp.bfloat16),
            pltpu.VMEM((2, rows, 128), jnp.float32),
            pltpu.VMEM((2, 2, 3, rows, 128), jnp.bfloat16),
            pltpu.VMEM(plan.shape + (32, 128), jnp.float32),
            pltpu.SemaphoreType.DMA((2 << len(plan.halves),)),
        ],
        compiler_params=pltpu.CompilerParams(vmem_limit_bytes=24 << 20),
        name="layers",
    )(came, near, last, phases, sizes).reshape(2 * rows, 128)

    if plan.orders[-1] != plan.wanted:
        bits = len(plan.wanted)
        shaped = result.reshape((2,) * bits + (2, 128))
        axes = [bits - 1 - plan.orders[-1].index(plan.wanted[bits - 1 - axis]) for axis in range(bits)]
        result = shaped.transpose(axes + [bits, bits + 1]).reshape(2 * rows, 128)
    if plan.extra:
        size = 1 << plan.extra
        groups = [list(range(first, first + size)) for first in range(0, devices, size)]
        result = lax.all_to_all(
            result.reshape(size, -1, 128), "hi", split_axis=0, concat_axis=0,
            axis_index_groups=groups, tiled=True,
        )
    return result.reshape(rows, 2, 128).transpose(1, 0, 2).reshape(2, amp_count)


def solution(mesh):
    placed = (
        P(None, ("paths", "hi")),
        P(),
        P("paths", None, None),
        P("paths", None),
        P("paths", None),
        P("paths"),
        P("paths"),
    )
    return jax.shard_map(
        shards, mesh=mesh, in_specs=placed, out_specs=P(None, ("paths", "hi")), check_vma=False
    )
```

```python
import functools

import jax
import jax.numpy as jnp
import numpy as np
from jax import lax
from jax.experimental import pallas as pl
from jax.experimental.layout import Layout, with_layout_constraint
from jax.experimental.pallas import tpu as pltpu
from jax.sharding import PartitionSpec as P

LANE_BITS = 7
GATE_BITS = 6
STEPS = 32767.0


def fitted(function, degree):
    nodes = np.cos(np.pi * (np.arange(64) + 0.5) / 64) * 0.125 + 0.125
    series = np.polynomial.chebyshev.Chebyshev.fit(nodes, function(np.sqrt(nodes)), degree, domain=[0, 0.25])
    return [float(c) for c in series.convert(kind=np.polynomial.Polynomial).coef]


COS_TERMS = fitted(lambda v: np.cos(2 * np.pi * v), 7)
SIN_TERMS = fitted(lambda v: np.sin(2 * np.pi * v) / v, 6)


def horner(terms, w):
    total = jnp.full_like(w, terms[-1])
    for term in terms[-2::-1]:
        total = total * w + term
    return total


def turn(angle):
    part = angle - jnp.round(angle)
    square = part * part
    return horner(COS_TERMS, square), part * horner(SIN_TERMS, square)


class Plan:
    def __init__(self, global_count, local_bits, layers):
        self.global_count, self.local_bits, self.layers = global_count, local_bits, layers
        self.top = top = local_bits - global_count
        place = {}
        for label in range(local_bits + global_count):
            if label < top:
                place[label] = label
            elif label < local_bits:
                place[label] = label + global_count
            else:
                place[label] = label - global_count
        held = list(range(local_bits + global_count))
        self.targets = []
        for layer in range(layers):
            if layer < global_count:
                low, high = 7 + layer, local_bits + layer
                held[low], held[high] = held[high], held[low]
                target = low
            else:
                if layer == global_count:
                    held = held[:top] + held[local_bits:] + held[top:local_bits]
                target = local_bits - 2 * global_count + layer
            self.targets.append(place[held[target]])
        assert all(LANE_BITS <= bit < local_bits for bit in self.targets)
        ends = [place[label] for label in held]
        self.extra = sum(ends[local_bits + k] != local_bits + k for k in range(global_count))
        swapped = ends[:]
        for k in range(self.extra):
            low, high = local_bits - self.extra + k, local_bits + k
            assert ends[low] == high
            swapped[low], swapped[high] = ends[high], ends[low]
        assert swapped[local_bits:] == list(range(local_bits, local_bits + global_count))
        assert swapped[:LANE_BITS] == list(range(LANE_BITS))
        self.wanted = swapped[LANE_BITS:local_bits]
        self.orders, self.steps = [], []
        order = list(range(LANE_BITS, local_bits))
        for layer, target in enumerate(self.targets):
            step = 0
            if target in order[:4]:
                step = max(range(1, len(order) - 2), key=lambda at: self.lasts(order[at:at + 3], layer))
                triple = order[step:step + 3]
                if triple == self.wanted[:3] and not set(self.wanted[:4]) & set(self.targets[layer:]):
                    order = self.wanted
                else:
                    rest = sorted((bit for bit in order if bit not in triple), key=lambda bit: -self.lasts([bit], layer))
                    order = triple + rest
                assert target not in order[:4]
            self.steps.append(step)
            self.orders.append(order)

        self.halves = [bit for bit in order if bit not in self.targets
                       and all(other.index(bit) >= 4 for other in self.orders)][:1]

        self.axes, shape = [], []
        for bit in order[:3:-1]:
            apart = bit in [self.targets[-1]] + self.halves
            if not apart and self.axes and self.axes[-1] is None:
                shape[-1] *= 2
            else:
                self.axes.append(bit if apart else None)
                shape.append(2)
        self.shape = tuple(shape)

    def lasts(self, bits, layer):
        uses = self.targets[layer:]
        count = next((k for k, bit in enumerate(uses) if bit in bits), len(uses))
        return count + (count == len(uses) and bits == self.wanted[:3])

    def locate(self, qubit, layer):
        low, count = 7, min(layer + 1, self.global_count)
        size, high = self.global_count, self.local_bits
        if layer >= size:
            qubit = jnp.where(qubit >= high, qubit - size, jnp.where(qubit >= self.top, qubit + size, qubit))
        up = (qubit >= low) & (qubit < low + count)
        down = (qubit >= high) & (qubit < high + count)
        label = jnp.where(up, qubit + (high - low), jnp.where(down, qubit - (high - low), qubit))
        return jnp.where(label >= high, label - size, jnp.where(label >= self.top, label + size, label))


def widen(turned, block):
    lane = lax.broadcasted_iota(jnp.int32, (128, 128), 1)
    for to_bit in range(2):
        kept = jnp.where((lane >= 64) == (to_bit == 1), turned, 0.0)
        moved = pltpu.roll(kept, 64, 1)
        first, second = (kept, moved) if to_bit == 0 else (moved, kept)
        for from_bit in range(2):
            part = slice(64 * from_bit, 64 * from_bit + 64)
            both = jnp.concatenate([first[part], second[part]], axis=0)
            block[128 * from_bit:128 * from_bit + 128, 128 * to_bit:128 * to_bit + 128] = both.astype(jnp.bfloat16)


def tables_kernel(plan, rows, gates, pair_qubits, pair_angles, cut_qubits, cut_angle, path_index,
                  near, last, phases, sizes):
    device_part = lax.axis_index("hi") << plan.local_bits
    for layer in range(plan.layers):
        for kind in range(2):
            turned = gates[layer, kind].astype(jnp.float32).T
            if layer == plan.layers - 1:
                last[kind] = turned.astype(jnp.bfloat16)
            else:
                widen(turned, near.at[layer, kind])

    block_rows = 64
    block_bits = block_rows.bit_length() - 1
    row = lax.broadcasted_iota(jnp.int32, (block_rows, 128), 0)
    lane = lax.broadcasted_iota(jnp.int32, (block_rows, 128), 1)
    for layer in range(plan.layers):
        order = plan.orders[layer]
        base = lane + device_part
        for bit in range(block_bits):
            base = base + (((row >> bit) & 1) << order[bit])
        masks, turns = [], []
        one = jnp.int32(1)
        for pair in range(pair_qubits.shape[2]):
            first = plan.locate(pair_qubits[layer, 0, pair], layer)
            second = plan.locate(pair_qubits[layer, 1, pair], layer)
            masks.append((one << first) | (one << second))
            turns.append(pair_angles[layer, pair] * np.float32(0.5 / np.pi))
        if layer == 0:
            size = jnp.ones((8, 128), jnp.float32)
            cut_masks, cut_turns = [], []
            for cut in range(cut_qubits.shape[1]):
                first = plan.locate(cut_qubits[0, cut], layer)
                second = plan.locate(cut_qubits[1, cut], layer)
                cut_masks.append((one << first) | (one << second))
                chosen = path_index[cut] == 0
                cosine, sine = turn(jnp.full((8, 128), cut_angle[cut] * np.float32(0.5 / np.pi)))
                size = size * jnp.where(chosen, cosine, sine)
                cut_turns.append(jnp.where(chosen, 0.0, 0.25))
            sizes[...] = size

        @pl.loop(0, rows // block_rows)
        def _(block):
            offset = jnp.int32(0)
            for bit in range(block_bits, len(order)):
                offset = offset + (((block >> (bit - block_bits)) & 1) << order[bit])
            index = base + offset
            angle = jnp.zeros((block_rows, 128), jnp.float32)
            for mask, amount in zip(masks, turns):
                angle = angle + jnp.where((index & mask) == mask, amount, 0.0)
            if layer == 0:
                for mask, amount in zip(cut_masks, cut_turns):
                    both = index & mask
                    angle = angle + jnp.where((both == 0) | (both == mask), -amount, amount)
            cosine, sine = turn(angle)
            at = pl.ds(pl.multiple_of(block * block_rows, block_rows), block_rows)
            cosine = jnp.round(cosine * STEPS).astype(jnp.int32)
            sine = jnp.round(sine * STEPS).astype(jnp.int32)
            phases[layer, at, :] = (cosine << 16) | (sine & 0xFFFF)


def offset_of(number, bits, order):
    return sum(((number >> k) & 1) << order.index(bit) for k, bit in enumerate(bits))


def split(values):
    large = values.astype(jnp.bfloat16)
    return large, (values - large.astype(jnp.float32)).astype(jnp.bfloat16)


def layers_kernel(plan, rows, came, taken, near, last, phases, sizes, result, last_here, held, parts, out, state, done):
    layers = plan.layers
    copies = []
    near_bit = lax.axis_index("hi") & 1
    size = taken.shape[1]
    for chip in range(taken.shape[0]):
        mine = pl.ds(pl.multiple_of(near_bit * size, size), size)
        state[pl.ds(pl.multiple_of((2 * chip + near_bit) * size, size), size), :] = came[chip, mine, :]
        state[pl.ds(pl.multiple_of((2 * chip + 1 - near_bit) * size, size), size), :] = taken[chip]

    def starts(layer, side, half, order, height):
        fixed = [plan.targets[layer]] + plan.halves
        rest = [bit for bit in plan.orders[layer] if bit not in fixed][height:]
        base = side << order.index(plan.targets[layer])
        if plan.halves:
            base += half << order.index(plan.halves[0])
        return [base + offset_of(number, rest, order) for number in range(1 << len(rest))]

    def products(layer, half):
        order, step = plan.orders[layer], plan.steps[layer]
        pieces = []
        for part in range(3):
            if layer == 0 or step:
                if part == 2:
                    pieces.append([-value for value in pieces[1]])
                    continue
                old_order = plan.orders[layer - 1] if layer else list(range(LANE_BITS, plan.local_bits))
                sides = []
                for side in range(2):
                    if layer == 0:
                        tiles = [state[pl.ds(2 * at + part, 8, 2 << step), :]
                                 for at in starts(layer, side, half, old_order, 3)]
                    else:
                        tiles = [held[part, pl.ds(at, 8, 1 << step), :]
                                 for at in starts(layer, side, half, old_order, 3)]
                    sides.append(jnp.concatenate(tiles, axis=0))
                pieces.append(split(jnp.concatenate(sides, axis=1)))
            else:
                pieces.append([
                    jnp.concatenate([
                        jnp.concatenate([parts[layer % 2, size, part, at:at + 16, :]
                                         for at in starts(layer, side, half, order, 4)], axis=0)
                        for side in range(2)
                    ], axis=1)
                    for size in range(2)
                ])
        weights = last_here if layer == layers - 1 else near.at[layer]
        real, imag = weights[0], weights[1]
        results = []
        for second, (upper, lower) in ((2, (real, imag)), (1, (imag, real))):
            joined = jnp.concatenate(
                [jnp.concatenate([pieces[0][size], pieces[second][size]], axis=1) for size in range(2)], axis=0
            )
            both = jnp.dot(joined, jnp.concatenate([upper, lower], axis=0), preferred_element_type=jnp.float32)
            results.append(both[:both.shape[0] // 2] + both[both.shape[0] // 2:])
        return results

    def turned(layer, half, results):
        order = plan.orders[layer]
        unit = jnp.full((16, 128), 1 / STEPS, jnp.float32)
        if layer == 0:
            unit = unit * sizes[0:1, :]
        for side in range(2):
            for tile, at in enumerate(starts(layer, side, half, order, 4)):
                real, imag = [result[16 * tile:16 * tile + 16, 128 * side:128 * side + 128] for result in results]
                word = phases[layer, at:at + 16, :]
                cosine = (word >> 16).astype(jnp.float32) * unit
                sine = ((word << 16) >> 16).astype(jnp.float32) * unit
                for part, value in enumerate((cosine * real - sine * imag, sine * real + cosine * imag)):
                    if layer == layers - 1:
                        block = tuple(int(k) for k in np.unravel_index(at // 16, plan.shape))
                        out[block + (pl.ds(part, 16, 2), slice(None))] = value
                    elif plan.steps[layer + 1]:
                        held[part, at:at + 16, :] = value
                    else:
                        large, small = split(value)
                        parts[(layer + 1) % 2, 0, part, at:at + 16, :] = large
                        parts[(layer + 1) % 2, 1, part, at:at + 16, :] = small
                        if part == 1:
                            parts[(layer + 1) % 2, 0, 2, at:at + 16, :] = -large
                            parts[(layer + 1) % 2, 1, 2, at:at + 16, :] = -small
            if layer == layers - 1:
                chosen = {plan.targets[layer]: side}
                if plan.halves:
                    chosen[plan.halves[0]] = half
                here = tuple(chosen.get(bit, slice(None)) for bit in plan.axes)
                copies.append(pltpu.make_async_copy(out.at[here], result.at[here], done.at[len(copies)]))
                copies[-1].start()

    waiting = None
    for layer in range(layers):
        for half in range(1 << len(plan.halves)):
            results = products(layer, half)
            if (layer, half) == (0, 0):
                for kind in range(2):
                    widen(last[kind].astype(jnp.float32), last_here.at[kind])
            if plan.halves and waiting:
                turned(*waiting)
                waiting = None
            if plan.halves:
                waiting = (layer, half, results)
            else:
                turned(layer, half, results)
    if waiting:
        turned(*waiting)
    for copy in copies:
        copy.wait()


def shards(
    amplitudes, gate_matrices, phase_qubits, phase_angles, cut_qubits, cut_angle, path_index
):
    devices = lax.axis_size("hi")
    global_count = devices.bit_length() - 1
    amp_count = amplitudes.shape[1]
    rows = amp_count >> LANE_BITS
    layers = gate_matrices.shape[0]
    plan = Plan(global_count, amp_count.bit_length() - 1, layers)

    shaped = with_layout_constraint(amplitudes.reshape(2, rows, 128), Layout(major_to_minor=(1, 0, 2)))
    sent = shaped.transpose(1, 0, 2).reshape(devices, -1, 128)
    near_bit = lax.axis_index("hi") & 1
    groups = [list(range(first, devices, 2)) for first in range(2)]
    came = lax.all_to_all(
        sent.reshape(devices // 2, -1, 128), "hi", split_axis=0, concat_axis=0, axis_index_groups=groups, tiled=True,
    )
    given = lax.dynamic_index_in_dim(came.reshape(devices // 2, 2, -1, 128), 1 - near_bit, 1, keepdims=False)
    taken = lax.ppermute(given, "hi", [(i, i ^ 1) for i in range(devices)])

    vmem, smem = pl.BlockSpec(memory_space=pltpu.VMEM), pl.BlockSpec(memory_space=pltpu.SMEM)
    weights_shape = (2, 256, 256)
    near, last, phases, sizes = pl.pallas_call(
        functools.partial(tables_kernel, plan, rows),
        out_shape=(
            jax.ShapeDtypeStruct((layers - 1,) + weights_shape, jnp.bfloat16),
            jax.ShapeDtypeStruct((2, 128, 128), jnp.bfloat16),
            jax.ShapeDtypeStruct((layers, rows, 128), jnp.int32),
            jax.ShapeDtypeStruct((8, 128), jnp.float32),
        ),
        in_specs=[vmem] + [smem] * 5,
        out_specs=[vmem] * 4,
        cost_estimate=pl.CostEstimate(flops=100 * layers * amp_count, bytes_accessed=4 * layers * amp_count, transcendentals=0),
        compiler_params=pltpu.CompilerParams(vmem_limit_bytes=24 << 20),
        name="tables",
    )(gate_matrices, phase_qubits.transpose(0, 2, 1), phase_angles, cut_qubits.T, cut_angle, path_index)

    result = pl.pallas_call(
        functools.partial(layers_kernel, plan, rows),
        out_shape=jax.ShapeDtypeStruct(plan.shape + (32, 128), jnp.float32),
        in_specs=[vmem] * 6,
        out_specs=pl.BlockSpec(memory_space=pltpu.HBM),
        scratch_shapes=[
            pltpu.VMEM(weights_shape, jnp.bfloat16),
            pltpu.VMEM((2, rows, 128), jnp.float32),
            pltpu.VMEM((2, 2, 3, rows, 128), jnp.bfloat16),
            pltpu.VMEM(plan.shape + (32, 128), jnp.float32),
            pltpu.VMEM((2 * rows, 128), jnp.float32),
            pltpu.SemaphoreType.DMA((2 << len(plan.halves),)),
        ],
        compiler_params=pltpu.CompilerParams(vmem_limit_bytes=24 << 20),
        name="layers",
    )(came, taken, near, last, phases, sizes).reshape(2 * rows, 128)

    if plan.orders[-1] != plan.wanted:
        bits = len(plan.wanted)
        shaped = result.reshape((2,) * bits + (2, 128))
        axes = [bits - 1 - plan.orders[-1].index(plan.wanted[bits - 1 - axis]) for axis in range(bits)]
        result = shaped.transpose(axes + [bits, bits + 1]).reshape(2 * rows, 128)
    if plan.extra:
        size = 1 << plan.extra
        groups = [list(range(first, first + size)) for first in range(0, devices, size)]
        result = lax.all_to_all(
            result.reshape(size, -1, 128), "hi", split_axis=0, concat_axis=0,
            axis_index_groups=groups, tiled=True,
        )
    return result.reshape(rows, 2, 128).transpose(1, 0, 2).reshape(2, amp_count)


def solution(mesh):
    placed = (
        P(None, ("paths", "hi")),
        P(),
        P("paths", None, None),
        P("paths", None),
        P("paths", None),
        P("paths"),
        P("paths"),
    )
    return jax.shard_map(
        shards, mesh=mesh, in_specs=placed, out_specs=P(None, ("paths", "hi")), check_vma=False
    )
```

```python
import functools

import jax
import jax.numpy as jnp
import numpy as np
from jax import lax
from jax.experimental import pallas as pl
from jax.experimental.layout import Layout, with_layout_constraint
from jax.experimental.pallas import tpu as pltpu
from jax.sharding import PartitionSpec as P

LANE_BITS = 7
GATE_BITS = 6
STEPS = 32767.0


def fitted(function, degree):
    nodes = np.cos(np.pi * (np.arange(64) + 0.5) / 64) * 0.125 + 0.125
    series = np.polynomial.chebyshev.Chebyshev.fit(nodes, function(np.sqrt(nodes)), degree, domain=[0, 0.25])
    return [float(c) for c in series.convert(kind=np.polynomial.Polynomial).coef]


COS_TERMS = fitted(lambda v: np.cos(2 * np.pi * v), 7)
SIN_TERMS = fitted(lambda v: np.sin(2 * np.pi * v) / v, 6)


def horner(terms, w):
    total = jnp.full_like(w, terms[-1])
    for term in terms[-2::-1]:
        total = total * w + term
    return total


def turn(angle):
    part = angle - jnp.round(angle)
    square = part * part
    return horner(COS_TERMS, square), part * horner(SIN_TERMS, square)


class Plan:
    def __init__(self, global_count, local_bits, layers):
        self.global_count, self.local_bits, self.layers = global_count, local_bits, layers
        self.top = top = local_bits - global_count
        place = {}
        for label in range(local_bits + global_count):
            if label < top:
                place[label] = label
            elif label < local_bits:
                place[label] = label + global_count
            else:
                place[label] = label - global_count
        held = list(range(local_bits + global_count))
        self.targets = []
        for layer in range(layers):
            if layer < global_count:
                low, high = 7 + layer, local_bits + layer
                held[low], held[high] = held[high], held[low]
                target = low
            else:
                if layer == global_count:
                    held = held[:top] + held[local_bits:] + held[top:local_bits]
                target = local_bits - 2 * global_count + layer
            self.targets.append(place[held[target]])
        assert all(LANE_BITS <= bit < local_bits for bit in self.targets)
        ends = [place[label] for label in held]
        self.extra = sum(ends[local_bits + k] != local_bits + k for k in range(global_count))
        swapped = ends[:]
        for k in range(self.extra):
            low, high = local_bits - self.extra + k, local_bits + k
            assert ends[low] == high
            swapped[low], swapped[high] = ends[high], ends[low]
        assert swapped[local_bits:] == list(range(local_bits, local_bits + global_count))
        assert swapped[:LANE_BITS] == list(range(LANE_BITS))
        self.wanted = swapped[LANE_BITS:local_bits]
        self.orders, self.steps = [], []
        order = list(range(LANE_BITS, local_bits))
        for layer, target in enumerate(self.targets):
            step = 0
            if target in order[:4]:
                step = max(range(1, len(order) - 2), key=lambda at: self.lasts(order[at:at + 3], layer))
                triple = order[step:step + 3]
                if triple == self.wanted[:3] and not set(self.wanted[:4]) & set(self.targets[layer:]):
                    order = self.wanted
                else:
                    rest = sorted((bit for bit in order if bit not in triple), key=lambda bit: -self.lasts([bit], layer))
                    order = triple + rest
                assert target not in order[:4]
            self.steps.append(step)
            self.orders.append(order)

        self.halves = [bit for bit in order if bit not in self.targets
                       and all(other.index(bit) >= 4 for other in self.orders)][:1]

        self.axes, shape = [], []
        for bit in order[:3:-1]:
            apart = bit in [self.targets[-1]] + self.halves
            if not apart and self.axes and self.axes[-1] is None:
                shape[-1] *= 2
            else:
                self.axes.append(bit if apart else None)
                shape.append(2)
        self.shape = tuple(shape)

    def lasts(self, bits, layer):
        uses = self.targets[layer:]
        count = next((k for k, bit in enumerate(uses) if bit in bits), len(uses))
        return count + (count == len(uses) and bits == self.wanted[:3])

    def locate(self, qubit, layer):
        low, count = 7, min(layer + 1, self.global_count)
        size, high = self.global_count, self.local_bits
        if layer >= size:
            qubit = jnp.where(qubit >= high, qubit - size, jnp.where(qubit >= self.top, qubit + size, qubit))
        up = (qubit >= low) & (qubit < low + count)
        down = (qubit >= high) & (qubit < high + count)
        label = jnp.where(up, qubit + (high - low), jnp.where(down, qubit - (high - low), qubit))
        return jnp.where(label >= high, label - size, jnp.where(label >= self.top, label + size, label))


def widen(turned, block):
    lane = lax.broadcasted_iota(jnp.int32, (128, 128), 1)
    for to_bit in range(2):
        kept = jnp.where((lane >= 64) == (to_bit == 1), turned, 0.0)
        moved = pltpu.roll(kept, 64, 1)
        first, second = (kept, moved) if to_bit == 0 else (moved, kept)
        for from_bit in range(2):
            part = slice(64 * from_bit, 64 * from_bit + 64)
            both = jnp.concatenate([first[part], second[part]], axis=0)
            block[128 * from_bit:128 * from_bit + 128, 128 * to_bit:128 * to_bit + 128] = both.astype(jnp.bfloat16)


def tables_kernel(plan, rows, gates, pair_qubits, pair_angles, cut_qubits, cut_angle, path_index,
                  near, last, phases, sizes):
    device_part = lax.axis_index("hi") << plan.local_bits
    for layer in range(plan.layers):
        for kind in range(2):
            turned = gates[layer, kind].astype(jnp.float32).T
            if layer == plan.layers - 1:
                last[kind] = turned.astype(jnp.bfloat16)
            else:
                widen(turned, near.at[layer, kind])

    block_rows = 64
    block_bits = block_rows.bit_length() - 1
    row = lax.broadcasted_iota(jnp.int32, (block_rows, 128), 0)
    lane = lax.broadcasted_iota(jnp.int32, (block_rows, 128), 1)
    for layer in range(plan.layers):
        order = plan.orders[layer]
        base = lane + device_part
        for bit in range(block_bits):
            base = base + (((row >> bit) & 1) << order[bit])
        masks, turns = [], []
        one = jnp.int32(1)
        for pair in range(pair_qubits.shape[2]):
            first = plan.locate(pair_qubits[layer, 0, pair], layer)
            second = plan.locate(pair_qubits[layer, 1, pair], layer)
            masks.append((one << first) | (one << second))
            turns.append(pair_angles[layer, pair] * np.float32(0.5 / np.pi))
        if layer == 0:
            size = jnp.ones((8, 128), jnp.float32)
            cut_masks, cut_turns = [], []
            for cut in range(cut_qubits.shape[1]):
                first = plan.locate(cut_qubits[0, cut], layer)
                second = plan.locate(cut_qubits[1, cut], layer)
                cut_masks.append((one << first) | (one << second))
                chosen = path_index[cut] == 0
                cosine, sine = turn(jnp.full((8, 128), cut_angle[cut] * np.float32(0.5 / np.pi)))
                size = size * jnp.where(chosen, cosine, sine)
                cut_turns.append(jnp.where(chosen, 0.0, 0.25))
            sizes[...] = size

        @pl.loop(0, rows // block_rows)
        def _(block):
            offset = jnp.int32(0)
            for bit in range(block_bits, len(order)):
                offset = offset + (((block >> (bit - block_bits)) & 1) << order[bit])
            index = base + offset
            angle = jnp.zeros((block_rows, 128), jnp.float32)
            for mask, amount in zip(masks, turns):
                angle = angle + jnp.where((index & mask) == mask, amount, 0.0)
            if layer == 0:
                for mask, amount in zip(cut_masks, cut_turns):
                    both = index & mask
                    angle = angle + jnp.where((both == 0) | (both == mask), -amount, amount)
            cosine, sine = turn(angle)
            at = pl.ds(pl.multiple_of(block * block_rows, block_rows), block_rows)
            cosine = jnp.round(cosine * STEPS).astype(jnp.int32)
            sine = jnp.round(sine * STEPS).astype(jnp.int32)
            phases[layer, at, :] = (cosine << 16) | (sine & 0xFFFF)


def offset_of(number, bits, order):
    return sum(((number >> k) & 1) << order.index(bit) for k, bit in enumerate(bits))


def split(values):
    large = values.astype(jnp.bfloat16)
    return large, (values - large.astype(jnp.float32)).astype(jnp.bfloat16)


def layers_kernel(plan, rows, state, near, last, phases, sizes, result, last_here, held, parts, out, done):
    layers = plan.layers
    copies = []

    def starts(layer, side, half, order, height):
        fixed = [plan.targets[layer]] + plan.halves
        rest = [bit for bit in plan.orders[layer] if bit not in fixed][height:]
        base = side << order.index(plan.targets[layer])
        if plan.halves:
            base += half << order.index(plan.halves[0])
        return [base + offset_of(number, rest, order) for number in range(1 << len(rest))]

    def products(layer, half):
        order, step = plan.orders[layer], plan.steps[layer]
        pieces = []
        for part in range(2):
            if layer == 0 or step:
                old_order = plan.orders[layer - 1] if layer else list(range(LANE_BITS, plan.local_bits))
                sides = []
                for side in range(2):
                    if layer == 0:
                        tiles = [state[pl.ds(2 * at + part, 8, 2 << step), :]
                                 for at in starts(layer, side, half, old_order, 3)]
                    else:
                        tiles = [held[part, pl.ds(at, 8, 1 << step), :]
                                 for at in starts(layer, side, half, old_order, 3)]
                    sides.append(jnp.concatenate(tiles, axis=0))
                pieces.append(split(jnp.concatenate(sides, axis=1)))
            else:
                pieces.append([
                    jnp.concatenate([
                        jnp.concatenate([parts[layer % 2, size, part, at:at + 16, :]
                                         for at in starts(layer, side, half, order, 4)], axis=0)
                        for side in range(2)
                    ], axis=1)
                    for size in range(2)
                ])
        weights = last_here if layer == layers - 1 else near.at[layer]
        real, imag = weights[0], weights[1]
        results = []
        joined = jnp.concatenate(
            [jnp.concatenate([pieces[0][size], pieces[1][size]], axis=1) for size in range(2)], axis=0
        )
        for upper, lower in ((real, -imag), (imag, real)):
            both = jnp.dot(joined, jnp.concatenate([upper, lower], axis=0), preferred_element_type=jnp.float32)
            results.append(both[:both.shape[0] // 2] + both[both.shape[0] // 2:])
        return results

    def turned(layer, half, results):
        order = plan.orders[layer]
        unit = jnp.full((16, 128), 1 / STEPS, jnp.float32)
        if layer == 0:
            unit = unit * sizes[0:1, :]
        for side in range(2):
            for tile, at in enumerate(starts(layer, side, half, order, 4)):
                real, imag = [result[16 * tile:16 * tile + 16, 128 * side:128 * side + 128] for result in results]
                word = phases[layer, at:at + 16, :]
                cosine = (word >> 16).astype(jnp.float32) * unit
                sine = ((word << 16) >> 16).astype(jnp.float32) * unit
                for part, value in enumerate((cosine * real - sine * imag, sine * real + cosine * imag)):
                    if layer == layers - 1:
                        block = tuple(int(k) for k in np.unravel_index(at // 16, plan.shape))
                        out[block + (pl.ds(part, 16, 2), slice(None))] = value
                    elif plan.steps[layer + 1]:
                        held[part, at:at + 16, :] = value
                    else:
                        large, small = split(value)
                        parts[(layer + 1) % 2, 0, part, at:at + 16, :] = large
                        parts[(layer + 1) % 2, 1, part, at:at + 16, :] = small
            if layer == layers - 1:
                chosen = {plan.targets[layer]: side}
                if plan.halves:
                    chosen[plan.halves[0]] = half
                here = tuple(chosen.get(bit, slice(None)) for bit in plan.axes)
                copies.append(pltpu.make_async_copy(out.at[here], result.at[here], done.at[len(copies)]))
                copies[-1].start()

    waiting = None
    for layer in range(layers):
        for half in range(1 << len(plan.halves)):
            results = products(layer, half)
            if (layer, half) == (0, 0):
                for kind in range(2):
                    widen(last[kind].astype(jnp.float32), last_here.at[kind])
            if plan.halves and waiting:
                turned(*waiting)
                waiting = None
            if plan.halves:
                waiting = (layer, half, results)
            else:
                turned(layer, half, results)
    if waiting:
        turned(*waiting)
    for copy in copies:
        copy.wait()


def shards(
    amplitudes, gate_matrices, phase_qubits, phase_angles, cut_qubits, cut_angle, path_index
):
    devices = lax.axis_size("hi")
    global_count = devices.bit_length() - 1
    amp_count = amplitudes.shape[1]
    rows = amp_count >> LANE_BITS
    layers = gate_matrices.shape[0]
    plan = Plan(global_count, amp_count.bit_length() - 1, layers)

    shaped = with_layout_constraint(amplitudes.reshape(2, rows, 128), Layout(major_to_minor=(1, 0, 2)))
    sent = shaped.transpose(1, 0, 2).reshape(devices, -1, 128)
    came = lax.all_to_all(sent, "hi", split_axis=0, concat_axis=0, tiled=True).reshape(2 * rows, 128)

    vmem, smem = pl.BlockSpec(memory_space=pltpu.VMEM), pl.BlockSpec(memory_space=pltpu.SMEM)
    weights_shape = (2, 256, 256)
    near, last, phases, sizes = pl.pallas_call(
        functools.partial(tables_kernel, plan, rows),
        out_shape=(
            jax.ShapeDtypeStruct((layers - 1,) + weights_shape, jnp.bfloat16),
            jax.ShapeDtypeStruct((2, 128, 128), jnp.bfloat16),
            jax.ShapeDtypeStruct((layers, rows, 128), jnp.int32),
            jax.ShapeDtypeStruct((8, 128), jnp.float32),
        ),
        in_specs=[vmem] + [smem] * 5,
        out_specs=[vmem] * 4,
        cost_estimate=pl.CostEstimate(flops=100 * layers * amp_count, bytes_accessed=4 * layers * amp_count, transcendentals=0),
        compiler_params=pltpu.CompilerParams(vmem_limit_bytes=24 << 20),
        name="tables",
    )(gate_matrices, phase_qubits.transpose(0, 2, 1), phase_angles, cut_qubits.T, cut_angle, path_index)

    result = pl.pallas_call(
        functools.partial(layers_kernel, plan, rows),
        out_shape=jax.ShapeDtypeStruct(plan.shape + (32, 128), jnp.float32),
        in_specs=[vmem] * 5,
        out_specs=pl.BlockSpec(memory_space=pltpu.HBM),
        scratch_shapes=[
            pltpu.VMEM(weights_shape, jnp.bfloat16),
            pltpu.VMEM((2, rows, 128), jnp.float32),
            pltpu.VMEM((2, 2, 2, rows, 128), jnp.bfloat16),
            pltpu.VMEM(plan.shape + (32, 128), jnp.float32),
            pltpu.SemaphoreType.DMA((2 << len(plan.halves),)),
        ],
        compiler_params=pltpu.CompilerParams(vmem_limit_bytes=24 << 20),
        name="layers",
    )(came, near, last, phases, sizes).reshape(2 * rows, 128)

    if plan.orders[-1] != plan.wanted:
        bits = len(plan.wanted)
        shaped = result.reshape((2,) * bits + (2, 128))
        axes = [bits - 1 - plan.orders[-1].index(plan.wanted[bits - 1 - axis]) for axis in range(bits)]
        result = shaped.transpose(axes + [bits, bits + 1]).reshape(2 * rows, 128)
    if plan.extra:
        size = 1 << plan.extra
        groups = [list(range(first, first + size)) for first in range(0, devices, size)]
        result = lax.all_to_all(
            result.reshape(size, -1, 128), "hi", split_axis=0, concat_axis=0,
            axis_index_groups=groups, tiled=True,
        )
    return result.reshape(rows, 2, 128).transpose(1, 0, 2).reshape(2, amp_count)


def solution(mesh):
    placed = (
        P(None, ("paths", "hi")),
        P(),
        P("paths", None, None),
        P("paths", None),
        P("paths", None),
        P("paths"),
        P("paths"),
    )
    return jax.shard_map(
        shards, mesh=mesh, in_specs=placed, out_specs=P(None, ("paths", "hi")), check_vma=False
    )
```

```python
import functools

import jax
import jax.numpy as jnp
import numpy as np
from jax import lax
from jax.experimental import pallas as pl
from jax.experimental.layout import Layout, with_layout_constraint
from jax.experimental.pallas import tpu as pltpu
from jax.sharding import PartitionSpec as P

LANE_BITS = 7
GATE_BITS = 6
STEPS = 32767.0


def fitted(function, degree):
    nodes = np.cos(np.pi * (np.arange(64) + 0.5) / 64) * 0.125 + 0.125
    series = np.polynomial.chebyshev.Chebyshev.fit(nodes, function(np.sqrt(nodes)), degree, domain=[0, 0.25])
    return [float(c) for c in series.convert(kind=np.polynomial.Polynomial).coef]


COS_TERMS = fitted(lambda v: np.cos(2 * np.pi * v), 7)
SIN_TERMS = fitted(lambda v: np.sin(2 * np.pi * v) / v, 6)


def horner(terms, w):
    total = jnp.full_like(w, terms[-1])
    for term in terms[-2::-1]:
        total = total * w + term
    return total


def turn(angle):
    part = angle - jnp.round(angle)
    square = part * part
    return horner(COS_TERMS, square), part * horner(SIN_TERMS, square)


class Plan:
    def __init__(self, global_count, local_bits, layers):
        self.global_count, self.local_bits, self.layers = global_count, local_bits, layers
        self.top = top = local_bits - global_count
        place = {}
        for label in range(local_bits + global_count):
            if label < top:
                place[label] = label
            elif label < local_bits:
                place[label] = label + global_count
            else:
                place[label] = label - global_count
        held = list(range(local_bits + global_count))
        self.targets = []
        for layer in range(layers):
            if layer < global_count:
                low, high = 7 + layer, local_bits + layer
                held[low], held[high] = held[high], held[low]
                target = low
            else:
                if layer == global_count:
                    held = held[:top] + held[local_bits:] + held[top:local_bits]
                target = local_bits - 2 * global_count + layer
            self.targets.append(place[held[target]])
        assert all(LANE_BITS <= bit < local_bits for bit in self.targets)
        ends = [place[label] for label in held]
        self.extra = sum(ends[local_bits + k] != local_bits + k for k in range(global_count))
        swapped = ends[:]
        for k in range(self.extra):
            low, high = local_bits - self.extra + k, local_bits + k
            assert ends[low] == high
            swapped[low], swapped[high] = ends[high], ends[low]
        assert swapped[local_bits:] == list(range(local_bits, local_bits + global_count))
        assert swapped[:LANE_BITS] == list(range(LANE_BITS))
        self.wanted = swapped[LANE_BITS:local_bits]
        self.orders, self.steps = [], []
        order = list(range(LANE_BITS, local_bits))
        for layer, target in enumerate(self.targets):
            step = 0
            if target in order[:4]:
                step = max(range(1, len(order) - 2), key=lambda at: self.lasts(order[at:at + 3], layer))
                triple = order[step:step + 3]
                if triple == self.wanted[:3] and not set(self.wanted[:4]) & set(self.targets[layer:]):
                    order = self.wanted
                else:
                    rest = sorted((bit for bit in order if bit not in triple), key=lambda bit: -self.lasts([bit], layer))
                    order = triple + rest
                assert target not in order[:4]
            self.steps.append(step)
            self.orders.append(order)

        self.halves = [bit for bit in order if bit not in self.targets
                       and all(other.index(bit) >= 4 for other in self.orders)][:1]

        self.axes, shape = [], []
        for bit in order[:3:-1]:
            apart = bit in [self.targets[-1]] + self.halves
            if not apart and self.axes and self.axes[-1] is None:
                shape[-1] *= 2
            else:
                self.axes.append(bit if apart else None)
                shape.append(2)
        self.shape = tuple(shape)

    def lasts(self, bits, layer):
        uses = self.targets[layer:]
        count = next((k for k, bit in enumerate(uses) if bit in bits), len(uses))
        return count + (count == len(uses) and bits == self.wanted[:3])

    def locate(self, qubit, layer):
        low, count = 7, min(layer + 1, self.global_count)
        size, high = self.global_count, self.local_bits
        if layer >= size:
            qubit = jnp.where(qubit >= high, qubit - size, jnp.where(qubit >= self.top, qubit + size, qubit))
        up = (qubit >= low) & (qubit < low + count)
        down = (qubit >= high) & (qubit < high + count)
        label = jnp.where(up, qubit + (high - low), jnp.where(down, qubit - (high - low), qubit))
        return jnp.where(label >= high, label - size, jnp.where(label >= self.top, label + size, label))


def widen(turned, block):
    lane = lax.broadcasted_iota(jnp.int32, (128, 128), 1)
    for to_bit in range(2):
        kept = jnp.where((lane >= 64) == (to_bit == 1), turned, 0.0)
        moved = pltpu.roll(kept, 64, 1)
        first, second = (kept, moved) if to_bit == 0 else (moved, kept)
        for from_bit in range(2):
            part = slice(64 * from_bit, 64 * from_bit + 64)
            both = jnp.concatenate([first[part], second[part]], axis=0)
            block[128 * from_bit:128 * from_bit + 128, 128 * to_bit:128 * to_bit + 128] = both.astype(jnp.bfloat16)


def tables_kernel(plan, rows, gates, pair_qubits, pair_angles, cut_qubits, cut_angle, path_index,
                  near, last, phases, sizes):
    device_part = lax.axis_index("hi") << plan.local_bits
    for layer in range(plan.layers):
        for kind in range(2):
            turned = gates[layer, kind].astype(jnp.float32).T
            if layer == plan.layers - 1:
                last[kind] = turned.astype(jnp.bfloat16)
            else:
                widen(turned, near.at[layer, kind])

    block_rows = 64
    block_bits = block_rows.bit_length() - 1
    row = lax.broadcasted_iota(jnp.int32, (block_rows, 128), 0)
    lane = lax.broadcasted_iota(jnp.int32, (block_rows, 128), 1)
    for layer in range(plan.layers):
        order = plan.orders[layer]
        base = lane + device_part
        for bit in range(block_bits):
            base = base + (((row >> bit) & 1) << order[bit])
        masks, turns = [], []
        one = jnp.int32(1)
        for pair in range(pair_qubits.shape[2]):
            first = plan.locate(pair_qubits[layer, 0, pair], layer)
            second = plan.locate(pair_qubits[layer, 1, pair], layer)
            masks.append((one << first) | (one << second))
            turns.append(pair_angles[layer, pair] * np.float32(0.5 / np.pi))
        if layer == 0:
            size = jnp.ones((8, 128), jnp.float32)
            cut_masks, cut_turns = [], []
            for cut in range(cut_qubits.shape[1]):
                first = plan.locate(cut_qubits[0, cut], layer)
                second = plan.locate(cut_qubits[1, cut], layer)
                cut_masks.append((one << first) | (one << second))
                chosen = path_index[cut] == 0
                cosine, sine = turn(jnp.full((8, 128), cut_angle[cut] * np.float32(0.5 / np.pi)))
                size = size * jnp.where(chosen, cosine, sine)
                cut_turns.append(jnp.where(chosen, 0.0, 0.25))
            sizes[...] = size

        @pl.loop(0, rows // block_rows)
        def _(block):
            offset = jnp.int32(0)
            for bit in range(block_bits, len(order)):
                offset = offset + (((block >> (bit - block_bits)) & 1) << order[bit])
            index = base + offset
            angle = jnp.zeros((block_rows, 128), jnp.float32)
            for mask, amount in zip(masks, turns):
                angle = angle + jnp.where((index & mask) == mask, amount, 0.0)
            if layer == 0:
                for mask, amount in zip(cut_masks, cut_turns):
                    both = index & mask
                    angle = angle + jnp.where((both == 0) | (both == mask), -amount, amount)
            cosine, sine = turn(angle)
            at = pl.ds(pl.multiple_of(block * block_rows, block_rows), block_rows)
            cosine = jnp.round(cosine * STEPS).astype(jnp.int32)
            sine = jnp.round(sine * STEPS).astype(jnp.int32)
            phases[layer, at, :] = (cosine << 16) | (sine & 0xFFFF)


def offset_of(number, bits, order):
    return sum(((number >> k) & 1) << order.index(bit) for k, bit in enumerate(bits))


def split(values):
    large = values.astype(jnp.bfloat16)
    return large, (values - large.astype(jnp.float32)).astype(jnp.bfloat16)


def layers_kernel(plan, rows, state, near, last, phases, sizes, result, last_here, held, parts, out, done):
    layers = plan.layers
    copies = []

    def starts(layer, side, half, order, height):
        fixed = [plan.targets[layer]] + plan.halves
        rest = [bit for bit in plan.orders[layer] if bit not in fixed][height:]
        base = side << order.index(plan.targets[layer])
        if plan.halves:
            base += half << order.index(plan.halves[0])
        return [base + offset_of(number, rest, order) for number in range(1 << len(rest))]

    def products(layer, half):
        order, step = plan.orders[layer], plan.steps[layer]
        pieces = []
        for part in range(2):
            if layer == 0 or step:
                old_order = plan.orders[layer - 1] if layer else list(range(LANE_BITS, plan.local_bits))
                sides = []
                for side in range(2):
                    if layer == 0:
                        tiles = [state[pl.ds(2 * at + part, 8, 2 << step), :]
                                 for at in starts(layer, side, half, old_order, 3)]
                    else:
                        tiles = [held[part, pl.ds(at, 8, 1 << step), :]
                                 for at in starts(layer, side, half, old_order, 3)]
                    sides.append(jnp.concatenate(tiles, axis=0))
                pieces.append(split(jnp.concatenate(sides, axis=1)))
            else:
                pieces.append([
                    jnp.concatenate([
                        jnp.concatenate([parts[layer % 2, size, part, at:at + 16, :]
                                         for at in starts(layer, side, half, order, 4)], axis=0)
                        for side in range(2)
                    ], axis=1)
                    for size in range(2)
                ])
        weights = last_here if layer == layers - 1 else near.at[layer]
        real, imag = weights[0], weights[1]
        joined = jnp.concatenate(
            [jnp.concatenate([pieces[0][size], pieces[1][size]], axis=1) for size in range(2)], axis=0
        )
        weight = jnp.concatenate(
            [jnp.concatenate([real, imag], axis=1), jnp.concatenate([-imag, real], axis=1)], axis=0
        )
        both = jnp.dot(joined, weight, preferred_element_type=jnp.float32)
        total = both[:both.shape[0] // 2] + both[both.shape[0] // 2:]
        results = [total[:, :256], total[:, 256:]]
        return results

    def turned(layer, half, results):
        order = plan.orders[layer]
        unit = jnp.full((16, 128), 1 / STEPS, jnp.float32)
        if layer == 0:
            unit = unit * sizes[0:1, :]
        for side in range(2):
            for tile, at in enumerate(starts(layer, side, half, order, 4)):
                real, imag = [result[16 * tile:16 * tile + 16, 128 * side:128 * side + 128] for result in results]
                word = phases[layer, at:at + 16, :]
                cosine = (word >> 16).astype(jnp.float32) * unit
                sine = ((word << 16) >> 16).astype(jnp.float32) * unit
                for part, value in enumerate((cosine * real - sine * imag, sine * real + cosine * imag)):
                    if layer == layers - 1:
                        block = tuple(int(k) for k in np.unravel_index(at // 16, plan.shape))
                        out[block + (pl.ds(part, 16, 2), slice(None))] = value
                    elif plan.steps[layer + 1]:
                        held[part, at:at + 16, :] = value
                    else:
                        large, small = split(value)
                        parts[(layer + 1) % 2, 0, part, at:at + 16, :] = large
                        parts[(layer + 1) % 2, 1, part, at:at + 16, :] = small
            if layer == layers - 1:
                chosen = {plan.targets[layer]: side}
                if plan.halves:
                    chosen[plan.halves[0]] = half
                here = tuple(chosen.get(bit, slice(None)) for bit in plan.axes)
                copies.append(pltpu.make_async_copy(out.at[here], result.at[here], done.at[len(copies)]))
                copies[-1].start()

    waiting = None
    for layer in range(layers):
        for half in range(1 << len(plan.halves)):
            results = products(layer, half)
            if (layer, half) == (0, 0):
                for kind in range(2):
                    widen(last[kind].astype(jnp.float32), last_here.at[kind])
            if plan.halves and waiting:
                turned(*waiting)
                waiting = None
            if plan.halves:
                waiting = (layer, half, results)
            else:
                turned(layer, half, results)
    if waiting:
        turned(*waiting)
    for copy in copies:
        copy.wait()


def shards(
    amplitudes, gate_matrices, phase_qubits, phase_angles, cut_qubits, cut_angle, path_index
):
    devices = lax.axis_size("hi")
    global_count = devices.bit_length() - 1
    amp_count = amplitudes.shape[1]
    rows = amp_count >> LANE_BITS
    layers = gate_matrices.shape[0]
    plan = Plan(global_count, amp_count.bit_length() - 1, layers)

    shaped = with_layout_constraint(amplitudes.reshape(2, rows, 128), Layout(major_to_minor=(1, 0, 2)))
    sent = shaped.transpose(1, 0, 2).reshape(devices, -1, 128)
    came = lax.all_to_all(sent, "hi", split_axis=0, concat_axis=0, tiled=True).reshape(2 * rows, 128)

    vmem, smem = pl.BlockSpec(memory_space=pltpu.VMEM), pl.BlockSpec(memory_space=pltpu.SMEM)
    weights_shape = (2, 256, 256)
    near, last, phases, sizes = pl.pallas_call(
        functools.partial(tables_kernel, plan, rows),
        out_shape=(
            jax.ShapeDtypeStruct((layers - 1,) + weights_shape, jnp.bfloat16),
            jax.ShapeDtypeStruct((2, 128, 128), jnp.bfloat16),
            jax.ShapeDtypeStruct((layers, rows, 128), jnp.int32),
            jax.ShapeDtypeStruct((8, 128), jnp.float32),
        ),
        in_specs=[vmem] + [smem] * 5,
        out_specs=[vmem] * 4,
        cost_estimate=pl.CostEstimate(flops=100 * layers * amp_count, bytes_accessed=4 * layers * amp_count, transcendentals=0),
        compiler_params=pltpu.CompilerParams(vmem_limit_bytes=24 << 20),
        name="tables",
    )(gate_matrices, phase_qubits.transpose(0, 2, 1), phase_angles, cut_qubits.T, cut_angle, path_index)

    result = pl.pallas_call(
        functools.partial(layers_kernel, plan, rows),
        out_shape=jax.ShapeDtypeStruct(plan.shape + (32, 128), jnp.float32),
        in_specs=[vmem] * 5,
        out_specs=pl.BlockSpec(memory_space=pltpu.HBM),
        scratch_shapes=[
            pltpu.VMEM(weights_shape, jnp.bfloat16),
            pltpu.VMEM((2, rows, 128), jnp.float32),
            pltpu.VMEM((2, 2, 2, rows, 128), jnp.bfloat16),
            pltpu.VMEM(plan.shape + (32, 128), jnp.float32),
            pltpu.SemaphoreType.DMA((2 << len(plan.halves),)),
        ],
        compiler_params=pltpu.CompilerParams(vmem_limit_bytes=24 << 20),
        name="layers",
    )(came, near, last, phases, sizes).reshape(2 * rows, 128)

    if plan.orders[-1] != plan.wanted:
        bits = len(plan.wanted)
        shaped = result.reshape((2,) * bits + (2, 128))
        axes = [bits - 1 - plan.orders[-1].index(plan.wanted[bits - 1 - axis]) for axis in range(bits)]
        result = shaped.transpose(axes + [bits, bits + 1]).reshape(2 * rows, 128)
    if plan.extra:
        size = 1 << plan.extra
        groups = [list(range(first, first + size)) for first in range(0, devices, size)]
        result = lax.all_to_all(
            result.reshape(size, -1, 128), "hi", split_axis=0, concat_axis=0,
            axis_index_groups=groups, tiled=True,
        )
    return result.reshape(rows, 2, 128).transpose(1, 0, 2).reshape(2, amp_count)


def solution(mesh):
    placed = (
        P(None, ("paths", "hi")),
        P(),
        P("paths", None, None),
        P("paths", None),
        P("paths", None),
        P("paths"),
        P("paths"),
    )
    return jax.shard_map(
        shards, mesh=mesh, in_specs=placed, out_specs=P(None, ("paths", "hi")), check_vma=False
    )
```
